512 devices in a mesh: dp: 8 (over y_lo, core), seq: 64 (over y_hi, x, z).
Axes of the slice: x: 4, y: 8 (y_hi: 2, y_lo: 4; y = y_hi * 4 + y_lo), z: 8, core: 2. Of those that a mesh axis runs over, the one named last changes fastest.
Arguments:
- query_key_value: bfloat16 [3, 8, 64, 128, 1152], P(None, 'dp', 'seq'), may hold values from -8 to 8
- out_weight: bfloat16 [768, 1152], P('seq'), may hold values from -0.1875 to 0.1875
- cotangent: bfloat16 [8, 64, 128, 768], P('dp', 'seq'), may hold values from -16 to 16
Outputs:
- projected: bfloat16 [8, 64, 128, 768], P('dp', 'seq')
- input_grads: bfloat16 [3, 8, 64, 128, 1152], P(None, 'dp', 'seq')
- weight_grad: float32 [768, 1152], P('seq')
The draws below stay inside these ranges and needn't reach their ends.
All inputs are finite; a program needn't handle non-finite values.
Results may differ from the reference program's by a relative error of at most 0.007.
Values may be sent and summed in bfloat16 or wider, within the bound.
No kernel may reach another device: no remote copies, remote signals or barrier semaphores. Data moves between devices by JAX's collectives and lax.ppermute only.
A program may use at most 64 MiB of HBM per device.

```python
import math
import jax
import jax.numpy as jnp
from jax import lax

D = 1152
HEADS = 16
HEAD_DIM = 72
OUT_COLS = 768
FRAMES = 64
SPATIAL = 128
SAMPLES = 8
TOKENS = 65536


def draw_query_key_value(key, part):
    key = jax.random.fold_in(key, 7)
    full_shape = (3, SAMPLES, FRAMES, SPATIAL, D)
    return jax.random.truncated_normal(key, -8.0, 8.0, full_shape, jnp.float32).astype(jnp.bfloat16)


def with_spikes(values, stream_key, source, target, shards_of, factor):
    owner, partner = [(jnp.arange(values.shape[dim]) // (values.shape[dim] // shards_of)).reshape([-1 if axis == dim else 1 for axis in range(values.ndim)]) for dim in (source, target)]
    chosen = jax.random.permutation(stream_key, shards_of)[partner]
    strong = (owner == chosen) | (owner == (partner + shards_of // 2) % shards_of)
    return jnp.where(strong, factor * values, values)


def steps_of(stream_key, shape, cuts, least, top_value):
    def one(position, parts):
        heights = jax.random.uniform(jax.random.fold_in(jax.random.fold_in(stream_key, 6), position), (parts,), jnp.float32, least / len(cuts), top_value / len(cuts))
        return jnp.repeat(jnp.exp(heights), shape[position] // parts).reshape((-1,) + (1,) * (len(shape) - position - 1))

    gain = one(*cuts[0])
    for cut in cuts[1:]:
        gain = gain * one(*cut)
    return gain


def bell_draw(stream_key, dims, spread, bound, cuts=(), dtype=jnp.bfloat16):
    factor_of = steps_of(stream_key, dims, cuts, -0.22, 0.18) if cuts else 1.0
    drawn = jax.random.normal(stream_key, dims, jnp.float32) * spread * factor_of
    return jnp.minimum(jnp.maximum(drawn, -bound), bound).astype(dtype)


def gaussian_with(rng, shape, scale, reach, cuts, heavy, dtype=jnp.bfloat16):
    values = scale * jax.random.normal(rng, shape, jnp.float32)
    if cuts:
        values = values * steps_of(rng, shape, cuts, -0.22, 0.18)
    return jnp.clip(with_spikes(values, jax.random.fold_in(rng, 3), *heavy), -reach, reach).astype(dtype)


def setup_inputs(seed: int = 0) -> dict:
    arg_keys = jax.random.split(jax.random.key(seed), 4)
    return {
        "query_key_value": draw_query_key_value(jax.random.fold_in(arg_keys[3], 71), 0),
        "out_weight": bell_draw(arg_keys[1], (OUT_COLS, D), D ** -0.5, 0.1875, ((0, 64),)),
        "cotangent": gaussian_with(arg_keys[2], (SAMPLES, FRAMES, SPATIAL, OUT_COLS), 1.0, 16.0, ((0, 8), (1, 64)), (1, 3, 64, 4.0)),
    }


def split_heads(tensor):
    return tensor.astype(jnp.float32).reshape(FRAMES, SPATIAL, HEADS, HEAD_DIM)

def reference(query_key_value, out_weight, cotangent):
    inv_root = 1.0 / math.sqrt(HEAD_DIM)

    def one_sample(operands):
        query_in, key_in, value_in, upstream = operands
        query_heads = split_heads(query_in)
        key_heads = split_heads(key_in)
        value_heads = split_heads(value_in)
        upstream_rows = upstream.reshape(-1, OUT_COLS)
        grad_attended = jnp.dot(upstream_rows, out_weight, preferred_element_type=jnp.float32).astype(jnp.bfloat16)
        grad_heads = split_heads(grad_attended)
        scores = jnp.einsum('qlhd,klhd->lhqk', query_heads, key_heads) * inv_root
        weights = jax.nn.softmax(scores, axis=-1)
        rounded_weights = weights.astype(jnp.bfloat16).astype(jnp.float32)
        attended = jnp.einsum('lhqk,klhd->qlhd', rounded_weights, value_heads).astype(jnp.bfloat16)
        attended_rows = attended.reshape(-1, D)
        projected = jnp.dot(attended_rows, out_weight.T, preferred_element_type=jnp.float32).astype(jnp.bfloat16)
        partial_grad = jnp.dot(upstream_rows.T, attended_rows, preferred_element_type=jnp.float32)
        grad_values = jnp.einsum('lhqk,qlhd->klhd', rounded_weights, grad_heads).astype(jnp.bfloat16)
        grad_weights = jnp.einsum('qlhd,klhd->lhqk', grad_heads, value_heads)
        centred = grad_weights - lax.optimization_barrier(jnp.sum(weights * grad_weights, axis=-1, keepdims=True))
        grad_scores = (weights * centred * inv_root).astype(jnp.bfloat16).astype(jnp.float32)
        grad_queries = jnp.einsum('lhqk,klhd->qlhd', grad_scores, key_heads).astype(jnp.bfloat16)
        grad_keys = jnp.einsum('lhqk,qlhd->klhd', grad_scores, query_heads).astype(jnp.bfloat16)
        stacked = jnp.stack([grad_queries, grad_keys, grad_values]).reshape(3, FRAMES, SPATIAL, D)
        return (projected.reshape(FRAMES, SPATIAL, OUT_COLS), stacked, partial_grad)
    projected, grads_all, partials = lax.map(one_sample, (query_key_value[0], query_key_value[1], query_key_value[2], cotangent))
    input_grads = jnp.moveaxis(grads_all, 1, 0)
    weight_grad = lax.optimization_barrier(jnp.sum(partials, axis=0)) * (1.0 / math.sqrt(TOKENS))
    return (projected, input_grads, weight_grad)
```

```python
import math

import jax
import jax.numpy as jnp
from jax import lax
from jax.experimental import pallas as pl
from jax.experimental.pallas import tpu as pltpu
from jax.sharding import Mesh
from jax.sharding import PartitionSpec as P

HEADS = 16
HEAD_DIM = 72
ROWS = 128
WIDTH = 1152
OUT = 768
HALF = OUT // 2
COLS = 3 * WIDTH + OUT
INV_ROOT = 1.0 / math.sqrt(HEAD_DIM)
BF16 = jnp.bfloat16
F32 = jnp.float32

SEQ = ("yh", "x", "z")
RING = ("x", "z")
YAXIS = ("yl", "yh")


def dot(lhs, rhs, lhs_dim, rhs_dim):
    return lax.dot_general(
        lhs, rhs, (((lhs_dim,), (rhs_dim,)), ((), ())), preferred_element_type=F32
    )


def head(ref, part, index):
    start = part * WIDTH + index * HEAD_DIM
    return ref[:, start : start + HEAD_DIM]


def forward_kernel(rows_ref, attended_ref, weights_ref):
    row = lax.broadcasted_iota(jnp.int32, (ROWS, ROWS), 0)
    col = lax.broadcasted_iota(jnp.int32, (ROWS, ROWS), 1)
    same_place = ((row ^ col) & 1) == 0
    attended = []
    for index in range(HEADS):
        query, key, value = (head(rows_ref, part, index) for part in range(3))
        scores = jnp.where(same_place, dot(query, key, 1, 1) * INV_ROOT, -1e30)
        powers = jnp.exp(scores - jnp.max(scores, axis=1, keepdims=True))
        weights = powers / jnp.sum(powers, axis=1, keepdims=True)
        weights_ref[index] = weights
        attended.append(dot(weights.astype(BF16), value, 1, 0).astype(BF16))
    attended_ref[...] = jnp.concatenate(attended, axis=1)


def backward_kernel(rows_ref, weights_ref, attended_ref, matrix_ref, out_ref, upstream_ref):
    upstream_ref[...] = dot(rows_ref[:, 3 * WIDTH :], matrix_ref[...], 1, 0).astype(BF16)
    out_ref[:, 3 * WIDTH :] = dot(attended_ref[...], matrix_ref[...], 1, 1).astype(BF16)
    grads = ([], [], [])
    for index in range(HEADS):
        query, key, value = (head(rows_ref, part, index) for part in range(3))
        upstream = head(upstream_ref, 0, index)
        weights = weights_ref[index]
        grads[2].append(dot(weights.astype(BF16), upstream, 0, 0).astype(BF16))
        grad_weights = dot(upstream, value, 1, 1)
        centred = grad_weights - jnp.sum(weights * grad_weights, axis=1, keepdims=True)
        grad_scores = (weights * centred * INV_ROOT).astype(BF16)
        grads[0].append(dot(grad_scores, key, 1, 0).astype(BF16))
        grads[1].append(dot(grad_scores, query, 0, 0).astype(BF16))
    for part in range(3):
        out_ref[:, part * WIDTH : (part + 1) * WIDTH] = jnp.concatenate(grads[part], axis=1)


WHOLE = pl.BlockSpec(memory_space=pltpu.VMEM)
PARAMS = pltpu.CompilerParams(vmem_limit_bytes=24 << 20)


def forward(rows):
    return pl.pallas_call(
        forward_kernel,
        out_shape=(
            jax.ShapeDtypeStruct((ROWS, WIDTH), BF16),
            jax.ShapeDtypeStruct((HEADS, ROWS, ROWS), F32),
        ),
        in_specs=[WHOLE],
        out_specs=(WHOLE, WHOLE),
        compiler_params=PARAMS,
        name="forward",
    )(rows)


def backward(rows, weights, attended, matrix):
    return pl.pallas_call(
        backward_kernel,
        out_shape=jax.ShapeDtypeStruct((ROWS, COLS), BF16),
        in_specs=[WHOLE] * 4,
        out_specs=WHOLE,
        scratch_shapes=[pltpu.VMEM((ROWS, WIDTH), BF16)],
        compiler_params=PARAMS,
        name="backward",
    )(rows, weights, attended, matrix)


def exchange(value, axes):
    return lax.all_to_all(value, axes, 0, 0, tiled=True)


def swap(value, axis):
    return lax.ppermute(value, axis, [(0, 1), (1, 0)])


def fold(blocks):
    return blocks.reshape(-1, 3, 4, WIDTH).transpose(0, 2, 1, 3).reshape(-1, 4, 3 * WIDTH)


def unfold(blocks):
    return blocks.reshape(-1, 4, 3, WIDTH).transpose(0, 2, 1, 3).reshape(-1, WIDTH)


def gather_weight(own_rows, core, y_high):
    rows = jnp.where(core == y_high, own_rows, swap(own_rows, "yh"))
    half = unfold(exchange(jnp.broadcast_to(fold(rows[None]), (32, 4, 3 * WIDTH)), RING))
    other = swap(half, "c")
    return jnp.where(
        core == 0, jnp.concatenate([half, other]), jnp.concatenate([other, half])
    )


def weight_gradient(cotangent, attended, core, y_high):
    low, high = cotangent[:, :HALF], cotangent[:, HALF:]
    mine = jnp.where(core == 0, low, high)
    theirs = jnp.where(core == 0, high, low)
    columns = jnp.concatenate([mine, swap(theirs, "c")])
    features = jnp.concatenate([attended, swap(attended, "c")])
    partial = dot(columns, features, 0, 0).astype(BF16)
    terms = exchange(fold(partial.reshape(32, 12, WIDTH)), RING)
    rows = jnp.sum(terms.astype(F32), axis=0).reshape(108, 128)
    everyone = exchange(jnp.broadcast_to(rows[None], (8, 108, 128)), YAXIS)
    total = unfold(jnp.sum(everyone, axis=0).reshape(1, 4, 3 * WIDTH))
    return jnp.where(core == y_high, total, swap(total, "c"))


def on_device(query_key_value, out_weight, cotangent):
    core, y_high = lax.axis_index("c"), lax.axis_index("yh")
    parts = query_key_value.reshape(3, ROWS, WIDTH)
    sent = jnp.concatenate([parts[0], parts[1], parts[2], cotangent.reshape(ROWS, OUT)], axis=1)
    rows = exchange(sent.reshape(64, 2, COLS), SEQ).reshape(ROWS, COLS)
    matrix = gather_weight(out_weight, core, y_high)
    attended, weights = forward(rows)
    owned = weight_gradient(rows[:, 3 * WIDTH :], attended, core, y_high)
    results = backward(rows, weights, attended, matrix)
    back = exchange(results.reshape(64, 2, COLS), SEQ).reshape(ROWS, COLS)
    grads = jnp.stack([back[:, part * WIDTH : (part + 1) * WIDTH] for part in range(3)])
    return (
        back[:, 3 * WIDTH :].reshape(1, 1, ROWS, OUT),
        grads.reshape(3, 1, 1, ROWS, WIDTH),
        owned * (1.0 / math.sqrt(512 * ROWS)),
    )


def solution(mesh):
    split = Mesh(mesh.devices.reshape(4, 2, 2, 4, 8), ("yl", "c", "yh", "x", "z"))
    groups, frames = ("yl", "c"), SEQ
    in_specs = (P(None, groups, frames, None, None), P(frames, None), P(groups, frames, None, None))
    out_specs = (P(groups, frames, None, None), P(None, groups, frames, None, None), P(frames, None))
    return jax.shard_map(
        on_device, mesh=split, in_specs=in_specs, out_specs=out_specs, check_vma=False
    )
```

```python
import math

import jax
import jax.numpy as jnp
from jax import lax
from jax.experimental import pallas as pl
from jax.experimental.pallas import tpu as pltpu
from jax.sharding import Mesh
from jax.sharding import PartitionSpec as P

HEADS = 16
HEAD_DIM = 72
ROWS = 128
LANES = 128
WIDTH = 1152
TILES = WIDTH // LANES
OUT = 768
HALF = OUT // 2
BASE = 3 * WIDTH + OUT
PIECE = 896
PIECE_TILES = PIECE // LANES
COLS = BASE + PIECE
INV_ROOT = 1.0 / math.sqrt(HEAD_DIM)
BF16 = jnp.bfloat16
F32 = jnp.float32

SEQ = ("yh", "x", "z")
GROUPS = ("yl", "c")


def dot(lhs, rhs, lhs_dim, rhs_dim):
    return lax.dot_general(
        lhs, rhs, (((lhs_dim,), (rhs_dim,)), ((), ())), preferred_element_type=F32
    )


def head(ref, part, index):
    start = part * WIDTH + index * HEAD_DIM
    return ref[:, start : start + HEAD_DIM]


def channel_order():
    natural = lax.broadcasted_iota(jnp.int32, (OUT, OUT), 0)
    place = lax.broadcasted_iota(jnp.int32, (OUT, OUT), 1)
    source = 12 * ((place & 127) >> 1) + 2 * (place >> 7) + (place & 1)
    return jnp.where(natural == source, 1.0, 0.0).astype(BF16)


def half_tiles():
    return [
        (tile // PIECE_TILES, tile % PIECE_TILES, tile // TILES, tile % TILES)
        for tile in range(3 * TILES)
    ]


def lanes(tile):
    return slice(tile * LANES, (tile + 1) * LANES)


def pack_kernel(core_ref, parts_ref, cotangent_ref, weight_ref, out_ref):
    for part in range(3):
        out_ref[:, part * WIDTH : (part + 1) * WIDTH] = parts_ref[part]
    out_ref[:, 3 * WIDTH : BASE] = cotangent_ref[...]
    row = lax.broadcasted_iota(jnp.int32, (16, 12), 0)
    col = lax.broadcasted_iota(jnp.int32, (16, 12), 1)
    repeated = []
    for pair in range(3):
        chosen = col == 6 * core_ref[0] + 2 * pair + (row & 1)
        repeated.append(
            dot(jnp.where(chosen, 1.0, 0.0).astype(BF16), weight_ref[...], 1, 0).astype(BF16)
        )
    for high in range(2):
        for piece, place, pair, tile in half_tiles():
            start = 64 * high + 16 * piece
            out_ref[start : start + 16, BASE + place * LANES : BASE + (place + 1) * LANES] = (
                repeated[pair][:, lanes(tile)]
            )
        start = 64 * high + 48
        out_ref[start : start + 16, COLS - LANES :] = jnp.zeros((16, LANES), BF16)


def forward_kernel(core_ref, rows_ref, share_ref, channels_ref, weights_ref):
    row = lax.broadcasted_iota(jnp.int32, (ROWS, ROWS), 0)
    col = lax.broadcasted_iota(jnp.int32, (ROWS, ROWS), 1)
    same_place = ((row ^ col) & 1) == 0
    attended = []
    for index in range(HEADS):
        query, key, value = (head(rows_ref, part, index) for part in range(3))
        scores = jnp.where(same_place, dot(query, key, 1, 1) * INV_ROOT, -1e30)
        powers = jnp.exp(scores - jnp.max(scores, axis=1, keepdims=True))
        weights = powers / jnp.sum(powers, axis=1, keepdims=True)
        weights_ref[index] = weights
        attended.append(dot(weights.astype(BF16), value, 1, 0).astype(BF16))
    share_ref[:, :WIDTH] = jnp.concatenate(attended, axis=1)
    channels_ref[...] = dot(rows_ref[:, 3 * WIDTH : BASE], channel_order(), 1, 0).astype(BF16)
    other = pl.multiple_of((1 - core_ref[0]) * HALF, HALF)
    share_ref[:, WIDTH:] = channels_ref[:, pl.ds(other, HALF)]


def weight_grad_kernel(core_ref, share_ref, received_ref, channels_ref, out_ref):
    own = pl.multiple_of(core_ref[0] * HALF, HALF)
    columns = jnp.concatenate([channels_ref[:, pl.ds(own, HALF)], received_ref[:, WIDTH:]], axis=0)
    features = jnp.concatenate([share_ref[:, :WIDTH], received_ref[:, :WIDTH]], axis=0)
    partial = dot(columns, features, 0, 0).astype(BF16)
    for piece, place, pair, tile in half_tiles():
        out_ref[piece, :, lanes(place)] = partial[pair * ROWS : (pair + 1) * ROWS, lanes(tile)]
    out_ref[3, :, lanes(PIECE_TILES - 1)] = jnp.zeros((ROWS, LANES), BF16)


def backward_kernel(
    core_ref, rows_ref, weights_ref, share_ref, channels_ref, mine_ref, theirs_ref,
    out_ref, matrix_ref, upstream_ref,
):
    own = pl.multiple_of(core_ref[0] * HALF, HALF)
    other = pl.multiple_of((1 - core_ref[0]) * HALF, HALF)
    for piece, place, pair, tile in half_tiles():
        for start, half_ref in ((own, mine_ref), (other, theirs_ref)):
            matrix_ref[pl.ds(start + pair * ROWS, ROWS), lanes(tile)] = half_ref[
                piece, :, lanes(place)
            ]
    matrix = matrix_ref[...]
    upstream_ref[...] = dot(channels_ref[...], matrix, 1, 0).astype(BF16)
    projected = dot(share_ref[:, :WIDTH], matrix, 1, 1).astype(BF16)
    out_ref[:, 3 * WIDTH :] = dot(projected, channel_order(), 1, 1).astype(BF16)
    grads = ([], [], [])
    for index in range(HEADS):
        query, key, value = (head(rows_ref, part, index) for part in range(3))
        upstream = head(upstream_ref, 0, index)
        weights = weights_ref[index]
        grads[2].append(dot(weights.astype(BF16), upstream, 0, 0).astype(BF16))
        grad_weights = dot(upstream, value, 1, 1)
        centred = grad_weights - jnp.sum(weights * grad_weights, axis=1, keepdims=True)
        grad_scores = (weights * centred * INV_ROOT).astype(BF16)
        grads[0].append(dot(grad_scores, key, 1, 0).astype(BF16))
        grads[1].append(dot(grad_scores, query, 0, 0).astype(BF16))
    for part in range(3):
        out_ref[:, part * WIDTH : (part + 1) * WIDTH] = jnp.concatenate(grads[part], axis=1)


def call(kernel, name, out_shapes, scratch, core, *operands):
    whole = pl.BlockSpec(memory_space=pltpu.VMEM)
    return pl.pallas_call(
        kernel,
        out_shape=[jax.ShapeDtypeStruct(shape, dtype) for shape, dtype in out_shapes],
        in_specs=[pl.BlockSpec(memory_space=pltpu.SMEM)] + [whole] * len(operands),
        out_specs=[whole] * len(out_shapes),
        scratch_shapes=scratch,
        compiler_params=pltpu.CompilerParams(vmem_limit_bytes=24 << 20),
        name=name,
    )(core, *operands)


def exchange(value, axes):
    return lax.all_to_all(value, axes, 0, 0, tiled=True)


def swap(value):
    return lax.ppermute(value, "c", [(0, 1), (1, 0)])


def on_device(query_key_value, out_weight, cotangent):
    core = lax.axis_index("c").astype(jnp.int32).reshape(1)
    parts = query_key_value.reshape(3, ROWS, WIDTH)
    (packed,) = call(
        pack_kernel, "pack", [((ROWS, COLS), BF16)], [],
        core, parts, cotangent.reshape(ROWS, OUT), out_weight,
    )
    rows = exchange(packed.reshape(64, 2, COLS), SEQ).reshape(ROWS, COLS)
    piece = jnp.broadcast_to(rows[None, :, BASE:], (4, ROWS, PIECE))
    mine = exchange(piece, "x")
    share, channels, weights = call(
        forward_kernel, "forward",
        [((ROWS, WIDTH + HALF), BF16), ((ROWS, OUT), BF16), ((HEADS, ROWS, ROWS), F32)], [],
        core, rows,
    )
    (partial,) = call(
        weight_grad_kernel, "weight_grad", [((4, ROWS, PIECE), BF16)], [],
        core, share, swap(share), channels,
    )
    terms = exchange(partial, "x")
    theirs = swap(mine)
    (results,) = call(
        backward_kernel, "backward", [((ROWS, BASE), BF16)],
        [pltpu.VMEM((OUT, WIDTH), BF16), pltpu.VMEM((ROWS, WIDTH), BF16)],
        core, rows, weights, share, channels, mine, theirs,
    )
    summed = jnp.sum(terms.astype(F32), axis=0).astype(BF16)
    sent = jnp.concatenate([results.reshape(64, 2, BASE), summed.reshape(64, 2, PIECE)], axis=2)
    back = exchange(sent, SEQ)
    owned = jnp.sum(back[:, :, BASE:].astype(F32).reshape(2, 4, 8, 2, PIECE), axis=(0, 2))
    everyone = exchange(jnp.broadcast_to(owned[None], (8, 4, 2, PIECE)), GROUPS)
    total = jnp.sum(everyone.reshape(4, 2, 4, 2, PIECE), axis=0)
    pairs = total.transpose(0, 2, 1, 3).reshape(2, 2, 4 * PIECE)[:, :, : 3 * WIDTH]
    own_rows = pairs.reshape(2, 2, 3, WIDTH).transpose(0, 2, 1, 3).reshape(12, WIDTH)
    frames = back.reshape(ROWS, COLS)
    grads = jnp.stack([frames[:, part * WIDTH : (part + 1) * WIDTH] for part in range(3)])
    return (
        frames[:, 3 * WIDTH : BASE].reshape(1, 1, ROWS, OUT),
        grads.reshape(3, 1, 1, ROWS, WIDTH),
        own_rows * (1.0 / math.sqrt(512 * ROWS)),
    )


def solution(mesh):
    split = Mesh(mesh.devices.reshape(4, 2, 2, 4, 8), ("yl", "c", "yh", "x", "z"))
    in_specs = (P(None, GROUPS, SEQ, None, None), P(SEQ, None), P(GROUPS, SEQ, None, None))
    out_specs = (P(GROUPS, SEQ, None, None), P(None, GROUPS, SEQ, None, None), P(SEQ, None))
    return jax.shard_map(
        on_device, mesh=split, in_specs=in_specs, out_specs=out_specs, check_vma=False
    )
```

```python
import math

import jax
import jax.numpy as jnp
from jax import lax
from jax.experimental import pallas as pl
from jax.experimental.pallas import tpu as pltpu
from jax.sharding import Mesh
from jax.sharding import PartitionSpec as P

HEADS = 16
HEAD_DIM = 72
ROWS = 128
LANES = 128
WIDTH = 1152
TILES = WIDTH // LANES
OUT = 768
HALF = OUT // 2
BASE = 3 * WIDTH + OUT
PIECE = 896
PIECE_TILES = PIECE // LANES
COLS = BASE + PIECE
INV_ROOT = 1.0 / math.sqrt(HEAD_DIM)
GRAD_SCALE = 1.0 / math.sqrt(512 * ROWS)
BF16 = jnp.bfloat16
F32 = jnp.float32

SEQ = ("yh", "x", "z")
GROUPS = ("yl", "c")


def dot(lhs, rhs, lhs_dim, rhs_dim):
    return lax.dot_general(
        lhs, rhs, (((lhs_dim,), (rhs_dim,)), ((), ())), preferred_element_type=F32
    )


def lanes(tile, base=0):
    return slice(base + tile * LANES, base + (tile + 1) * LANES)


def only_head(index, start, value):
    feature = lax.broadcasted_iota(jnp.int32, value.shape, 1) + start
    inside = (feature >= index * HEAD_DIM) & (feature < (index + 1) * HEAD_DIM)
    return jnp.where(inside, value, jnp.zeros_like(value))


def head_lanes(index):
    first = index * HEAD_DIM // LANES
    last = ((index + 1) * HEAD_DIM - 1) // LANES + 1
    return first * LANES, last * LANES


def head_products(lhs_ref, lhs_base, rhs_ref, rhs_base, index):
    start, stop = head_lanes(index)
    rhs = only_head(index, start, rhs_ref[:, rhs_base + start : rhs_base + stop])
    return dot(lhs_ref[:, lhs_base + start : lhs_base + stop], rhs, 1, 1)


def tile_heads(tile):
    return [
        index
        for index in range(HEADS)
        if index * HEAD_DIM < (tile + 1) * LANES and (index + 1) * HEAD_DIM > tile * LANES
    ]


def stacked_heads(ref, base, tile):
    value = ref[:, lanes(tile, base)]
    return jnp.concatenate(
        [only_head(index, tile * LANES, value) for index in tile_heads(tile)], axis=0
    )


def channel_order():
    natural = lax.broadcasted_iota(jnp.int32, (OUT, OUT), 0)
    place = lax.broadcasted_iota(jnp.int32, (OUT, OUT), 1)
    source = 12 * ((place & 127) >> 1) + 2 * (place >> 7) + (place & 1)
    return jnp.where(natural == source, 1.0, 0.0).astype(BF16)


def half_tiles():
    return [
        (tile // PIECE_TILES, tile % PIECE_TILES, tile // TILES, tile % TILES)
        for tile in range(3 * TILES)
    ]


def pack_kernel(
    core_ref, parts_hbm, cotangent_hbm, weight_hbm, out_ref, parts, cotangent, weight, sems
):
    pairs = [(parts_hbm.at[part], parts.at[part]) for part in range(3)]
    pairs += [(cotangent_hbm, cotangent), (weight_hbm, weight)]
    copies = [
        pltpu.make_async_copy(source, target, sems.at[place])
        for place, (source, target) in enumerate(pairs)
    ]
    for copy in copies:
        copy.start()
    row = lax.broadcasted_iota(jnp.int32, (ROWS, 12), 0)
    col = lax.broadcasted_iota(jnp.int32, (ROWS, 12), 1)
    copies[4].wait()
    repeated = []
    for pair in range(3):
        chosen = col == 6 * core_ref[0] + 2 * pair + (row & 1)
        repeated.append(
            dot(jnp.where(chosen, 1.0, 0.0).astype(BF16), weight[...], 1, 0).astype(BF16)
        )
    column = (lax.broadcasted_iota(jnp.int32, (ROWS, LANES), 0) >> 4) & 3
    for place in range(PIECE_TILES):
        value = jnp.zeros((ROWS, LANES), BF16)
        for piece, at, pair, tile in half_tiles():
            if at == place:
                value = jnp.where(column == piece, repeated[pair][:, lanes(tile)], value)
        out_ref[:, :, lanes(place, BASE)] = value.reshape(64, 2, LANES)
    for part in range(3):
        copies[part].wait()
        out_ref[:, :, part * WIDTH : (part + 1) * WIDTH] = parts[part].reshape(64, 2, WIDTH)
    copies[3].wait()
    out_ref[:, :, 3 * WIDTH : BASE] = cotangent[...].reshape(64, 2, OUT)


def forward_kernel(core_ref, sent_ref, share_ref, channels_ref, weights_ref, rows_ref):
    rows_ref[...] = sent_ref[...].reshape(ROWS, COLS)
    row = lax.broadcasted_iota(jnp.int32, (ROWS, ROWS), 0)
    col = lax.broadcasted_iota(jnp.int32, (ROWS, ROWS), 1)
    bias = jnp.where(((row ^ col) & 1) == 0, 0.0, -1e30)
    for index in range(HEADS):
        weights_ref[index] = head_products(rows_ref, 0, rows_ref, WIDTH, index)
    channels_ref[...] = dot(rows_ref[:, 3 * WIDTH : BASE], channel_order(), 1, 0).astype(BF16)
    for index in range(HEADS):
        scores = weights_ref[index] * INV_ROOT + bias
        powers = jnp.exp(scores - jnp.max(scores, axis=1, keepdims=True))
        weights_ref[index] = powers * (1.0 / jnp.sum(powers, axis=1, keepdims=True))
    for tile in range(TILES):
        rounded = [weights_ref[index].astype(BF16) for index in tile_heads(tile)]
        values = stacked_heads(rows_ref, 2 * WIDTH, tile)
        share_ref[:, lanes(tile)] = dot(jnp.concatenate(rounded, axis=1), values, 1, 0).astype(BF16)
    other = pl.multiple_of((1 - core_ref[0]) * HALF, HALF)
    share_ref[:, WIDTH:] = channels_ref[:, pl.ds(other, HALF)]


def weight_grad_kernel(core_ref, share_ref, received_ref, channels_ref, out_ref):
    own = pl.multiple_of(core_ref[0] * HALF, HALF)
    columns = jnp.concatenate([channels_ref[:, pl.ds(own, HALF)], received_ref[:, WIDTH:]], axis=0)
    features = jnp.concatenate([share_ref[:, :WIDTH], received_ref[:, :WIDTH]], axis=0)
    partial = dot(columns, features, 0, 0).astype(BF16)
    for piece, place, pair, tile in half_tiles():
        out_ref[piece, :, lanes(place)] = partial[pair * ROWS : (pair + 1) * ROWS, lanes(tile)]
    out_ref[3, :, lanes(PIECE_TILES - 1)] = jnp.zeros((ROWS, LANES), BF16)


def backward_kernel(
    core_ref, sent_ref, weights_ref, share_ref, channels_ref, mine_ref, theirs_ref,
    out_ref, rows_ref, matrix_ref, upstream_ref, grad_scores_ref,
):
    rows_ref[...] = sent_ref[...].reshape(ROWS, COLS)
    own = pl.multiple_of(core_ref[0] * HALF, HALF)
    other = pl.multiple_of((1 - core_ref[0]) * HALF, HALF)
    for piece, place, pair, tile in half_tiles():
        for start, half_ref in ((own, mine_ref), (other, theirs_ref)):
            matrix_ref[pl.ds(start + pair * ROWS, ROWS), lanes(tile)] = half_ref[
                piece, :, lanes(place)
            ]
    upstream_ref[...] = dot(channels_ref[...], matrix_ref[...], 1, 0).astype(BF16)
    products = [
        head_products(upstream_ref, 0, rows_ref, 2 * WIDTH, index) for index in range(HEADS)
    ]
    for index in range(HEADS):
        weights, grad_weights = weights_ref[index], products[index]
        centred = grad_weights - jnp.sum(weights * grad_weights, axis=1, keepdims=True)
        grad_scores_ref[index] = (weights * centred * INV_ROOT).astype(BF16)

    def put(start, value):
        out_ref[:, :, start : start + value.shape[1]] = value.astype(BF16).reshape(64, 2, -1)

    projected = dot(share_ref[:, :WIDTH], matrix_ref[...], 1, 1).astype(BF16)
    put(3 * WIDTH, dot(projected, channel_order(), 1, 1))
    for tile in range(TILES):
        heads = tile_heads(tile)
        grad_scores = [grad_scores_ref[index] for index in heads]
        rounded = [weights_ref[index].astype(BF16) for index in heads]
        across, down = jnp.concatenate(grad_scores, axis=1), jnp.concatenate(grad_scores, axis=0)
        put(tile * LANES, dot(across, stacked_heads(rows_ref, WIDTH, tile), 1, 0))
        put(WIDTH + tile * LANES, dot(down, stacked_heads(rows_ref, 0, tile), 0, 0))
        put(
            2 * WIDTH + tile * LANES,
            dot(jnp.concatenate(rounded, axis=0), stacked_heads(upstream_ref, 0, tile), 0, 0),
        )


def merge_kernel(terms_ref, results_ref, out_ref):
    total = terms_ref[0].astype(F32)
    for place in range(1, 4):
        total += terms_ref[place].astype(F32)
    out_ref[:, :, BASE:] = total.astype(BF16).reshape(64, 2, PIECE)


def owned_kernel(back_ref, out_ref):
    rows = back_ref[:, :, BASE:].reshape(ROWS, PIECE)
    target = lax.broadcasted_iota(jnp.int32, (8, ROWS), 0)
    source = lax.broadcasted_iota(jnp.int32, (8, ROWS), 1)
    chosen = target == 2 * ((source >> 4) & 3) + (source & 1)
    total = dot(jnp.where(chosen, 1.0, 0.0).astype(BF16), rows, 1, 0)
    for place in range(8):
        out_ref[place] = total


def total_kernel(terms_ref, out_ref):
    for core in range(2):
        total = terms_ref[core] + terms_ref[2 + core] + terms_ref[4 + core] + terms_ref[6 + core]
        total = total * GRAD_SCALE
        for piece, place, pair, tile in half_tiles():
            start = 6 * core + 2 * pair
            out_ref[start : start + 2, lanes(tile)] = total[
                2 * piece : 2 * piece + 2, lanes(place)
            ]


IN_VMEM = pl.BlockSpec(memory_space=pltpu.VMEM)
IN_SMEM = pl.BlockSpec(memory_space=pltpu.SMEM)
IN_HBM = pl.BlockSpec(memory_space=pltpu.HBM)


def call(kernel, name, operands, specs, outs, scratch=(), aliases=None, grant=12, micros=1):
    return pl.pallas_call(
        kernel,
        out_shape=[jax.ShapeDtypeStruct(shape, dtype) for shape, dtype in outs],
        in_specs=specs,
        out_specs=[IN_VMEM] * len(outs),
        scratch_shapes=list(scratch),
        input_output_aliases=aliases or {},
        compiler_params=pltpu.CompilerParams(vmem_limit_bytes=grant << 20),
        cost_estimate=pl.CostEstimate(
            flops=micros * 10**9, bytes_accessed=micros * 3 * 10**6, transcendentals=0
        ),
        name=name,
    )(*operands)


def exchange(value, axes):
    return lax.all_to_all(value, axes, 0, 0, tiled=True)


def swap(value):
    return lax.ppermute(value, "c", [(0, 1), (1, 0)])


def on_device(query_key_value, out_weight, cotangent):
    core = lax.axis_index("c").astype(jnp.int32).reshape(1)
    (packed,) = call(
        pack_kernel,
        "pack",
        (core, query_key_value.reshape(3, ROWS, WIDTH), cotangent.reshape(ROWS, OUT), out_weight),
        [IN_SMEM] + [IN_HBM] * 3,
        [((64, 2, COLS), BF16)],
        [
            pltpu.VMEM((3, ROWS, WIDTH), BF16),
            pltpu.VMEM((ROWS, OUT), BF16),
            pltpu.VMEM((12, WIDTH), BF16),
            pltpu.SemaphoreType.DMA((5,)),
        ],
        grant=56,
    )
    sent = exchange(packed, SEQ)
    piece = sent[:, :, BASE:].reshape(1, ROWS, PIECE)
    mine = exchange(jnp.broadcast_to(piece, (4, ROWS, PIECE)), "x")
    share, channels, weights = call(
        forward_kernel,
        "forward",
        (core, sent),
        [IN_SMEM, IN_VMEM],
        [((ROWS, WIDTH + HALF), BF16), ((ROWS, OUT), BF16), ((HEADS, ROWS, ROWS), F32)],
        [pltpu.VMEM((ROWS, COLS), BF16)],
        micros=3,
    )
    (partial,) = call(
        weight_grad_kernel,
        "weight_grad",
        (core, share, swap(share), channels),
        [IN_SMEM] + [IN_VMEM] * 3,
        [((4, ROWS, PIECE), BF16)],
    )
    mine, _ = lax.optimization_barrier((mine, share))
    partial, theirs = lax.optimization_barrier((partial, swap(mine)))
    terms = exchange(partial, "x")
    (results,) = call(
        backward_kernel,
        "backward",
        (core, sent, weights, share, channels, mine, theirs),
        [IN_SMEM] + [IN_VMEM] * 6,
        [((64, 2, COLS), BF16)],
        [
            pltpu.VMEM((ROWS, COLS), BF16),
            pltpu.VMEM((OUT, WIDTH), BF16),
            pltpu.VMEM((ROWS, WIDTH), BF16),
            pltpu.VMEM((HEADS, ROWS, ROWS), BF16),
        ],
        micros=4,
    )
    (results,) = call(
        merge_kernel, "merge", (terms, results), [IN_VMEM] * 2, [((64, 2, COLS), BF16)], (), {1: 0}
    )
    back = exchange(results, SEQ)
    (owned,) = call(owned_kernel, "owned", (back,), [IN_VMEM], [((8, 8, PIECE), F32)])
    (total,) = call(
        total_kernel, "total", (exchange(owned, GROUPS),), [IN_VMEM], [((12, WIDTH), F32)]
    )
    frames = back.reshape(ROWS, COLS)
    grads = jnp.stack([frames[:, part * WIDTH : (part + 1) * WIDTH] for part in range(3)])
    return (
        frames[:, 3 * WIDTH : BASE].reshape(1, 1, ROWS, OUT),
        grads.reshape(3, 1, 1, ROWS, WIDTH),
        total,
    )


def solution(mesh):
    split = Mesh(mesh.devices.reshape(4, 2, 2, 4, 8), ("yl", "c", "yh", "x", "z"))
    in_specs = (P(None, GROUPS, SEQ, None, None), P(SEQ, None), P(GROUPS, SEQ, None, None))
    out_specs = (P(GROUPS, SEQ, None, None), P(None, GROUPS, SEQ, None, None), P(SEQ, None))
    return jax.shard_map(
        on_device, mesh=split, in_specs=in_specs, out_specs=out_specs, check_vma=False
    )
```

```python
import math

import jax
import jax.numpy as jnp
from jax import lax
from jax.experimental import pallas as pl
from jax.experimental.pallas import tpu as pltpu
from jax.sharding import Mesh
from jax.sharding import PartitionSpec as P

HEADS = 16
HEAD_DIM = 72
ROWS = 128
LANES = 128
WIDTH = 1152
TILES = WIDTH // LANES
OUT = 768
HALF = OUT // 2
BASE = 3 * WIDTH + OUT
PIECE = 896
PIECE_TILES = PIECE // LANES
COLS = BASE + PIECE
INV_ROOT = 1.0 / math.sqrt(HEAD_DIM)
GRAD_SCALE = 1.0 / math.sqrt(512 * ROWS)
BF16 = jnp.bfloat16
F32 = jnp.float32

SEQ = ("yh", "x", "z")
GROUPS = ("yl", "c")


def dot(lhs, rhs, lhs_dim, rhs_dim):
    return lax.dot_general(
        lhs, rhs, (((lhs_dim,), (rhs_dim,)), ((), ())), preferred_element_type=F32
    )


def lanes(tile, base=0):
    return slice(base + tile * LANES, base + (tile + 1) * LANES)


def only_head(index, start, value):
    feature = lax.broadcasted_iota(jnp.int32, value.shape, 1) + start
    inside = (feature >= index * HEAD_DIM) & (feature < (index + 1) * HEAD_DIM)
    return jnp.where(inside, value, jnp.zeros_like(value))


def head_lanes(index):
    first = index * HEAD_DIM // LANES
    last = ((index + 1) * HEAD_DIM - 1) // LANES + 1
    return first * LANES, last * LANES


def head_products(lhs_ref, lhs_base, rhs_ref, rhs_base, index):
    start, stop = head_lanes(index)
    rhs = only_head(index, start, rhs_ref[:, rhs_base + start : rhs_base + stop])
    return dot(lhs_ref[:, lhs_base + start : lhs_base + stop], rhs, 1, 1)


def tile_heads(tile):
    return [
        index
        for index in range(HEADS)
        if index * HEAD_DIM < (tile + 1) * LANES and (index + 1) * HEAD_DIM > tile * LANES
    ]


def stacked_heads(ref, base, tile):
    value = ref[:, lanes(tile, base)]
    return jnp.concatenate(
        [only_head(index, tile * LANES, value) for index in tile_heads(tile)], axis=0
    )


def channel_order():
    natural = lax.broadcasted_iota(jnp.int32, (OUT, OUT), 0)
    place = lax.broadcasted_iota(jnp.int32, (OUT, OUT), 1)
    source = 12 * ((place & 127) >> 1) + 2 * (place >> 7) + (place & 1)
    return jnp.where(natural == source, 1.0, 0.0).astype(BF16)


def half_tiles():
    return [
        (tile // PIECE_TILES, tile % PIECE_TILES, tile // TILES, tile % TILES)
        for tile in range(3 * TILES)
    ]


def pack_kernel(
    place_ref, parts_hbm, cotangent_hbm, weight_hbm, out_ref, parts, cotangent, weight, sems
):
    pairs = [(parts_hbm.at[part], parts.at[part]) for part in range(3)]
    pairs += [(cotangent_hbm, cotangent), (weight_hbm, weight)]
    copies = [
        pltpu.make_async_copy(source, target, sems.at[place])
        for place, (source, target) in enumerate(pairs)
    ]
    for copy in copies:
        copy.start()
    row = lax.broadcasted_iota(jnp.int32, (ROWS, 12), 0)
    col = lax.broadcasted_iota(jnp.int32, (ROWS, 12), 1)
    copies[4].wait()
    repeated = []
    for pair in range(3):
        chosen = col == 6 * place_ref[0] + 2 * pair + (row & 1)
        repeated.append(
            dot(jnp.where(chosen, 1.0, 0.0).astype(BF16), weight[...], 1, 0).astype(BF16)
        )
    column = (lax.broadcasted_iota(jnp.int32, (ROWS, LANES), 0) >> 4) & 3
    for place in range(PIECE_TILES):
        value = jnp.zeros((ROWS, LANES), BF16)
        for piece, at, pair, tile in half_tiles():
            if at == place:
                value = jnp.where(column == piece, repeated[pair][:, lanes(tile)], value)
        out_ref[:, :, lanes(place, BASE)] = value.reshape(64, 2, LANES)
    for part in range(3):
        copies[part].wait()
        out_ref[:, :, part * WIDTH : (part + 1) * WIDTH] = parts[part].reshape(64, 2, WIDTH)
    copies[3].wait()
    out_ref[:, :, 3 * WIDTH : BASE] = cotangent[...].reshape(64, 2, OUT)


def attend(rows_ref, weights_ref, put):
    row = lax.broadcasted_iota(jnp.int32, (ROWS, ROWS), 0)
    col = lax.broadcasted_iota(jnp.int32, (ROWS, ROWS), 1)
    bias = jnp.where(((row ^ col) & 1) == 0, 0.0, -1e30)
    for index in range(HEADS):
        weights_ref[index] = head_products(rows_ref, 0, rows_ref, WIDTH, index)
    for index in range(HEADS):
        scores = weights_ref[index] * INV_ROOT + bias
        powers = jnp.exp(scores - jnp.max(scores, axis=1, keepdims=True))
        weights_ref[index] = powers * (1.0 / jnp.sum(powers, axis=1, keepdims=True))
    for tile in range(TILES):
        rounded = [weights_ref[index].astype(BF16) for index in tile_heads(tile)]
        values = stacked_heads(rows_ref, 2 * WIDTH, tile)
        put(tile, dot(jnp.concatenate(rounded, axis=1), values, 1, 0).astype(BF16))


def ordered_channels(rows_ref):
    return dot(rows_ref[:, 3 * WIDTH : BASE], channel_order(), 1, 0).astype(BF16)


def forward_kernel(place_ref, sent_ref, share_ref, columns_ref, rows_ref, weights_ref, channels_ref):
    rows_ref[...] = sent_ref[...].reshape(ROWS, COLS)
    channels_ref[...] = ordered_channels(rows_ref)

    def put(tile, value):
        share_ref[:, lanes(tile)] = value

    attend(rows_ref, weights_ref, put)
    own = pl.multiple_of(place_ref[0] * HALF, HALF)
    other = pl.multiple_of((1 - place_ref[0]) * HALF, HALF)
    columns_ref[...] = channels_ref[:, pl.ds(own, HALF)]
    share_ref[:, WIDTH:] = channels_ref[:, pl.ds(other, HALF)]


def weight_grad_kernel(place_ref, share_ref, received_ref, columns_ref, *out_refs):
    columns = jnp.concatenate([columns_ref[...], received_ref[:, WIDTH:]], axis=0)
    features = jnp.concatenate([share_ref[:, :WIDTH], received_ref[:, :WIDTH]], axis=0)
    partial = dot(columns, features, 0, 0).astype(BF16)
    for step, out_ref in enumerate(out_refs):
        target = (place_ref[1] + step) & 3
        for chosen in range(4):

            @pl.when(target == chosen)
            def _():
                for piece, place, pair, tile in half_tiles():
                    if piece == chosen:
                        out_ref[:, lanes(place)] = partial[
                            pair * ROWS : (pair + 1) * ROWS, lanes(tile)
                        ]
                if chosen == 3:
                    out_ref[:, lanes(PIECE_TILES - 1)] = jnp.zeros((ROWS, LANES), BF16)


def backward_kernel(
    place_ref, sent_ref, mine_ref, theirs_ref,
    out_ref, rows_ref, weights_ref, channels_ref, attended_ref, matrix_ref, upstream_ref,
    grad_scores_ref,
):
    rows_ref[...] = sent_ref[...].reshape(ROWS, COLS)
    channels_ref[...] = ordered_channels(rows_ref)

    def put_attended(tile, value):
        attended_ref[:, lanes(tile)] = value

    attend(rows_ref, weights_ref, put_attended)
    own = pl.multiple_of(place_ref[0] * HALF, HALF)
    other = pl.multiple_of((1 - place_ref[0]) * HALF, HALF)
    for piece, place, pair, tile in half_tiles():
        for start, half_ref in ((own, mine_ref), (other, theirs_ref)):
            matrix_ref[pl.ds(start + pair * ROWS, ROWS), lanes(tile)] = half_ref[
                piece, :, lanes(place)
            ]
    upstream_ref[...] = dot(channels_ref[...], matrix_ref[...], 1, 0).astype(BF16)
    products = [
        head_products(upstream_ref, 0, rows_ref, 2 * WIDTH, index) for index in range(HEADS)
    ]
    for index in range(HEADS):
        weights, grad_weights = weights_ref[index], products[index]
        centred = grad_weights - jnp.sum(weights * grad_weights, axis=1, keepdims=True)
        grad_scores_ref[index] = (weights * centred * INV_ROOT).astype(BF16)

    def put(start, value):
        out_ref[:, :, start : start + value.shape[1]] = value.astype(BF16).reshape(64, 2, -1)

    projected = dot(attended_ref[...], matrix_ref[...], 1, 1).astype(BF16)
    put(3 * WIDTH, dot(projected, channel_order(), 1, 1))
    for tile in range(TILES):
        heads = tile_heads(tile)
        grad_scores = [grad_scores_ref[index] for index in heads]
        rounded = [weights_ref[index].astype(BF16) for index in heads]
        across, down = jnp.concatenate(grad_scores, axis=1), jnp.concatenate(grad_scores, axis=0)
        put(tile * LANES, dot(across, stacked_heads(rows_ref, WIDTH, tile), 1, 0))
        put(WIDTH + tile * LANES, dot(down, stacked_heads(rows_ref, 0, tile), 0, 0))
        put(
            2 * WIDTH + tile * LANES,
            dot(jnp.concatenate(rounded, axis=0), stacked_heads(upstream_ref, 0, tile), 0, 0),
        )


def merge_kernel(*refs):
    *terms, _, out_ref = refs
    total = terms[0][...].astype(F32)
    for term in terms[1:]:
        total += term[...].astype(F32)
    out_ref[:, :, BASE:] = total.astype(BF16).reshape(64, 2, PIECE)


def owned_kernel(back_ref, out_ref):
    rows = back_ref[:, :, BASE:].reshape(ROWS, PIECE)
    target = lax.broadcasted_iota(jnp.int32, (8, ROWS), 0)
    source = lax.broadcasted_iota(jnp.int32, (8, ROWS), 1)
    chosen = target == 2 * ((source >> 4) & 3) + (source & 1)
    out_ref[...] = dot(jnp.where(chosen, 1.0, 0.0).astype(BF16), rows, 1, 0)


def group_kernel(*refs):
    *terms, out_ref = refs
    total = terms[0][...]
    for term in terms[1:]:
        total += term[...]
    out_ref[...] = total * GRAD_SCALE


def total_kernel(place_ref, mine_ref, theirs_ref, out_ref):
    for core in range(2):
        total = jnp.where(place_ref[0] == core, mine_ref[...], theirs_ref[...])
        for piece, place, pair, tile in half_tiles():
            start = 6 * core + 2 * pair
            out_ref[start : start + 2, lanes(tile)] = total[
                2 * piece : 2 * piece + 2, lanes(place)
            ]


IN_VMEM = pl.BlockSpec(memory_space=pltpu.VMEM)
IN_SMEM = pl.BlockSpec(memory_space=pltpu.SMEM)
IN_HBM = pl.BlockSpec(memory_space=pltpu.HBM)


def call(kernel, name, operands, specs, outs, scratch=(), aliases=None, grant=12, micros=1):
    return pl.pallas_call(
        kernel,
        out_shape=[jax.ShapeDtypeStruct(shape, dtype) for shape, dtype in outs],
        in_specs=specs,
        out_specs=[IN_VMEM] * len(outs),
        scratch_shapes=list(scratch),
        input_output_aliases=aliases or {},
        compiler_params=pltpu.CompilerParams(vmem_limit_bytes=grant << 20),
        cost_estimate=pl.CostEstimate(
            flops=micros * 10**9, bytes_accessed=micros * 3 * 10**6, transcendentals=0
        ),
        name=name,
    )(*operands)


def exchange(value, axes):
    return lax.all_to_all(value, axes, 0, 0, tiled=True)


def swap(value):
    return lax.ppermute(value, "c", [(0, 1), (1, 0)])


def turn(value, axis, step):
    return lax.ppermute(value, axis, [(place, (place + step) % 4) for place in range(4)])


def on_device(query_key_value, out_weight, cotangent):
    place = jnp.stack([lax.axis_index("c"), lax.axis_index("x")]).astype(jnp.int32)
    (packed,) = call(
        pack_kernel,
        "pack",
        (place, query_key_value.reshape(3, ROWS, WIDTH), cotangent.reshape(ROWS, OUT), out_weight),
        [IN_SMEM] + [IN_HBM] * 3,
        [((64, 2, COLS), BF16)],
        [
            pltpu.VMEM((3, ROWS, WIDTH), BF16),
            pltpu.VMEM((ROWS, OUT), BF16),
            pltpu.VMEM((12, WIDTH), BF16),
            pltpu.SemaphoreType.DMA((5,)),
        ],
        grant=56,
    )
    sent = exchange(packed, SEQ)
    piece = sent[:, :, BASE:].reshape(1, ROWS, PIECE)
    mine = exchange(jnp.broadcast_to(piece, (4, ROWS, PIECE)), "x")
    share, columns = call(
        forward_kernel,
        "forward",
        (place, sent),
        [IN_SMEM, IN_VMEM],
        [((ROWS, WIDTH + HALF), BF16), ((ROWS, HALF), BF16)],
        [
            pltpu.VMEM((ROWS, COLS), BF16),
            pltpu.VMEM((HEADS, ROWS, ROWS), F32),
            pltpu.VMEM((ROWS, OUT), BF16),
        ],
        micros=3,
    )
    partial = call(
        weight_grad_kernel,
        "weight_grad",
        (place, share, swap(share), columns),
        [IN_SMEM] + [IN_VMEM] * 3,
        [((ROWS, PIECE), BF16)] * 4,
    )
    terms = [partial[0]] + [turn(partial[step], "x", step) for step in range(1, 4)]
    mine, _ = lax.optimization_barrier((mine, partial[0]))
    (results,) = call(
        backward_kernel,
        "backward",
        (place, sent, mine, swap(mine)),
        [IN_SMEM] + [IN_VMEM] * 3,
        [((64, 2, COLS), BF16)],
        [
            pltpu.VMEM((ROWS, COLS), BF16),
            pltpu.VMEM((HEADS, ROWS, ROWS), F32),
            pltpu.VMEM((ROWS, OUT), BF16),
            pltpu.VMEM((ROWS, WIDTH), BF16),
            pltpu.VMEM((OUT, WIDTH), BF16),
            pltpu.VMEM((ROWS, WIDTH), BF16),
            pltpu.VMEM((HEADS, ROWS, ROWS), BF16),
        ],
        micros=4,
    )
    (results,) = call(
        merge_kernel,
        "merge",
        (*terms, results),
        [IN_VMEM] * 5,
        [((64, 2, COLS), BF16)],
        aliases={4: 0},
    )
    back = exchange(results, SEQ)
    (owned,) = call(owned_kernel, "owned", (back,), [IN_VMEM], [((8, PIECE), F32)])
    (group,) = call(
        group_kernel,
        "group",
        (owned, *(turn(owned, "yl", step) for step in range(1, 4))),
        [IN_VMEM] * 4,
        [((8, PIECE), F32)],
    )
    (total,) = call(
        total_kernel,
        "total",
        (place, group, swap(group)),
        [IN_SMEM] + [IN_VMEM] * 2,
        [((12, WIDTH), F32)],
    )
    frames = back.reshape(ROWS, COLS)
    grads = jnp.stack([frames[:, part * WIDTH : (part + 1) * WIDTH] for part in range(3)])
    return (
        frames[:, 3 * WIDTH : BASE].reshape(1, 1, ROWS, OUT),
        grads.reshape(3, 1, 1, ROWS, WIDTH),
        total,
    )


def solution(mesh):
    split = Mesh(mesh.devices.reshape(4, 2, 2, 4, 8), ("yl", "c", "yh", "x", "z"))
    in_specs = (P(None, GROUPS, SEQ, None, None), P(SEQ, None), P(GROUPS, SEQ, None, None))
    out_specs = (P(GROUPS, SEQ, None, None), P(None, GROUPS, SEQ, None, None), P(SEQ, None))
    return jax.shard_map(
        on_device, mesh=split, in_specs=in_specs, out_specs=out_specs, check_vma=False
    )
```

```python
import math

import jax
import jax.numpy as jnp
from jax import lax
from jax.experimental import pallas as pl
from jax.experimental.pallas import tpu as pltpu
from jax.sharding import Mesh
from jax.sharding import PartitionSpec as P

HEADS = 16
HEAD_DIM = 72
ROWS = 128
LANES = 128
WIDTH = 1152
TILES = WIDTH // LANES
OUT = 768
HALF = OUT // 2
BASE = 3 * WIDTH + OUT
PIECE = 896
PIECE_TILES = PIECE // LANES
COLS = BASE + PIECE
HALF_WIDTH = 3 * WIDTH
INV_ROOT = 1.0 / math.sqrt(HEAD_DIM)
GRAD_SCALE = 1.0 / math.sqrt(512 * ROWS)
BF16 = jnp.bfloat16
F32 = jnp.float32

SEQ = ("yh", "x", "z")
GROUPS = ("yl", "c")


def dot(lhs, rhs, lhs_dim, rhs_dim):
    return lax.dot_general(
        lhs, rhs, (((lhs_dim,), (rhs_dim,)), ((), ())), preferred_element_type=F32
    )


def lanes(tile, base=0):
    return slice(base + tile * LANES, base + (tile + 1) * LANES)


def only_head(index, start, value):
    feature = lax.broadcasted_iota(jnp.int32, value.shape, 1) + start
    inside = (feature >= index * HEAD_DIM) & (feature < (index + 1) * HEAD_DIM)
    return jnp.where(inside, value, jnp.zeros_like(value))


def head_lanes(index):
    first = index * HEAD_DIM // LANES
    last = ((index + 1) * HEAD_DIM - 1) // LANES + 1
    return first * LANES, last * LANES


def head_products(lhs_ref, lhs_base, rhs_ref, rhs_base, index):
    start, stop = head_lanes(index)
    rhs = only_head(index, start, rhs_ref[:, rhs_base + start : rhs_base + stop])
    return dot(lhs_ref[:, lhs_base + start : lhs_base + stop], rhs, 1, 1)


def tile_heads(tile):
    return [
        index
        for index in range(HEADS)
        if index * HEAD_DIM < (tile + 1) * LANES and (index + 1) * HEAD_DIM > tile * LANES
    ]


def stacked_heads(ref, base, tile):
    value = ref[:, lanes(tile, base)]
    return jnp.concatenate(
        [only_head(index, tile * LANES, value) for index in tile_heads(tile)], axis=0
    )


def channel_order():
    natural = lax.broadcasted_iota(jnp.int32, (OUT, OUT), 0)
    place = lax.broadcasted_iota(jnp.int32, (OUT, OUT), 1)
    source = 12 * ((place & 127) >> 1) + 2 * (place >> 7) + (place & 1)
    return jnp.where(natural == source, 1.0, 0.0).astype(BF16)


def half_tiles():
    return [
        (tile // PIECE_TILES, tile % PIECE_TILES, tile // TILES, tile % TILES)
        for tile in range(3 * TILES)
    ]


def pack_kernel(
    core_ref, parts_hbm, cotangent_hbm, weight_hbm, out_ref, parts, cotangent, weight, sems
):
    pairs = [(parts_hbm.at[part], parts.at[part]) for part in range(3)]
    pairs += [(cotangent_hbm, cotangent), (weight_hbm, weight)]
    copies = [
        pltpu.make_async_copy(source, target, sems.at[place])
        for place, (source, target) in enumerate(pairs)
    ]
    for copy in copies:
        copy.start()
    row = lax.broadcasted_iota(jnp.int32, (ROWS, 12), 0)
    col = lax.broadcasted_iota(jnp.int32, (ROWS, 12), 1)
    copies[4].wait()
    repeated = []
    for pair in range(3):
        chosen = col == 6 * core_ref[0] + 2 * pair + (row & 1)
        repeated.append(
            dot(jnp.where(chosen, 1.0, 0.0).astype(BF16), weight[...], 1, 0).astype(BF16)
        )
    column = (lax.broadcasted_iota(jnp.int32, (ROWS, LANES), 0) >> 4) & 3
    for place in range(PIECE_TILES):
        value = jnp.zeros((ROWS, LANES), BF16)
        for piece, at, pair, tile in half_tiles():
            if at == place:
                value = jnp.where(column == piece, repeated[pair][:, lanes(tile)], value)
        out_ref[:, :, lanes(place, BASE)] = value.reshape(64, 2, LANES)
    for part in range(3):
        copies[part].wait()
        out_ref[:, :, part * WIDTH : (part + 1) * WIDTH] = parts[part].reshape(64, 2, WIDTH)
    copies[3].wait()
    out_ref[:, :, 3 * WIDTH : BASE] = cotangent[...].reshape(64, 2, OUT)


def attend(rows_ref, weights_ref, put):
    row = lax.broadcasted_iota(jnp.int32, (ROWS, ROWS), 0)
    col = lax.broadcasted_iota(jnp.int32, (ROWS, ROWS), 1)
    bias = jnp.where(((row ^ col) & 1) == 0, 0.0, -1e30)
    for index in range(HEADS):
        weights_ref[index] = head_products(rows_ref, 0, rows_ref, WIDTH, index)
    for index in range(HEADS):
        scores = weights_ref[index] * INV_ROOT + bias
        powers = jnp.exp(scores - jnp.max(scores, axis=1, keepdims=True))
        weights_ref[index] = powers * (1.0 / jnp.sum(powers, axis=1, keepdims=True))
    for tile in range(TILES):
        rounded = [weights_ref[index].astype(BF16) for index in tile_heads(tile)]
        values = stacked_heads(rows_ref, 2 * WIDTH, tile)
        put(tile, dot(jnp.concatenate(rounded, axis=1), values, 1, 0).astype(BF16))


def ordered_channels(rows_ref):
    return dot(rows_ref[:, 3 * WIDTH : BASE], channel_order(), 1, 0).astype(BF16)


def forward_kernel(core_ref, sent_ref, share_ref, columns_ref, rows_ref, weights_ref, channels_ref):
    rows_ref[...] = sent_ref[...].reshape(ROWS, COLS)
    channels_ref[...] = ordered_channels(rows_ref)

    def put(tile, value):
        share_ref[:, lanes(tile)] = value

    attend(rows_ref, weights_ref, put)
    own = pl.multiple_of(core_ref[0] * HALF, HALF)
    other = pl.multiple_of((1 - core_ref[0]) * HALF, HALF)
    columns_ref[...] = channels_ref[:, pl.ds(own, HALF)]
    share_ref[:, WIDTH:] = channels_ref[:, pl.ds(other, HALF)]


def weight_grad_kernel(x_ref, share_ref, received_ref, columns_ref, *refs):
    *out_refs, partial_ref = refs
    columns = jnp.concatenate([columns_ref[...], received_ref[:, WIDTH:]], axis=0)
    features = jnp.concatenate([share_ref[:, :WIDTH], received_ref[:, :WIDTH]], axis=0)
    partial_ref[...] = dot(columns, features, 0, 0).astype(BF16)
    for step, out_ref in enumerate(out_refs):
        target = ((x_ref[0] + step) & 3) * 16
        for high in range(2):
            for pair in range(3):
                start = pl.multiple_of(pair * ROWS + high * 64 + target, 16)
                out_ref[high * 16 : high * 16 + 16, pair * WIDTH : (pair + 1) * WIDTH] = (
                    partial_ref[pl.ds(start, 16), :]
                )


def backward_kernel(
    core_ref, sent_ref, mine_ref, theirs_ref,
    out_ref, rows_ref, weights_ref, channels_ref, attended_ref, matrix_ref, upstream_ref,
    grad_scores_ref,
):
    rows_ref[...] = sent_ref[...].reshape(ROWS, COLS)
    channels_ref[...] = ordered_channels(rows_ref)

    def put_attended(tile, value):
        attended_ref[:, lanes(tile)] = value

    attend(rows_ref, weights_ref, put_attended)
    own = pl.multiple_of(core_ref[0] * HALF, HALF)
    other = pl.multiple_of((1 - core_ref[0]) * HALF, HALF)
    for piece, place, pair, tile in half_tiles():
        for start, half_ref in ((own, mine_ref), (other, theirs_ref)):
            matrix_ref[pl.ds(start + pair * ROWS, ROWS), lanes(tile)] = half_ref[
                piece, :, lanes(place)
            ]
    upstream_ref[...] = dot(channels_ref[...], matrix_ref[...], 1, 0).astype(BF16)
    products = [
        head_products(upstream_ref, 0, rows_ref, 2 * WIDTH, index) for index in range(HEADS)
    ]
    for index in range(HEADS):
        weights, grad_weights = weights_ref[index], products[index]
        centred = grad_weights - jnp.sum(weights * grad_weights, axis=1, keepdims=True)
        grad_scores_ref[index] = (weights * centred * INV_ROOT).astype(BF16)

    def put(start, value):
        out_ref[:, :, start : start + value.shape[1]] = value.astype(BF16).reshape(64, 2, -1)

    projected = dot(attended_ref[...], matrix_ref[...], 1, 1).astype(BF16)
    put(3 * WIDTH, dot(projected, channel_order(), 1, 1))
    for tile in range(TILES):
        heads = tile_heads(tile)
        grad_scores = [grad_scores_ref[index] for index in heads]
        rounded = [weights_ref[index].astype(BF16) for index in heads]
        across, down = jnp.concatenate(grad_scores, axis=1), jnp.concatenate(grad_scores, axis=0)
        put(tile * LANES, dot(across, stacked_heads(rows_ref, WIDTH, tile), 1, 0))
        put(WIDTH + tile * LANES, dot(down, stacked_heads(rows_ref, 0, tile), 0, 0))
        put(
            2 * WIDTH + tile * LANES,
            dot(jnp.concatenate(rounded, axis=0), stacked_heads(upstream_ref, 0, tile), 0, 0),
        )


def merge_kernel(*refs):
    *terms, out_ref = refs
    total = terms[0][...].astype(F32)
    for term in terms[1:]:
        total += term[...].astype(F32)
    out_ref[...] = total.astype(BF16).reshape(16, 2, HALF_WIDTH)


def owned_kernel(terms_ref, out_ref):
    rows = terms_ref[...].reshape(32, HALF_WIDTH)
    target = lax.broadcasted_iota(jnp.int32, (8, 32), 0)
    source = lax.broadcasted_iota(jnp.int32, (8, 32), 1)
    chosen = jnp.where(target == (source & 1), 1.0, 0.0).astype(BF16)
    out_ref[...] = dot(chosen, rows, 1, 0)[:2]


def group_kernel(*refs):
    *terms, out_ref = refs
    total = terms[0][...]
    for term in terms[1:]:
        total += term[...]
    out_ref[...] = total * GRAD_SCALE


def total_kernel(core_ref, mine_ref, theirs_ref, out_ref):
    for core in range(2):
        total = jnp.where(core_ref[0] == core, mine_ref[...], theirs_ref[...])
        for pair in range(3):
            start = 6 * core + 2 * pair
            out_ref[start : start + 2, :] = total[:, pair * WIDTH : (pair + 1) * WIDTH]


IN_VMEM = pl.BlockSpec(memory_space=pltpu.VMEM)
IN_SMEM = pl.BlockSpec(memory_space=pltpu.SMEM)
IN_HBM = pl.BlockSpec(memory_space=pltpu.HBM)


def call(kernel, name, operands, specs, outs, scratch=(), aliases=None, grant=12, micros=1):
    return pl.pallas_call(
        kernel,
        out_shape=[jax.ShapeDtypeStruct(shape, dtype) for shape, dtype in outs],
        in_specs=specs,
        out_specs=[IN_VMEM] * len(outs),
        scratch_shapes=list(scratch),
        input_output_aliases=aliases or {},
        compiler_params=pltpu.CompilerParams(vmem_limit_bytes=grant << 20),
        cost_estimate=pl.CostEstimate(
            flops=micros * 10**9, bytes_accessed=micros * 3 * 10**6, transcendentals=0
        ),
        name=name,
    )(*operands)


def exchange(value, axes):
    return lax.all_to_all(value, axes, 0, 0, tiled=True)


def swap(value):
    return lax.ppermute(value, "c", [(0, 1), (1, 0)])


def turn(value, axis, step):
    return lax.ppermute(value, axis, [(place, (place + step) % 4) for place in range(4)])


def on_device(query_key_value, out_weight, cotangent):
    core = lax.axis_index("c").astype(jnp.int32).reshape(1)
    x_place = lax.axis_index("x").astype(jnp.int32).reshape(1)
    (packed,) = call(
        pack_kernel,
        "pack",
        (core, query_key_value.reshape(3, ROWS, WIDTH), cotangent.reshape(ROWS, OUT), out_weight),
        [IN_SMEM] + [IN_HBM] * 3,
        [((64, 2, COLS), BF16)],
        [
            pltpu.VMEM((3, ROWS, WIDTH), BF16),
            pltpu.VMEM((ROWS, OUT), BF16),
            pltpu.VMEM((12, WIDTH), BF16),
            pltpu.SemaphoreType.DMA((5,)),
        ],
        grant=56,
    )
    sent = exchange(packed, SEQ)
    share, columns = call(
        forward_kernel,
        "forward",
        (core, sent),
        [IN_SMEM, IN_VMEM],
        [((ROWS, WIDTH + HALF), BF16), ((ROWS, HALF), BF16)],
        [
            pltpu.VMEM((ROWS, COLS), BF16),
            pltpu.VMEM((HEADS, ROWS, ROWS), F32),
            pltpu.VMEM((ROWS, OUT), BF16),
        ],
        micros=3,
    )
    piece, _ = lax.optimization_barrier((sent[:, :, BASE:], share))
    mine = exchange(jnp.broadcast_to(piece.reshape(1, ROWS, PIECE), (4, ROWS, PIECE)), "x")
    partial = call(
        weight_grad_kernel,
        "weight_grad",
        (x_place, share, swap(share), columns),
        [IN_SMEM] + [IN_VMEM] * 3,
        [((32, HALF_WIDTH), BF16)] * 4,
        [pltpu.VMEM((HALF, WIDTH), BF16)],
    )
    terms = [partial[0]] + [turn(partial[step], "x", step) for step in range(1, 4)]
    (summed,) = call(
        merge_kernel, "merge", terms, [IN_VMEM] * 4, [((16, 2, HALF_WIDTH), BF16)]
    )
    mine, summed = lax.optimization_barrier((mine, summed))
    (results,) = call(
        backward_kernel,
        "backward",
        (core, sent, mine, swap(mine)),
        [IN_SMEM] + [IN_VMEM] * 3,
        [((64, 2, BASE), BF16)],
        [
            pltpu.VMEM((ROWS, COLS), BF16),
            pltpu.VMEM((HEADS, ROWS, ROWS), F32),
            pltpu.VMEM((ROWS, OUT), BF16),
            pltpu.VMEM((ROWS, WIDTH), BF16),
            pltpu.VMEM((OUT, WIDTH), BF16),
            pltpu.VMEM((ROWS, WIDTH), BF16),
            pltpu.VMEM((HEADS, ROWS, ROWS), BF16),
        ],
        micros=4,
    )
    collected = exchange(summed, ("yh", "z"))
    results, collected = lax.optimization_barrier((results, collected))
    (owned,) = call(owned_kernel, "owned", (collected,), [IN_VMEM], [((2, HALF_WIDTH), F32)])
    turned = [turn(owned, "yl", step) for step in range(1, 4)]
    back = exchange(results, SEQ)
    (group,) = call(
        group_kernel, "group", (owned, *turned), [IN_VMEM] * 4, [((2, HALF_WIDTH), F32)]
    )
    (total,) = call(
        total_kernel,
        "total",
        (core, group, swap(group)),
        [IN_SMEM] + [IN_VMEM] * 2,
        [((12, WIDTH), F32)],
    )
    frames = back.reshape(ROWS, BASE)
    grads = jnp.stack([frames[:, part * WIDTH : (part + 1) * WIDTH] for part in range(3)])
    return (
        frames[:, 3 * WIDTH :].reshape(1, 1, ROWS, OUT),
        grads.reshape(3, 1, 1, ROWS, WIDTH),
        total,
    )


def solution(mesh):
    split = Mesh(mesh.devices.reshape(4, 2, 2, 4, 8), ("yl", "c", "yh", "x", "z"))
    in_specs = (P(None, GROUPS, SEQ, None, None), P(SEQ, None), P(GROUPS, SEQ, None, None))
    out_specs = (P(GROUPS, SEQ, None, None), P(None, GROUPS, SEQ, None, None), P(SEQ, None))
    return jax.shard_map(
        on_device, mesh=split, in_specs=in_specs, out_specs=out_specs, check_vma=False
    )
```

```python
import math

import jax
import jax.numpy as jnp
from jax import lax
from jax.experimental import pallas as pl
from jax.experimental.pallas import tpu as pltpu
from jax.sharding import Mesh
from jax.sharding import PartitionSpec as P

HEADS = 16
HEAD_DIM = 72
ROWS = 128
LANES = 128
WIDTH = 1152
TILES = WIDTH // LANES
OUT = 768
HALF = OUT // 2
BASE = 3 * WIDTH + OUT
PIECE = 896
PIECE_TILES = PIECE // LANES
COLS = BASE + PIECE
HALF_WIDTH = 3 * WIDTH
INV_ROOT = 1.0 / math.sqrt(HEAD_DIM)
GRAD_SCALE = 1.0 / math.sqrt(512 * ROWS)
BF16 = jnp.bfloat16
F32 = jnp.float32

SEQ = ("yh", "x", "z")
GROUPS = ("yl", "c")


def dot(lhs, rhs, lhs_dim, rhs_dim):
    return lax.dot_general(
        lhs, rhs, (((lhs_dim,), (rhs_dim,)), ((), ())), preferred_element_type=F32
    )


def lanes(tile, base=0):
    return slice(base + tile * LANES, base + (tile + 1) * LANES)


def only_head(index, start, value):
    feature = lax.broadcasted_iota(jnp.int32, value.shape, 1) + start
    inside = (feature >= index * HEAD_DIM) & (feature < (index + 1) * HEAD_DIM)
    return jnp.where(inside, value, jnp.zeros_like(value))


def head_lanes(index):
    first = index * HEAD_DIM // LANES
    last = ((index + 1) * HEAD_DIM - 1) // LANES + 1
    return first * LANES, last * LANES


def head_products(lhs_ref, lhs_base, rhs_ref, rhs_base, index):
    start, stop = head_lanes(index)
    rhs = only_head(index, start, rhs_ref[:, rhs_base + start : rhs_base + stop])
    return dot(lhs_ref[:, lhs_base + start : lhs_base + stop], rhs, 1, 1)


def tile_heads(tile):
    return [
        index
        for index in range(HEADS)
        if index * HEAD_DIM < (tile + 1) * LANES and (index + 1) * HEAD_DIM > tile * LANES
    ]


def stacked_heads(ref, base, tile):
    value = ref[:, lanes(tile, base)]
    return jnp.concatenate(
        [only_head(index, tile * LANES, value) for index in tile_heads(tile)], axis=0
    )


def channel_order():
    natural = lax.broadcasted_iota(jnp.int32, (OUT, OUT), 0)
    place = lax.broadcasted_iota(jnp.int32, (OUT, OUT), 1)
    source = 12 * ((place & 127) >> 1) + 2 * (place >> 7) + (place & 1)
    return jnp.where(natural == source, 1.0, 0.0).astype(BF16)


def half_tiles():
    return [
        (tile // PIECE_TILES, tile % PIECE_TILES, tile // TILES, tile % TILES)
        for tile in range(3 * TILES)
    ]


def pack_kernel(
    core_ref, parts_hbm, cotangent_hbm, weight_hbm, out_ref, parts, cotangent, weight, sems
):
    pairs = [(parts_hbm.at[part], parts.at[part]) for part in range(3)]
    pairs += [(cotangent_hbm, cotangent), (weight_hbm, weight)]
    copies = [
        pltpu.make_async_copy(source, target, sems.at[place])
        for place, (source, target) in enumerate(pairs)
    ]
    for copy in copies:
        copy.start()
    row = lax.broadcasted_iota(jnp.int32, (ROWS, 12), 0)
    col = lax.broadcasted_iota(jnp.int32, (ROWS, 12), 1)
    copies[4].wait()
    repeated = []
    for pair in range(3):
        chosen = col == 6 * core_ref[0] + 2 * pair + (row & 1)
        repeated.append(
            dot(jnp.where(chosen, 1.0, 0.0).astype(BF16), weight[...], 1, 0).astype(BF16)
        )
    column = (lax.broadcasted_iota(jnp.int32, (ROWS, LANES), 0) >> 4) & 3
    for place in range(PIECE_TILES):
        value = jnp.zeros((ROWS, LANES), BF16)
        for piece, at, pair, tile in half_tiles():
            if at == place:
                value = jnp.where(column == piece, repeated[pair][:, lanes(tile)], value)
        out_ref[:, :, lanes(place, BASE)] = value.reshape(64, 2, LANES)
    for part in range(3):
        copies[part].wait()
        out_ref[:, :, part * WIDTH : (part + 1) * WIDTH] = parts[part].reshape(64, 2, WIDTH)
    copies[3].wait()
    out_ref[:, :, 3 * WIDTH : BASE] = cotangent[...].reshape(64, 2, OUT)


def attend(rows_ref, weights_ref, put):
    row = lax.broadcasted_iota(jnp.int32, (ROWS, ROWS), 0)
    col = lax.broadcasted_iota(jnp.int32, (ROWS, ROWS), 1)
    bias = jnp.where(((row ^ col) & 1) == 0, 0.0, -1e30)
    for index in range(HEADS):
        weights_ref[index] = head_products(rows_ref, 0, rows_ref, WIDTH, index)
    for index in range(HEADS):
        scores = weights_ref[index] * INV_ROOT + bias
        powers = jnp.exp(scores - jnp.max(scores, axis=1, keepdims=True))
        weights_ref[index] = powers * (1.0 / jnp.sum(powers, axis=1, keepdims=True))
    for tile in range(TILES):
        rounded = [weights_ref[index].astype(BF16) for index in tile_heads(tile)]
        values = stacked_heads(rows_ref, 2 * WIDTH, tile)
        put(tile, dot(jnp.concatenate(rounded, axis=1), values, 1, 0).astype(BF16))


def ordered_channels(rows_ref):
    return dot(rows_ref[:, 3 * WIDTH : BASE], channel_order(), 1, 0).astype(BF16)


def forward_kernel(core_ref, sent_ref, share_ref, columns_ref, rows_ref, weights_ref, channels_ref):
    rows_ref[...] = sent_ref[...].reshape(ROWS, COLS)
    channels_ref[...] = ordered_channels(rows_ref)

    def put(tile, value):
        share_ref[:, lanes(tile)] = value

    attend(rows_ref, weights_ref, put)
    own = pl.multiple_of(core_ref[0] * HALF, HALF)
    other = pl.multiple_of((1 - core_ref[0]) * HALF, HALF)
    columns_ref[...] = channels_ref[:, pl.ds(own, HALF)]
    share_ref[:, WIDTH:] = channels_ref[:, pl.ds(other, HALF)]


def weight_grad_kernel(share_ref, received_ref, columns_ref, out_ref):
    columns = jnp.concatenate([columns_ref[...], received_ref[:, WIDTH:]], axis=0)
    features = jnp.concatenate([share_ref[:, :WIDTH], received_ref[:, :WIDTH]], axis=0)
    partial = dot(columns, features, 0, 0).astype(BF16)
    for high in range(2):
        for pair in range(3):
            start, column = pair * ROWS + high * 64, high * HALF_WIDTH + pair * WIDTH
            out_ref[:, :, column : column + WIDTH] = partial[start : start + 64].reshape(
                32, 2, WIDTH
            )


def backward_kernel(
    core_ref, x_ref, sent_ref, mine_ref, theirs_ref,
    out_ref, rows_ref, weights_ref, channels_ref, attended_ref, matrix_ref, upstream_ref,
    grad_scores_ref,
):
    rows_ref[...] = sent_ref[...].reshape(ROWS, COLS)
    channels_ref[...] = ordered_channels(rows_ref)

    def put_attended(tile, value):
        attended_ref[:, lanes(tile)] = value

    attend(rows_ref, weights_ref, put_attended)
    own = pl.multiple_of(core_ref[0] * HALF, HALF)
    other = pl.multiple_of((1 - core_ref[0]) * HALF, HALF)
    for step in range(4):
        first = ((x_ref[0] - step) & 3) * PIECE_TILES
        for place in range(PIECE_TILES):
            tile = first + place
            row = pl.multiple_of(lax.div(tile, TILES) * ROWS, ROWS)
            column = pl.multiple_of(lax.rem(tile, TILES) * LANES, LANES)

            @pl.when(tile < 3 * TILES)
            def _():
                for start, half_ref in ((own, mine_ref), (other, theirs_ref)):
                    matrix_ref[pl.ds(start + row, ROWS), pl.ds(column, LANES)] = half_ref[
                        step, :, lanes(place)
                    ]

    upstream_ref[...] = dot(channels_ref[...], matrix_ref[...], 1, 0).astype(BF16)
    products = [
        head_products(upstream_ref, 0, rows_ref, 2 * WIDTH, index) for index in range(HEADS)
    ]
    for index in range(HEADS):
        weights, grad_weights = weights_ref[index], products[index]
        centred = grad_weights - jnp.sum(weights * grad_weights, axis=1, keepdims=True)
        grad_scores_ref[index] = (weights * centred * INV_ROOT).astype(BF16)

    def put(start, value):
        out_ref[:, :, start : start + value.shape[1]] = value.astype(BF16).reshape(64, 2, -1)

    projected = dot(attended_ref[...], matrix_ref[...], 1, 1).astype(BF16)
    put(3 * WIDTH, dot(projected, channel_order(), 1, 1))
    for tile in range(TILES):
        heads = tile_heads(tile)
        grad_scores = [grad_scores_ref[index] for index in heads]
        rounded = [weights_ref[index].astype(BF16) for index in heads]
        across, down = jnp.concatenate(grad_scores, axis=1), jnp.concatenate(grad_scores, axis=0)
        put(tile * LANES, dot(across, stacked_heads(rows_ref, WIDTH, tile), 1, 0))
        put(WIDTH + tile * LANES, dot(down, stacked_heads(rows_ref, 0, tile), 0, 0))
        put(
            2 * WIDTH + tile * LANES,
            dot(jnp.concatenate(rounded, axis=0), stacked_heads(upstream_ref, 0, tile), 0, 0),
        )


def owned_kernel(high_ref, terms_ref, keep_ref, send_ref, total_ref):
    rows = terms_ref[...].reshape(64, 2 * HALF_WIDTH)
    target = lax.broadcasted_iota(jnp.int32, (8, 64), 0)
    source = lax.broadcasted_iota(jnp.int32, (8, 64), 1)
    chosen = jnp.where(target == (source & 1), 1.0, 0.0).astype(BF16)
    total_ref[...] = dot(chosen, rows, 1, 0)
    own = pl.multiple_of(high_ref[0] * HALF_WIDTH, LANES)
    other = pl.multiple_of((1 - high_ref[0]) * HALF_WIDTH, LANES)
    keep_ref[...] = total_ref[0:2, pl.ds(own, HALF_WIDTH)]
    send_ref[...] = total_ref[0:2, pl.ds(other, HALF_WIDTH)]


def group_kernel(*refs):
    *terms, out_ref = refs
    total = terms[0][...]
    for term in terms[1:]:
        total += term[...]
    out_ref[...] = total * GRAD_SCALE


def total_kernel(core_ref, mine_ref, theirs_ref, out_ref):
    for core in range(2):
        total = jnp.where(core_ref[0] == core, mine_ref[...], theirs_ref[...])
        for pair in range(3):
            start = 6 * core + 2 * pair
            out_ref[start : start + 2, :] = total[:, pair * WIDTH : (pair + 1) * WIDTH]


IN_VMEM = pl.BlockSpec(memory_space=pltpu.VMEM)
IN_SMEM = pl.BlockSpec(memory_space=pltpu.SMEM)
IN_HBM = pl.BlockSpec(memory_space=pltpu.HBM)


def call(kernel, name, operands, specs, outs, scratch=(), aliases=None, grant=12, micros=1):
    return pl.pallas_call(
        kernel,
        out_shape=[jax.ShapeDtypeStruct(shape, dtype) for shape, dtype in outs],
        in_specs=specs,
        out_specs=[IN_VMEM] * len(outs),
        scratch_shapes=list(scratch),
        input_output_aliases=aliases or {},
        compiler_params=pltpu.CompilerParams(vmem_limit_bytes=grant << 20),
        cost_estimate=pl.CostEstimate(
            flops=micros * 10**9, bytes_accessed=micros * 3 * 10**6, transcendentals=0
        ),
        name=name,
    )(*operands)


def exchange(value, axes):
    return lax.all_to_all(value, axes, 0, 0, tiled=True)


def swap(value):
    return lax.ppermute(value, "c", [(0, 1), (1, 0)])


def turn(value, axis, step):
    return lax.ppermute(value, axis, [(place, (place + step) % 4) for place in range(4)])


def cross(value, step):
    pairs = [
        (2 * low + high, 2 * ((low + step) % 4) + 1 - high) for low in range(4) for high in range(2)
    ]
    return lax.ppermute(value, ("yl", "yh"), pairs)


def on_device(query_key_value, out_weight, cotangent):
    core = lax.axis_index("c").astype(jnp.int32).reshape(1)
    x_place = lax.axis_index("x").astype(jnp.int32).reshape(1)
    y_high = lax.axis_index("yh").astype(jnp.int32).reshape(1)
    (packed,) = call(
        pack_kernel,
        "pack",
        (core, query_key_value.reshape(3, ROWS, WIDTH), cotangent.reshape(ROWS, OUT), out_weight),
        [IN_SMEM] + [IN_HBM] * 3,
        [((64, 2, COLS), BF16)],
        [
            pltpu.VMEM((3, ROWS, WIDTH), BF16),
            pltpu.VMEM((ROWS, OUT), BF16),
            pltpu.VMEM((12, WIDTH), BF16),
            pltpu.SemaphoreType.DMA((5,)),
        ],
        grant=56,
    )
    sent = exchange(packed, SEQ)
    share, columns = call(
        forward_kernel,
        "forward",
        (core, sent),
        [IN_SMEM, IN_VMEM],
        [((ROWS, WIDTH + HALF), BF16), ((ROWS, HALF), BF16)],
        [
            pltpu.VMEM((ROWS, COLS), BF16),
            pltpu.VMEM((HEADS, ROWS, ROWS), F32),
            pltpu.VMEM((ROWS, OUT), BF16),
        ],
        micros=3,
    )
    (partial,) = call(
        weight_grad_kernel,
        "weight_grad",
        (share, swap(share), columns),
        [IN_VMEM] * 3,
        [((32, 2, 2 * HALF_WIDTH), BF16)],
    )
    piece, partial = lax.optimization_barrier((sent[:, :, BASE:].reshape(ROWS, PIECE), partial))
    collected = exchange(partial, ("x", "z"))
    mine = jnp.stack([piece] + [turn(piece, "x", step) for step in range(1, 4)])
    (results,) = call(
        backward_kernel,
        "backward",
        (core, x_place, sent, mine, swap(mine)),
        [IN_SMEM] * 2 + [IN_VMEM] * 3,
        [((64, 2, BASE), BF16)],
        [
            pltpu.VMEM((ROWS, COLS), BF16),
            pltpu.VMEM((HEADS, ROWS, ROWS), F32),
            pltpu.VMEM((ROWS, OUT), BF16),
            pltpu.VMEM((ROWS, WIDTH), BF16),
            pltpu.VMEM((OUT, WIDTH), BF16),
            pltpu.VMEM((ROWS, WIDTH), BF16),
            pltpu.VMEM((HEADS, ROWS, ROWS), BF16),
        ],
        micros=4,
    )
    results, collected = lax.optimization_barrier((results, collected))
    back = exchange(results, SEQ)
    keep, send = call(
        owned_kernel,
        "owned",
        (y_high, collected),
        [IN_SMEM, IN_VMEM],
        [((2, HALF_WIDTH), F32)] * 2,
        [pltpu.VMEM((8, 2 * HALF_WIDTH), F32)],
    )
    turned = [turn(keep, "yl", step) for step in range(1, 4)]
    turned += [cross(send, step) for step in range(4)]
    (group,) = call(
        group_kernel, "group", (keep, *turned), [IN_VMEM] * 8, [((2, HALF_WIDTH), F32)]
    )
    (total,) = call(
        total_kernel,
        "total",
        (core, group, swap(group)),
        [IN_SMEM] + [IN_VMEM] * 2,
        [((12, WIDTH), F32)],
    )
    frames = back.reshape(ROWS, BASE)
    grads = jnp.stack([frames[:, part * WIDTH : (part + 1) * WIDTH] for part in range(3)])
    return (
        frames[:, 3 * WIDTH :].reshape(1, 1, ROWS, OUT),
        grads.reshape(3, 1, 1, ROWS, WIDTH),
        total,
    )


def solution(mesh):
    split = Mesh(mesh.devices.reshape(4, 2, 2, 4, 8), ("yl", "c", "yh", "x", "z"))
    in_specs = (P(None, GROUPS, SEQ, None, None), P(SEQ, None), P(GROUPS, SEQ, None, None))
    out_specs = (P(GROUPS, SEQ, None, None), P(None, GROUPS, SEQ, None, None), P(SEQ, None))
    return jax.shard_map(
        on_device, mesh=split, in_specs=in_specs, out_specs=out_specs, check_vma=False
    )
```

```python
import math

import jax
import jax.numpy as jnp
from jax import lax
from jax.experimental import pallas as pl
from jax.experimental.pallas import tpu as pltpu
from jax.sharding import Mesh
from jax.sharding import PartitionSpec as P

HEADS = 16
HEAD_DIM = 72
ROWS = 128
LANES = 128
WIDTH = 1152
TILES = WIDTH // LANES
OUT = 768
HALF = OUT // 2
BASE = 3 * WIDTH + OUT
PIECE = 896
PIECE_TILES = PIECE // LANES
COLS = BASE + PIECE
HALF_WIDTH = 3 * WIDTH
INV_ROOT = 1.0 / math.sqrt(HEAD_DIM)
GRAD_SCALE = 1.0 / math.sqrt(512 * ROWS)
BF16 = jnp.bfloat16
F32 = jnp.float32

SEQ = ("yh", "x", "z")
GROUPS = ("yl", "c")


def dot(lhs, rhs, lhs_dim, rhs_dim):
    return lax.dot_general(
        lhs, rhs, (((lhs_dim,), (rhs_dim,)), ((), ())), preferred_element_type=F32
    )


def lanes(tile, base=0):
    return slice(base + tile * LANES, base + (tile + 1) * LANES)


def only_head(index, start, value):
    feature = lax.broadcasted_iota(jnp.int32, value.shape, 1) + start
    inside = (feature >= index * HEAD_DIM) & (feature < (index + 1) * HEAD_DIM)
    return jnp.where(inside, value, jnp.zeros_like(value))


def head_lanes(index):
    first = index * HEAD_DIM // LANES
    last = ((index + 1) * HEAD_DIM - 1) // LANES + 1
    return first * LANES, last * LANES


def head_products(lhs_ref, lhs_base, rhs_ref, rhs_base, index):
    start, stop = head_lanes(index)
    rhs = only_head(index, start, rhs_ref[:, rhs_base + start : rhs_base + stop])
    return dot(lhs_ref[:, lhs_base + start : lhs_base + stop], rhs, 1, 1)


def tile_heads(tile):
    return [
        index
        for index in range(HEADS)
        if index * HEAD_DIM < (tile + 1) * LANES and (index + 1) * HEAD_DIM > tile * LANES
    ]


def stacked_heads(ref, base, tile):
    value = ref[:, lanes(tile, base)]
    return jnp.concatenate(
        [only_head(index, tile * LANES, value) for index in tile_heads(tile)], axis=0
    )


def channel_order():
    natural = lax.broadcasted_iota(jnp.int32, (OUT, OUT), 0)
    place = lax.broadcasted_iota(jnp.int32, (OUT, OUT), 1)
    source = 12 * ((place & 127) >> 1) + 2 * (place >> 7) + (place & 1)
    return jnp.where(natural == source, 1.0, 0.0).astype(BF16)


def half_tiles():
    return [
        (tile // PIECE_TILES, tile % PIECE_TILES, tile // TILES, tile % TILES)
        for tile in range(3 * TILES)
    ]


def pack_kernel(
    core_ref, parts_hbm, cotangent_hbm, weight_hbm, out_ref, parts, cotangent, weight, sems
):
    pairs = [(parts_hbm.at[part], parts.at[part]) for part in range(3)]
    pairs += [(cotangent_hbm, cotangent), (weight_hbm, weight)]
    copies = [
        pltpu.make_async_copy(source, target, sems.at[place])
        for place, (source, target) in enumerate(pairs)
    ]
    for copy in copies:
        copy.start()
    row = lax.broadcasted_iota(jnp.int32, (ROWS, 12), 0)
    col = lax.broadcasted_iota(jnp.int32, (ROWS, 12), 1)
    copies[4].wait()
    repeated = []
    for pair in range(3):
        chosen = col == 6 * core_ref[0] + 2 * pair + (row & 1)
        repeated.append(
            dot(jnp.where(chosen, 1.0, 0.0).astype(BF16), weight[...], 1, 0).astype(BF16)
        )
    column = (lax.broadcasted_iota(jnp.int32, (ROWS, LANES), 0) >> 4) & 3
    for place in range(PIECE_TILES):
        value = jnp.zeros((ROWS, LANES), BF16)
        for piece, at, pair, tile in half_tiles():
            if at == place:
                value = jnp.where(column == piece, repeated[pair][:, lanes(tile)], value)
        out_ref[:, :, lanes(place, BASE)] = value.reshape(64, 2, LANES)
    for part in range(3):
        copies[part].wait()
        out_ref[:, :, part * WIDTH : (part + 1) * WIDTH] = parts[part].reshape(64, 2, WIDTH)
    copies[3].wait()
    out_ref[:, :, 3 * WIDTH : BASE] = cotangent[...].reshape(64, 2, OUT)


def attend(rows_ref, weights_ref, put):
    row = lax.broadcasted_iota(jnp.int32, (ROWS, ROWS), 0)
    col = lax.broadcasted_iota(jnp.int32, (ROWS, ROWS), 1)
    bias = jnp.where(((row ^ col) & 1) == 0, 0.0, -1e30)
    for index in range(HEADS):
        weights_ref[index] = head_products(rows_ref, 0, rows_ref, WIDTH, index)
    for index in range(HEADS):
        scores = weights_ref[index] * INV_ROOT + bias
        powers = jnp.exp(scores - jnp.max(scores, axis=1, keepdims=True))
        weights_ref[index] = powers * (1.0 / jnp.sum(powers, axis=1, keepdims=True))
    for tile in range(TILES):
        rounded = [weights_ref[index].astype(BF16) for index in tile_heads(tile)]
        values = stacked_heads(rows_ref, 2 * WIDTH, tile)
        put(tile, dot(jnp.concatenate(rounded, axis=1), values, 1, 0).astype(BF16))


def ordered_channels(rows_ref):
    return dot(rows_ref[:, 3 * WIDTH : BASE], channel_order(), 1, 0).astype(BF16)


def forward_kernel(core_ref, sent_ref, share_ref, columns_ref, rows_ref, weights_ref, channels_ref):
    rows_ref[...] = sent_ref[...].reshape(ROWS, COLS)
    channels_ref[...] = ordered_channels(rows_ref)

    def put(tile, value):
        share_ref[:, lanes(tile)] = value

    attend(rows_ref, weights_ref, put)
    own = pl.multiple_of(core_ref[0] * HALF, HALF)
    other = pl.multiple_of((1 - core_ref[0]) * HALF, HALF)
    columns_ref[...] = channels_ref[:, pl.ds(own, HALF)]
    share_ref[:, WIDTH:] = channels_ref[:, pl.ds(other, HALF)]


def weight_grad_kernel(share_ref, received_ref, columns_ref, out_ref):
    columns = jnp.concatenate([columns_ref[...], received_ref[:, WIDTH:]], axis=0)
    features = jnp.concatenate([share_ref[:, :WIDTH], received_ref[:, :WIDTH]], axis=0)
    partial = dot(columns, features, 0, 0).astype(BF16)
    for pair in range(3):
        out_ref[:, :, pair * WIDTH : (pair + 1) * WIDTH] = partial[
            pair * ROWS : (pair + 1) * ROWS
        ].reshape(64, 2, WIDTH)


def backward_kernel(
    sent_ref, pieces_ref,
    out_ref, rows_ref, weights_ref, channels_ref, attended_ref, matrix_ref, upstream_ref,
    grad_scores_ref,
):
    rows_ref[...] = sent_ref[...].reshape(ROWS, COLS)
    channels_ref[...] = ordered_channels(rows_ref)

    def put_attended(tile, value):
        attended_ref[:, lanes(tile)] = value

    attend(rows_ref, weights_ref, put_attended)
    for core in range(2):
        for piece, place, pair, tile in half_tiles():
            start = core * HALF + pair * ROWS
            matrix_ref[start : start + ROWS, lanes(tile)] = pieces_ref[
                4 * core + piece, :, lanes(place)
            ]
    upstream_ref[...] = dot(channels_ref[...], matrix_ref[...], 1, 0).astype(BF16)
    products = [
        head_products(upstream_ref, 0, rows_ref, 2 * WIDTH, index) for index in range(HEADS)
    ]
    for index in range(HEADS):
        weights, grad_weights = weights_ref[index], products[index]
        centred = grad_weights - jnp.sum(weights * grad_weights, axis=1, keepdims=True)
        grad_scores_ref[index] = (weights * centred * INV_ROOT).astype(BF16)

    def put(start, value):
        out_ref[:, :, start : start + value.shape[1]] = value.astype(BF16).reshape(64, 2, -1)

    projected = dot(attended_ref[...], matrix_ref[...], 1, 1).astype(BF16)
    put(3 * WIDTH, dot(projected, channel_order(), 1, 1))
    for tile in range(TILES):
        heads = tile_heads(tile)
        grad_scores = [grad_scores_ref[index] for index in heads]
        rounded = [weights_ref[index].astype(BF16) for index in heads]
        across, down = jnp.concatenate(grad_scores, axis=1), jnp.concatenate(grad_scores, axis=0)
        put(tile * LANES, dot(across, stacked_heads(rows_ref, WIDTH, tile), 1, 0))
        put(WIDTH + tile * LANES, dot(down, stacked_heads(rows_ref, 0, tile), 0, 0))
        put(
            2 * WIDTH + tile * LANES,
            dot(jnp.concatenate(rounded, axis=0), stacked_heads(upstream_ref, 0, tile), 0, 0),
        )


def owned_kernel(terms_ref, out_ref):
    rows = terms_ref[...].reshape(ROWS, HALF_WIDTH)
    target = lax.broadcasted_iota(jnp.int32, (8, ROWS), 0)
    source = lax.broadcasted_iota(jnp.int32, (8, ROWS), 1)
    chosen = jnp.where(target == (source & 1), 1.0, 0.0).astype(BF16)
    out_ref[...] = dot(chosen, rows, 1, 0)[:2]


def group_kernel(*refs):
    *terms, out_ref = refs
    total = terms[0][...]
    for term in terms[1:]:
        total += term[...]
    out_ref[...] = total * GRAD_SCALE


def total_kernel(core_ref, mine_ref, theirs_ref, out_ref):
    for core in range(2):
        total = jnp.where(core_ref[0] == core, mine_ref[...], theirs_ref[...])
        for pair in range(3):
            start = 6 * core + 2 * pair
            out_ref[start : start + 2, :] = total[:, pair * WIDTH : (pair + 1) * WIDTH]


IN_VMEM = pl.BlockSpec(memory_space=pltpu.VMEM)
IN_SMEM = pl.BlockSpec(memory_space=pltpu.SMEM)
IN_HBM = pl.BlockSpec(memory_space=pltpu.HBM)


def call(kernel, name, operands, specs, outs, scratch=(), aliases=None, grant=12, micros=1):
    return pl.pallas_call(
        kernel,
        out_shape=[jax.ShapeDtypeStruct(shape, dtype) for shape, dtype in outs],
        in_specs=specs,
        out_specs=[IN_VMEM] * len(outs),
        scratch_shapes=list(scratch),
        input_output_aliases=aliases or {},
        compiler_params=pltpu.CompilerParams(vmem_limit_bytes=grant << 20),
        cost_estimate=pl.CostEstimate(
            flops=micros * 10**9, bytes_accessed=micros * 3 * 10**6, transcendentals=0
        ),
        name=name,
    )(*operands)


def exchange(value, axes):
    return lax.all_to_all(value, axes, 0, 0, tiled=True)


def swap(value):
    return lax.ppermute(value, "c", [(0, 1), (1, 0)])


def turn(value, axis, step):
    return lax.ppermute(value, axis, [(place, (place + step) % 4) for place in range(4)])


def on_device(query_key_value, out_weight, cotangent):
    core = lax.axis_index("c").astype(jnp.int32).reshape(1)
    (packed,) = call(
        pack_kernel,
        "pack",
        (core, query_key_value.reshape(3, ROWS, WIDTH), cotangent.reshape(ROWS, OUT), out_weight),
        [IN_SMEM] + [IN_HBM] * 3,
        [((64, 2, COLS), BF16)],
        [
            pltpu.VMEM((3, ROWS, WIDTH), BF16),
            pltpu.VMEM((ROWS, OUT), BF16),
            pltpu.VMEM((12, WIDTH), BF16),
            pltpu.SemaphoreType.DMA((5,)),
        ],
        grant=56,
    )
    sent = exchange(packed, SEQ)
    pieces = lax.all_gather(sent[:, :, BASE:].reshape(ROWS, PIECE), ("c", "x"))
    share, columns = call(
        forward_kernel,
        "forward",
        (core, sent),
        [IN_SMEM, IN_VMEM],
        [((ROWS, WIDTH + HALF), BF16), ((ROWS, HALF), BF16)],
        [
            pltpu.VMEM((ROWS, COLS), BF16),
            pltpu.VMEM((HEADS, ROWS, ROWS), F32),
            pltpu.VMEM((ROWS, OUT), BF16),
        ],
        micros=3,
    )
    (partial,) = call(
        weight_grad_kernel,
        "weight_grad",
        (share, swap(share), columns),
        [IN_VMEM] * 3,
        [((64, 2, HALF_WIDTH), BF16)],
    )
    collected = exchange(partial, SEQ)
    (results,) = call(
        backward_kernel,
        "backward",
        (sent, pieces),
        [IN_VMEM] * 2,
        [((64, 2, BASE), BF16)],
        [
            pltpu.VMEM((ROWS, COLS), BF16),
            pltpu.VMEM((HEADS, ROWS, ROWS), F32),
            pltpu.VMEM((ROWS, OUT), BF16),
            pltpu.VMEM((ROWS, WIDTH), BF16),
            pltpu.VMEM((OUT, WIDTH), BF16),
            pltpu.VMEM((ROWS, WIDTH), BF16),
            pltpu.VMEM((HEADS, ROWS, ROWS), BF16),
        ],
        micros=4,
    )
    results, collected = lax.optimization_barrier((results, collected))
    back = exchange(results, SEQ)
    (owned,) = call(owned_kernel, "owned", (collected,), [IN_VMEM], [((2, HALF_WIDTH), F32)])
    turned = [turn(owned, "yl", step) for step in range(1, 4)]
    (group,) = call(
        group_kernel, "group", (owned, *turned), [IN_VMEM] * 4, [((2, HALF_WIDTH), F32)]
    )
    (total,) = call(
        total_kernel,
        "total",
        (core, group, swap(group)),
        [IN_SMEM] + [IN_VMEM] * 2,
        [((12, WIDTH), F32)],
    )
    frames = back.reshape(ROWS, BASE)
    grads = jnp.stack([frames[:, part * WIDTH : (part + 1) * WIDTH] for part in range(3)])
    return (
        frames[:, 3 * WIDTH :].reshape(1, 1, ROWS, OUT),
        grads.reshape(3, 1, 1, ROWS, WIDTH),
        total,
    )


def solution(mesh):
    split = Mesh(mesh.devices.reshape(4, 2, 2, 4, 8), ("yl", "c", "yh", "x", "z"))
    in_specs = (P(None, GROUPS, SEQ, None, None), P(SEQ, None), P(GROUPS, SEQ, None, None))
    out_specs = (P(GROUPS, SEQ, None, None), P(None, GROUPS, SEQ, None, None), P(SEQ, None))
    return jax.shard_map(
        on_device, mesh=split, in_specs=in_specs, out_specs=out_specs, check_vma=False
    )
```

```python
import math

import jax
import jax.numpy as jnp
from jax import lax
from jax.experimental import pallas as pl
from jax.experimental.pallas import tpu as pltpu
from jax.sharding import Mesh
from jax.sharding import PartitionSpec as P

HEADS = 16
HEAD_DIM = 72
ROWS = 128
LANES = 128
WIDTH = 1152
TILES = WIDTH // LANES
OUT = 768
HALF = OUT // 2
BASE = 3 * WIDTH + OUT
PIECE = 896
PIECE_TILES = PIECE // LANES
COLS = BASE + PIECE
HALF_WIDTH = 3 * WIDTH
INV_ROOT = 1.0 / math.sqrt(HEAD_DIM)
GRAD_SCALE = 1.0 / math.sqrt(512 * ROWS)
BF16 = jnp.bfloat16
F32 = jnp.float32

SEQ = ("yh", "x", "z")
GROUPS = ("yl", "c")


def dot(lhs, rhs, lhs_dim, rhs_dim):
    return lax.dot_general(
        lhs, rhs, (((lhs_dim,), (rhs_dim,)), ((), ())), preferred_element_type=F32
    )


def lanes(tile, base=0):
    return slice(base + tile * LANES, base + (tile + 1) * LANES)


def only_head(index, start, value):
    feature = lax.broadcasted_iota(jnp.int32, value.shape, 1) + start
    inside = (feature >= index * HEAD_DIM) & (feature < (index + 1) * HEAD_DIM)
    return jnp.where(inside, value, jnp.zeros_like(value))


def head_lanes(index):
    first = index * HEAD_DIM // LANES
    last = ((index + 1) * HEAD_DIM - 1) // LANES + 1
    return first * LANES, last * LANES


def head_products(lhs_ref, lhs_base, rhs_ref, rhs_base, index):
    start, stop = head_lanes(index)
    rhs = only_head(index, start, rhs_ref[:, rhs_base + start : rhs_base + stop])
    return dot(lhs_ref[:, lhs_base + start : lhs_base + stop], rhs, 1, 1)


def tile_heads(tile):
    return [
        index
        for index in range(HEADS)
        if index * HEAD_DIM < (tile + 1) * LANES and (index + 1) * HEAD_DIM > tile * LANES
    ]


def stacked_heads(ref, base, tile):
    value = ref[:, lanes(tile, base)]
    return jnp.concatenate(
        [only_head(index, tile * LANES, value) for index in tile_heads(tile)], axis=0
    )


def channel_order():
    natural = lax.broadcasted_iota(jnp.int32, (OUT, OUT), 0)
    place = lax.broadcasted_iota(jnp.int32, (OUT, OUT), 1)
    source = 12 * ((place & 127) >> 1) + 2 * (place >> 7) + (place & 1)
    return jnp.where(natural == source, 1.0, 0.0).astype(BF16)


def half_tiles():
    return [
        (tile // PIECE_TILES, tile % PIECE_TILES, tile // TILES, tile % TILES)
        for tile in range(3 * TILES)
    ]


def pack_kernel(
    core_ref, parts_hbm, cotangent_hbm, weight_hbm, out_ref, parts, cotangent, weight, sems
):
    pairs = [(parts_hbm.at[part], parts.at[part]) for part in range(3)]
    pairs += [(cotangent_hbm, cotangent), (weight_hbm, weight)]
    copies = [
        pltpu.make_async_copy(source, target, sems.at[place])
        for place, (source, target) in enumerate(pairs)
    ]
    for copy in copies:
        copy.start()
    row = lax.broadcasted_iota(jnp.int32, (ROWS, 12), 0)
    col = lax.broadcasted_iota(jnp.int32, (ROWS, 12), 1)
    copies[4].wait()
    repeated = []
    for pair in range(3):
        chosen = col == 6 * core_ref[0] + 2 * pair + (row & 1)
        repeated.append(
            dot(jnp.where(chosen, 1.0, 0.0).astype(BF16), weight[...], 1, 0).astype(BF16)
        )
    column = (lax.broadcasted_iota(jnp.int32, (ROWS, LANES), 0) >> 4) & 3
    for place in range(PIECE_TILES):
        value = jnp.zeros((ROWS, LANES), BF16)
        for piece, at, pair, tile in half_tiles():
            if at == place:
                value = jnp.where(column == piece, repeated[pair][:, lanes(tile)], value)
        out_ref[:, :, lanes(place, BASE)] = value.reshape(64, 2, LANES)
    for part in range(3):
        copies[part].wait()
        out_ref[:, :, part * WIDTH : (part + 1) * WIDTH] = parts[part].reshape(64, 2, WIDTH)
    copies[3].wait()
    out_ref[:, :, 3 * WIDTH : BASE] = cotangent[...].reshape(64, 2, OUT)


def attend(rows_ref, weights_ref, put):
    row = lax.broadcasted_iota(jnp.int32, (ROWS, ROWS), 0)
    col = lax.broadcasted_iota(jnp.int32, (ROWS, ROWS), 1)
    bias = jnp.where(((row ^ col) & 1) == 0, 0.0, -1e30)
    for index in range(HEADS):
        weights_ref[index] = head_products(rows_ref, 0, rows_ref, WIDTH, index)
    for index in range(HEADS):
        scores = weights_ref[index] * INV_ROOT + bias
        powers = jnp.exp(scores - jnp.max(scores, axis=1, keepdims=True))
        weights_ref[index] = powers * (1.0 / jnp.sum(powers, axis=1, keepdims=True))
    for tile in range(TILES):
        rounded = [weights_ref[index].astype(BF16) for index in tile_heads(tile)]
        values = stacked_heads(rows_ref, 2 * WIDTH, tile)
        put(tile, dot(jnp.concatenate(rounded, axis=1), values, 1, 0).astype(BF16))


def ordered_channels(rows_ref):
    return dot(rows_ref[:, 3 * WIDTH : BASE], channel_order(), 1, 0).astype(BF16)


def forward_kernel(core_ref, sent_ref, share_ref, columns_ref, rows_ref, weights_ref, channels_ref):
    rows_ref[...] = sent_ref[...].reshape(ROWS, COLS)
    channels_ref[...] = ordered_channels(rows_ref)

    def put(tile, value):
        share_ref[:, lanes(tile)] = value

    attend(rows_ref, weights_ref, put)
    own = pl.multiple_of(core_ref[0] * HALF, HALF)
    other = pl.multiple_of((1 - core_ref[0]) * HALF, HALF)
    columns_ref[...] = channels_ref[:, pl.ds(own, HALF)]
    share_ref[:, WIDTH:] = channels_ref[:, pl.ds(other, HALF)]


def weight_grad_kernel(share_ref, received_ref, columns_ref, out_ref):
    columns = jnp.concatenate([columns_ref[...], received_ref[:, WIDTH:]], axis=0)
    features = jnp.concatenate([share_ref[:, :WIDTH], received_ref[:, :WIDTH]], axis=0)
    partial = dot(columns, features, 0, 0).astype(BF16)
    for target in range(4):
        for high in range(2):
            for pair in range(3):
                start = pair * ROWS + high * 64 + target * 16
                out_ref[
                    target, high * 16 : high * 16 + 16, pair * WIDTH : (pair + 1) * WIDTH
                ] = partial[start : start + 16]


def backward_kernel(
    core_ref, x_ref, sent_ref, mine_ref, theirs_ref,
    out_ref, rows_ref, weights_ref, channels_ref, attended_ref, matrix_ref, upstream_ref,
    grad_scores_ref,
):
    rows_ref[...] = sent_ref[...].reshape(ROWS, COLS)
    channels_ref[...] = ordered_channels(rows_ref)

    def put_attended(tile, value):
        attended_ref[:, lanes(tile)] = value

    attend(rows_ref, weights_ref, put_attended)
    own = pl.multiple_of(core_ref[0] * HALF, HALF)
    other = pl.multiple_of((1 - core_ref[0]) * HALF, HALF)
    for here in range(4):

        @pl.when(x_ref[0] == here)
        def _():
            for piece, place, pair, tile in half_tiles():
                for start, half_ref in ((own, mine_ref), (other, theirs_ref)):
                    matrix_ref[pl.ds(start + pair * ROWS, ROWS), lanes(tile)] = half_ref[
                        (here - piece) & 3, :, lanes(place)
                    ]

    upstream_ref[...] = dot(channels_ref[...], matrix_ref[...], 1, 0).astype(BF16)
    products = [
        head_products(upstream_ref, 0, rows_ref, 2 * WIDTH, index) for index in range(HEADS)
    ]
    for index in range(HEADS):
        weights, grad_weights = weights_ref[index], products[index]
        centred = grad_weights - jnp.sum(weights * grad_weights, axis=1, keepdims=True)
        grad_scores_ref[index] = (weights * centred * INV_ROOT).astype(BF16)

    def put(start, value):
        out_ref[:, :, start : start + value.shape[1]] = value.astype(BF16).reshape(64, 2, -1)

    projected = dot(attended_ref[...], matrix_ref[...], 1, 1).astype(BF16)
    put(3 * WIDTH, dot(projected, channel_order(), 1, 1))
    for tile in range(TILES):
        heads = tile_heads(tile)
        grad_scores = [grad_scores_ref[index] for index in heads]
        rounded = [weights_ref[index].astype(BF16) for index in heads]
        across, down = jnp.concatenate(grad_scores, axis=1), jnp.concatenate(grad_scores, axis=0)
        put(tile * LANES, dot(across, stacked_heads(rows_ref, WIDTH, tile), 1, 0))
        put(WIDTH + tile * LANES, dot(down, stacked_heads(rows_ref, 0, tile), 0, 0))
        put(
            2 * WIDTH + tile * LANES,
            dot(jnp.concatenate(rounded, axis=0), stacked_heads(upstream_ref, 0, tile), 0, 0),
        )


def merge_kernel(terms_ref, out_ref):
    total = terms_ref[0].astype(F32)
    for place in range(1, 4):
        total += terms_ref[place].astype(F32)
    out_ref[...] = total.astype(BF16).reshape(16, 2, HALF_WIDTH)


def owned_kernel(terms_ref, out_ref):
    rows = terms_ref[...].reshape(32, HALF_WIDTH)
    target = lax.broadcasted_iota(jnp.int32, (8, 32), 0)
    source = lax.broadcasted_iota(jnp.int32, (8, 32), 1)
    chosen = jnp.where(target == (source & 1), 1.0, 0.0).astype(BF16)
    out_ref[...] = dot(chosen, rows, 1, 0)[:2]


def group_kernel(*refs):
    *terms, out_ref = refs
    total = terms[0][...]
    for term in terms[1:]:
        total += term[...]
    out_ref[...] = total * GRAD_SCALE


def total_kernel(core_ref, mine_ref, theirs_ref, out_ref):
    for core in range(2):
        total = jnp.where(core_ref[0] == core, mine_ref[...], theirs_ref[...])
        for pair in range(3):
            start = 6 * core + 2 * pair
            out_ref[start : start + 2, :] = total[:, pair * WIDTH : (pair + 1) * WIDTH]


IN_VMEM = pl.BlockSpec(memory_space=pltpu.VMEM)
IN_SMEM = pl.BlockSpec(memory_space=pltpu.SMEM)
IN_HBM = pl.BlockSpec(memory_space=pltpu.HBM)


def call(kernel, name, operands, specs, outs, scratch=(), aliases=None, grant=12, micros=1):
    return pl.pallas_call(
        kernel,
        out_shape=[jax.ShapeDtypeStruct(shape, dtype) for shape, dtype in outs],
        in_specs=specs,
        out_specs=[IN_VMEM] * len(outs),
        scratch_shapes=list(scratch),
        input_output_aliases=aliases or {},
        compiler_params=pltpu.CompilerParams(vmem_limit_bytes=grant << 20),
        cost_estimate=pl.CostEstimate(
            flops=micros * 10**9, bytes_accessed=micros * 3 * 10**6, transcendentals=0
        ),
        name=name,
    )(*operands)


def exchange(value, axes):
    return lax.all_to_all(value, axes, 0, 0, tiled=True)


def swap(value):
    return lax.ppermute(value, "c", [(0, 1), (1, 0)])


def turn(value, axis, step):
    return lax.ppermute(value, axis, [(place, (place + step) % 4) for place in range(4)])


def on_device(query_key_value, out_weight, cotangent):
    core = lax.axis_index("c").astype(jnp.int32).reshape(1)
    x_place = lax.axis_index("x").astype(jnp.int32).reshape(1)
    (packed,) = call(
        pack_kernel,
        "pack",
        (core, query_key_value.reshape(3, ROWS, WIDTH), cotangent.reshape(ROWS, OUT), out_weight),
        [IN_SMEM] + [IN_HBM] * 3,
        [((64, 2, COLS), BF16)],
        [
            pltpu.VMEM((3, ROWS, WIDTH), BF16),
            pltpu.VMEM((ROWS, OUT), BF16),
            pltpu.VMEM((12, WIDTH), BF16),
            pltpu.SemaphoreType.DMA((5,)),
        ],
        grant=56,
    )
    sent = exchange(packed, SEQ)
    share, columns = call(
        forward_kernel,
        "forward",
        (core, sent),
        [IN_SMEM, IN_VMEM],
        [((ROWS, WIDTH + HALF), BF16), ((ROWS, HALF), BF16)],
        [
            pltpu.VMEM((ROWS, COLS), BF16),
            pltpu.VMEM((HEADS, ROWS, ROWS), F32),
            pltpu.VMEM((ROWS, OUT), BF16),
        ],
        micros=3,
    )
    (partial,) = call(
        weight_grad_kernel,
        "weight_grad",
        (share, swap(share), columns),
        [IN_VMEM] * 3,
        [((4, 32, HALF_WIDTH), BF16)],
    )
    piece, partial = lax.optimization_barrier((sent[:, :, BASE:].reshape(ROWS, PIECE), partial))
    terms = exchange(partial, "x")
    turned = [turn(piece, "x", step) for step in range(1, 4)]
    (summed,) = call(
        merge_kernel, "merge", (terms,), [IN_VMEM], [((16, 2, HALF_WIDTH), BF16)]
    )
    collected = exchange(summed, ("yh", "z"))
    piece, *turned = lax.optimization_barrier((piece, *turned, summed))[:4]
    mine = jnp.stack([piece, *turned])
    (results,) = call(
        backward_kernel,
        "backward",
        (core, x_place, sent, mine, swap(mine)),
        [IN_SMEM] * 2 + [IN_VMEM] * 3,
        [((64, 2, BASE), BF16)],
        [
            pltpu.VMEM((ROWS, COLS), BF16),
            pltpu.VMEM((HEADS, ROWS, ROWS), F32),
            pltpu.VMEM((ROWS, OUT), BF16),
            pltpu.VMEM((ROWS, WIDTH), BF16),
            pltpu.VMEM((OUT, WIDTH), BF16),
            pltpu.VMEM((ROWS, WIDTH), BF16),
            pltpu.VMEM((HEADS, ROWS, ROWS), BF16),
        ],
        micros=4,
    )
    results, collected = lax.optimization_barrier((results, collected))
    (owned,) = call(owned_kernel, "owned", (collected,), [IN_VMEM], [((2, HALF_WIDTH), F32)])
    turned = [turn(owned, "yl", step) for step in range(1, 4)]
    back = exchange(results, SEQ)
    (group,) = call(
        group_kernel, "group", (owned, *turned), [IN_VMEM] * 4, [((2, HALF_WIDTH), F32)]
    )
    (total,) = call(
        total_kernel,
        "total",
        (core, group, swap(group)),
        [IN_SMEM] + [IN_VMEM] * 2,
        [((12, WIDTH), F32)],
    )
    frames = back.reshape(ROWS, BASE)
    grads = jnp.stack([frames[:, part * WIDTH : (part + 1) * WIDTH] for part in range(3)])
    return (
        frames[:, 3 * WIDTH :].reshape(1, 1, ROWS, OUT),
        grads.reshape(3, 1, 1, ROWS, WIDTH),
        total,
    )


def solution(mesh):
    split = Mesh(mesh.devices.reshape(4, 2, 2, 4, 8), ("yl", "c", "yh", "x", "z"))
    in_specs = (P(None, GROUPS, SEQ, None, None), P(SEQ, None), P(GROUPS, SEQ, None, None))
    out_specs = (P(GROUPS, SEQ, None, None), P(None, GROUPS, SEQ, None, None), P(SEQ, None))
    return jax.shard_map(
        on_device, mesh=split, in_specs=in_specs, out_specs=out_specs, check_vma=False
    )
```

```python
import math

import jax
import jax.numpy as jnp
from jax import lax
from jax.experimental import pallas as pl
from jax.experimental.pallas import tpu as pltpu
from jax.sharding import Mesh
from jax.sharding import PartitionSpec as P

HEADS = 16
HEAD_DIM = 72
ROWS = 128
LANES = 128
WIDTH = 1152
TILES = WIDTH // LANES
OUT = 768
HALF = OUT // 2
BASE = 3 * WIDTH + OUT
PIECE = 896
PIECE_TILES = PIECE // LANES
COLS = BASE + PIECE
HALF_WIDTH = 3 * WIDTH
INV_ROOT = 1.0 / math.sqrt(HEAD_DIM)
GRAD_SCALE = 1.0 / math.sqrt(512 * ROWS)
BF16 = jnp.bfloat16
F32 = jnp.float32

SEQ = ("yh", "x", "z")
GROUPS = ("yl", "c")


def dot(lhs, rhs, lhs_dim, rhs_dim):
    return lax.dot_general(
        lhs, rhs, (((lhs_dim,), (rhs_dim,)), ((), ())), preferred_element_type=F32
    )


def lanes(tile, base=0):
    return slice(base + tile * LANES, base + (tile + 1) * LANES)


def only_head(index, start, value):
    feature = lax.broadcasted_iota(jnp.int32, value.shape, 1) + start
    inside = (feature >= index * HEAD_DIM) & (feature < (index + 1) * HEAD_DIM)
    return jnp.where(inside, value, jnp.zeros_like(value))


def head_lanes(index):
    first = index * HEAD_DIM // LANES
    last = ((index + 1) * HEAD_DIM - 1) // LANES + 1
    return first * LANES, last * LANES


def head_products(lhs_ref, lhs_base, rhs_ref, rhs_base, index):
    start, stop = head_lanes(index)
    rhs = only_head(index, start, rhs_ref[:, rhs_base + start : rhs_base + stop])
    return dot(lhs_ref[:, lhs_base + start : lhs_base + stop], rhs, 1, 1)


def tile_heads(tile):
    return [
        index
        for index in range(HEADS)
        if index * HEAD_DIM < (tile + 1) * LANES and (index + 1) * HEAD_DIM > tile * LANES
    ]


def stacked_heads(ref, base, tile):
    value = ref[:, lanes(tile, base)]
    return jnp.concatenate(
        [only_head(index, tile * LANES, value) for index in tile_heads(tile)], axis=0
    )


def channel_order():
    natural = lax.broadcasted_iota(jnp.int32, (OUT, OUT), 0)
    place = lax.broadcasted_iota(jnp.int32, (OUT, OUT), 1)
    source = 12 * ((place & 127) >> 1) + 2 * (place >> 7) + (place & 1)
    return jnp.where(natural == source, 1.0, 0.0).astype(BF16)


def half_tiles():
    return [
        (tile // PIECE_TILES, tile % PIECE_TILES, tile // TILES, tile % TILES)
        for tile in range(3 * TILES)
    ]


def pack_kernel(
    core_ref, parts_hbm, cotangent_hbm, weight_hbm, out_ref, parts, cotangent, weight, sems
):
    pairs = [(parts_hbm.at[part], parts.at[part]) for part in range(3)]
    pairs += [(cotangent_hbm, cotangent), (weight_hbm, weight)]
    copies = [
        pltpu.make_async_copy(source, target, sems.at[place])
        for place, (source, target) in enumerate(pairs)
    ]
    for copy in copies:
        copy.start()
    row = lax.broadcasted_iota(jnp.int32, (ROWS, 12), 0)
    col = lax.broadcasted_iota(jnp.int32, (ROWS, 12), 1)
    copies[4].wait()
    repeated = []
    for pair in range(3):
        chosen = col == 6 * core_ref[0] + 2 * pair + (row & 1)
        repeated.append(
            dot(jnp.where(chosen, 1.0, 0.0).astype(BF16), weight[...], 1, 0).astype(BF16)
        )
    column = (lax.broadcasted_iota(jnp.int32, (ROWS, LANES), 0) >> 4) & 3
    for place in range(PIECE_TILES):
        value = jnp.zeros((ROWS, LANES), BF16)
        for piece, at, pair, tile in half_tiles():
            if at == place:
                value = jnp.where(column == piece, repeated[pair][:, lanes(tile)], value)
        out_ref[:, :, lanes(place, BASE)] = value.reshape(64, 2, LANES)
    for part in range(3):
        copies[part].wait()
        out_ref[:, :, part * WIDTH : (part + 1) * WIDTH] = parts[part].reshape(64, 2, WIDTH)
    copies[3].wait()
    out_ref[:, :, 3 * WIDTH : BASE] = cotangent[...].reshape(64, 2, OUT)


def attend(rows_ref, weights_ref, put):
    row = lax.broadcasted_iota(jnp.int32, (ROWS, ROWS), 0)
    col = lax.broadcasted_iota(jnp.int32, (ROWS, ROWS), 1)
    bias = jnp.where(((row ^ col) & 1) == 0, 0.0, -1e30)
    for index in range(HEADS):
        weights_ref[index] = head_products(rows_ref, 0, rows_ref, WIDTH, index)
    for index in range(HEADS):
        scores = weights_ref[index] * INV_ROOT + bias
        powers = jnp.exp(scores - jnp.max(scores, axis=1, keepdims=True))
        weights_ref[index] = powers * (1.0 / jnp.sum(powers, axis=1, keepdims=True))
    for tile in range(TILES):
        rounded = [weights_ref[index].astype(BF16) for index in tile_heads(tile)]
        values = stacked_heads(rows_ref, 2 * WIDTH, tile)
        put(tile, dot(jnp.concatenate(rounded, axis=1), values, 1, 0).astype(BF16))


def ordered_channels(rows_ref):
    return dot(rows_ref[:, 3 * WIDTH : BASE], channel_order(), 1, 0).astype(BF16)


def forward_kernel(core_ref, sent_ref, share_ref, columns_ref, rows_ref, weights_ref, channels_ref):
    rows_ref[...] = sent_ref[...].reshape(ROWS, COLS)
    channels_ref[...] = ordered_channels(rows_ref)

    def put(tile, value):
        share_ref[:, lanes(tile)] = value

    attend(rows_ref, weights_ref, put)
    own = pl.multiple_of(core_ref[0] * HALF, HALF)
    other = pl.multiple_of((1 - core_ref[0]) * HALF, HALF)
    columns_ref[...] = channels_ref[:, pl.ds(own, HALF)]
    share_ref[:, WIDTH:] = channels_ref[:, pl.ds(other, HALF)]


def weight_grad_kernel(share_ref, received_ref, columns_ref, out_ref):
    columns = jnp.concatenate([columns_ref[...], received_ref[:, WIDTH:]], axis=0)
    features = jnp.concatenate([share_ref[:, :WIDTH], received_ref[:, :WIDTH]], axis=0)
    partial = dot(columns, features, 0, 0).astype(BF16)
    for target in range(4):
        for high in range(2):
            for pair in range(3):
                start = pair * ROWS + high * 64 + target * 16
                out_ref[
                    target, high * 16 : high * 16 + 16, pair * WIDTH : (pair + 1) * WIDTH
                ] = partial[start : start + 16]


def backward_kernel(
    core_ref, sent_ref, mine_ref, theirs_ref,
    out_ref, rows_ref, weights_ref, channels_ref, attended_ref, matrix_ref, upstream_ref,
    grad_scores_ref,
):
    rows_ref[...] = sent_ref[...].reshape(ROWS, COLS)
    channels_ref[...] = ordered_channels(rows_ref)

    def put_attended(tile, value):
        attended_ref[:, lanes(tile)] = value

    attend(rows_ref, weights_ref, put_attended)
    own = pl.multiple_of(core_ref[0] * HALF, HALF)
    other = pl.multiple_of((1 - core_ref[0]) * HALF, HALF)
    for piece, place, pair, tile in half_tiles():
        for start, half_ref in ((own, mine_ref), (other, theirs_ref)):
            matrix_ref[pl.ds(start + pair * ROWS, ROWS), lanes(tile)] = half_ref[
                piece, :, lanes(place)
            ]
    upstream_ref[...] = dot(channels_ref[...], matrix_ref[...], 1, 0).astype(BF16)
    products = [
        head_products(upstream_ref, 0, rows_ref, 2 * WIDTH, index) for index in range(HEADS)
    ]
    for index in range(HEADS):
        weights, grad_weights = weights_ref[index], products[index]
        centred = grad_weights - jnp.sum(weights * grad_weights, axis=1, keepdims=True)
        grad_scores_ref[index] = (weights * centred * INV_ROOT).astype(BF16)

    def put(start, value):
        out_ref[:, :, start : start + value.shape[1]] = value.astype(BF16).reshape(64, 2, -1)

    projected = dot(attended_ref[...], matrix_ref[...], 1, 1).astype(BF16)
    put(3 * WIDTH, dot(projected, channel_order(), 1, 1))
    for tile in range(TILES):
        heads = tile_heads(tile)
        grad_scores = [grad_scores_ref[index] for index in heads]
        rounded = [weights_ref[index].astype(BF16) for index in heads]
        across, down = jnp.concatenate(grad_scores, axis=1), jnp.concatenate(grad_scores, axis=0)
        put(tile * LANES, dot(across, stacked_heads(rows_ref, WIDTH, tile), 1, 0))
        put(WIDTH + tile * LANES, dot(down, stacked_heads(rows_ref, 0, tile), 0, 0))
        put(
            2 * WIDTH + tile * LANES,
            dot(jnp.concatenate(rounded, axis=0), stacked_heads(upstream_ref, 0, tile), 0, 0),
        )


def merge_kernel(terms_ref, out_ref):
    total = terms_ref[0].astype(F32)
    for place in range(1, 4):
        total += terms_ref[place].astype(F32)
    out_ref[...] = total.astype(BF16).reshape(16, 2, HALF_WIDTH)


def owned_kernel(terms_ref, out_ref):
    rows = terms_ref[...].reshape(32, HALF_WIDTH)
    target = lax.broadcasted_iota(jnp.int32, (8, 32), 0)
    source = lax.broadcasted_iota(jnp.int32, (8, 32), 1)
    chosen = jnp.where(target == (source & 1), 1.0, 0.0).astype(BF16)
    out_ref[...] = dot(chosen, rows, 1, 0)[:2]


def unpack_kernel(back_ref, projected_hbm, grads_hbm, rows_ref, sems):
    rows_ref[...] = back_ref[...].reshape(ROWS, BASE)
    parts = [(rows_ref.at[:, 3 * WIDTH :], projected_hbm)]
    for part in range(3):
        parts.append((rows_ref.at[:, part * WIDTH : (part + 1) * WIDTH], grads_hbm.at[part]))
    copies = [
        pltpu.make_async_copy(source, target, sems.at[place])
        for place, (source, target) in enumerate(parts)
    ]
    for copy in copies:
        copy.start()
    for copy in copies:
        copy.wait()


def group_kernel(*refs):
    *terms, out_ref = refs
    total = terms[0][...]
    for term in terms[1:]:
        total += term[...]
    out_ref[...] = total * GRAD_SCALE


def total_kernel(core_ref, mine_ref, theirs_ref, out_ref):
    for core in range(2):
        total = jnp.where(core_ref[0] == core, mine_ref[...], theirs_ref[...])
        for pair in range(3):
            start = 6 * core + 2 * pair
            out_ref[start : start + 2, :] = total[:, pair * WIDTH : (pair + 1) * WIDTH]


IN_VMEM = pl.BlockSpec(memory_space=pltpu.VMEM)
IN_SMEM = pl.BlockSpec(memory_space=pltpu.SMEM)
IN_HBM = pl.BlockSpec(memory_space=pltpu.HBM)


def call(kernel, name, operands, specs, outs, scratch=(), grant=12, micros=1, out_spec=IN_VMEM):
    return pl.pallas_call(
        kernel,
        out_shape=[jax.ShapeDtypeStruct(shape, dtype) for shape, dtype in outs],
        in_specs=specs,
        out_specs=[out_spec] * len(outs),
        scratch_shapes=list(scratch),
        compiler_params=pltpu.CompilerParams(vmem_limit_bytes=grant << 20),
        cost_estimate=pl.CostEstimate(
            flops=micros * 10**9, bytes_accessed=micros * 3 * 10**6, transcendentals=0
        ),
        name=name,
    )(*operands)


def exchange(value, axes):
    return lax.all_to_all(value, axes, 0, 0, tiled=True)


def swap(value):
    return lax.ppermute(value, "c", [(0, 1), (1, 0)])


def turn(value, axis, step):
    return lax.ppermute(value, axis, [(place, (place + step) % 4) for place in range(4)])


def on_device(query_key_value, out_weight, cotangent):
    core = lax.axis_index("c").astype(jnp.int32).reshape(1)
    (packed,) = call(
        pack_kernel,
        "pack",
        (core, query_key_value.reshape(3, ROWS, WIDTH), cotangent.reshape(ROWS, OUT), out_weight),
        [IN_SMEM] + [IN_HBM] * 3,
        [((64, 2, COLS), BF16)],
        [
            pltpu.VMEM((3, ROWS, WIDTH), BF16),
            pltpu.VMEM((ROWS, OUT), BF16),
            pltpu.VMEM((12, WIDTH), BF16),
            pltpu.SemaphoreType.DMA((5,)),
        ],
        grant=56,
    )
    sent = exchange(packed, SEQ)
    piece = sent[:, :, BASE:].reshape(1, ROWS, PIECE)
    mine = exchange(jnp.broadcast_to(piece, (4, ROWS, PIECE)), "x")
    share, columns = call(
        forward_kernel,
        "forward",
        (core, sent),
        [IN_SMEM, IN_VMEM],
        [((ROWS, WIDTH + HALF), BF16), ((ROWS, HALF), BF16)],
        [
            pltpu.VMEM((ROWS, COLS), BF16),
            pltpu.VMEM((HEADS, ROWS, ROWS), F32),
            pltpu.VMEM((ROWS, OUT), BF16),
        ],
        micros=3,
    )
    (partial,) = call(
        weight_grad_kernel,
        "weight_grad",
        (share, swap(share), columns),
        [IN_VMEM] * 3,
        [((4, 32, HALF_WIDTH), BF16)],
    )
    mine, partial = lax.optimization_barrier((mine, partial))
    terms = exchange(partial, "x")
    (results,) = call(
        backward_kernel,
        "backward",
        (core, sent, mine, swap(mine)),
        [IN_SMEM] + [IN_VMEM] * 3,
        [((64, 2, BASE), BF16)],
        [
            pltpu.VMEM((ROWS, COLS), BF16),
            pltpu.VMEM((HEADS, ROWS, ROWS), F32),
            pltpu.VMEM((ROWS, OUT), BF16),
            pltpu.VMEM((ROWS, WIDTH), BF16),
            pltpu.VMEM((OUT, WIDTH), BF16),
            pltpu.VMEM((ROWS, WIDTH), BF16),
            pltpu.VMEM((HEADS, ROWS, ROWS), BF16),
        ],
        micros=4,
    )
    results, terms = lax.optimization_barrier((results, terms))
    (summed,) = call(
        merge_kernel, "merge", (terms,), [IN_VMEM], [((16, 2, HALF_WIDTH), BF16)]
    )
    collected = exchange(summed, ("yh", "z"))
    results, collected = lax.optimization_barrier((results, collected))
    (owned,) = call(owned_kernel, "owned", (collected,), [IN_VMEM], [((2, HALF_WIDTH), F32)])
    turned = [turn(owned, "yl", step) for step in range(1, 4)]
    back = exchange(results, SEQ)
    (group,) = call(
        group_kernel, "group", (owned, *turned), [IN_VMEM] * 4, [((2, HALF_WIDTH), F32)]
    )
    (total,) = call(
        total_kernel,
        "total",
        (core, group, swap(group)),
        [IN_SMEM] + [IN_VMEM] * 2,
        [((12, WIDTH), F32)],
    )
    projected, grads = call(
        unpack_kernel,
        "unpack",
        (back,),
        [IN_VMEM],
        [((ROWS, OUT), BF16), ((3, ROWS, WIDTH), BF16)],
        [pltpu.VMEM((ROWS, BASE), BF16), pltpu.SemaphoreType.DMA((4,))],
        out_spec=IN_HBM,
    )
    return (
        projected.reshape(1, 1, ROWS, OUT),
        grads.reshape(3, 1, 1, ROWS, WIDTH),
        total,
    )


def solution(mesh):
    split = Mesh(mesh.devices.reshape(4, 2, 2, 4, 8), ("yl", "c", "yh", "x", "z"))
    in_specs = (P(None, GROUPS, SEQ, None, None), P(SEQ, None), P(GROUPS, SEQ, None, None))
    out_specs = (P(GROUPS, SEQ, None, None), P(None, GROUPS, SEQ, None, None), P(SEQ, None))
    return jax.shard_map(
        on_device, mesh=split, in_specs=in_specs, out_specs=out_specs, check_vma=False
    )
```

```python
import math

import jax
import jax.numpy as jnp
from jax import lax
from jax.experimental import pallas as pl
from jax.experimental.pallas import tpu as pltpu
from jax.sharding import Mesh
from jax.sharding import PartitionSpec as P

HEADS = 16
HEAD_DIM = 72
ROWS = 128
LANES = 128
WIDTH = 1152
TILES = WIDTH // LANES
OUT = 768
HALF = OUT // 2
BASE = 3 * WIDTH + OUT
PIECE = 896
PIECE_TILES = PIECE // LANES
COLS = BASE + PIECE
HALF_WIDTH = 3 * WIDTH
SHARE = WIDTH + HALF + PIECE
INV_ROOT = 1.0 / math.sqrt(HEAD_DIM)
GRAD_SCALE = 1.0 / math.sqrt(512 * ROWS)
BF16 = jnp.bfloat16
F32 = jnp.float32

SEQ = ("yh", "x", "z")
GROUPS = ("yl", "c")


def dot(lhs, rhs, lhs_dim, rhs_dim):
    return lax.dot_general(
        lhs, rhs, (((lhs_dim,), (rhs_dim,)), ((), ())), preferred_element_type=F32
    )


def lanes(tile, base=0):
    return slice(base + tile * LANES, base + (tile + 1) * LANES)


def only_head(index, start, value):
    feature = lax.broadcasted_iota(jnp.int32, value.shape, 1) + start
    inside = (feature >= index * HEAD_DIM) & (feature < (index + 1) * HEAD_DIM)
    return jnp.where(inside, value, jnp.zeros_like(value))


def head_lanes(index):
    first = index * HEAD_DIM // LANES
    last = ((index + 1) * HEAD_DIM - 1) // LANES + 1
    return first * LANES, last * LANES


def head_products(lhs_ref, lhs_base, rhs_ref, rhs_base, index):
    start, stop = head_lanes(index)
    rhs = only_head(index, start, rhs_ref[:, rhs_base + start : rhs_base + stop])
    return dot(lhs_ref[:, lhs_base + start : lhs_base + stop], rhs, 1, 1)


def tile_heads(tile):
    return [
        index
        for index in range(HEADS)
        if index * HEAD_DIM < (tile + 1) * LANES and (index + 1) * HEAD_DIM > tile * LANES
    ]


def stacked_heads(ref, base, tile):
    value = ref[:, lanes(tile, base)]
    return jnp.concatenate(
        [only_head(index, tile * LANES, value) for index in tile_heads(tile)], axis=0
    )


def channel_order():
    natural = lax.broadcasted_iota(jnp.int32, (OUT, OUT), 0)
    place = lax.broadcasted_iota(jnp.int32, (OUT, OUT), 1)
    source = 12 * ((place & 127) >> 1) + 2 * (place >> 7) + (place & 1)
    return jnp.where(natural == source, 1.0, 0.0).astype(BF16)


def half_tiles():
    return [
        (tile // PIECE_TILES, tile % PIECE_TILES, tile // TILES, tile % TILES)
        for tile in range(3 * TILES)
    ]


def pack_kernel(
    core_ref, parts_hbm, cotangent_hbm, weight_hbm, out_ref, parts, cotangent, weight, sems
):
    pairs = [(parts_hbm.at[part], parts.at[part]) for part in range(3)]
    pairs += [(cotangent_hbm, cotangent), (weight_hbm, weight)]
    copies = [
        pltpu.make_async_copy(source, target, sems.at[place])
        for place, (source, target) in enumerate(pairs)
    ]
    for copy in copies:
        copy.start()
    row = lax.broadcasted_iota(jnp.int32, (ROWS, 12), 0)
    col = lax.broadcasted_iota(jnp.int32, (ROWS, 12), 1)
    copies[4].wait()
    repeated = []
    for pair in range(3):
        chosen = col == 6 * core_ref[0] + 2 * pair + (row & 1)
        repeated.append(
            dot(jnp.where(chosen, 1.0, 0.0).astype(BF16), weight[...], 1, 0).astype(BF16)
        )
    column = (lax.broadcasted_iota(jnp.int32, (ROWS, LANES), 0) >> 4) & 3
    for place in range(PIECE_TILES):
        value = jnp.zeros((ROWS, LANES), BF16)
        for piece, at, pair, tile in half_tiles():
            if at == place:
                value = jnp.where(column == piece, repeated[pair][:, lanes(tile)], value)
        out_ref[:, :, lanes(place, BASE)] = value.reshape(64, 2, LANES)
    for part in range(3):
        copies[part].wait()
        out_ref[:, :, part * WIDTH : (part + 1) * WIDTH] = parts[part].reshape(64, 2, WIDTH)
    copies[3].wait()
    out_ref[:, :, 3 * WIDTH : BASE] = cotangent[...].reshape(64, 2, OUT)


def attend(rows_ref, weights_ref, put):
    row = lax.broadcasted_iota(jnp.int32, (ROWS, ROWS), 0)
    col = lax.broadcasted_iota(jnp.int32, (ROWS, ROWS), 1)
    bias = jnp.where(((row ^ col) & 1) == 0, 0.0, -1e30)
    for index in range(HEADS):
        weights_ref[index] = head_products(rows_ref, 0, rows_ref, WIDTH, index)
    for index in range(HEADS):
        scores = weights_ref[index] * INV_ROOT + bias
        powers = jnp.exp(scores - jnp.max(scores, axis=1, keepdims=True))
        weights_ref[index] = powers * (1.0 / jnp.sum(powers, axis=1, keepdims=True))
    for tile in range(TILES):
        rounded = [weights_ref[index].astype(BF16) for index in tile_heads(tile)]
        values = stacked_heads(rows_ref, 2 * WIDTH, tile)
        put(tile, dot(jnp.concatenate(rounded, axis=1), values, 1, 0).astype(BF16))


def ordered_channels(rows_ref):
    return dot(rows_ref[:, 3 * WIDTH : BASE], channel_order(), 1, 0).astype(BF16)


def forward_kernel(core_ref, sent_ref, share_ref, columns_ref, rows_ref, weights_ref, channels_ref):
    rows_ref[...] = sent_ref[...].reshape(ROWS, COLS)
    channels_ref[...] = ordered_channels(rows_ref)

    def put(tile, value):
        share_ref[:, lanes(tile)] = value

    attend(rows_ref, weights_ref, put)
    own = pl.multiple_of(core_ref[0] * HALF, HALF)
    other = pl.multiple_of((1 - core_ref[0]) * HALF, HALF)
    columns_ref[...] = channels_ref[:, pl.ds(own, HALF)]
    share_ref[:, WIDTH : WIDTH + HALF] = channels_ref[:, pl.ds(other, HALF)]
    share_ref[:, WIDTH + HALF :] = rows_ref[:, BASE:]


def weight_grad_kernel(core_ref, share_ref, received_ref, columns_ref, out_ref, pieces_ref):
    own = pl.multiple_of(core_ref[0] * PIECE, PIECE)
    other = pl.multiple_of((1 - core_ref[0]) * PIECE, PIECE)
    pieces_ref[:, pl.ds(own, PIECE)] = share_ref[:, WIDTH + HALF :]
    pieces_ref[:, pl.ds(other, PIECE)] = received_ref[:, WIDTH + HALF :]
    columns = jnp.concatenate([columns_ref[...], received_ref[:, WIDTH : WIDTH + HALF]], axis=0)
    features = jnp.concatenate([share_ref[:, :WIDTH], received_ref[:, :WIDTH]], axis=0)
    partial = dot(columns, features, 0, 0).astype(BF16)
    for pair in range(3):
        out_ref[:, :, pair * WIDTH : (pair + 1) * WIDTH] = partial[
            pair * ROWS : (pair + 1) * ROWS
        ].reshape(64, 2, WIDTH)


def backward_kernel(x_ref, sent_ref, *refs):
    pieces_refs, refs = refs[:4], refs[4:]
    (
        out_ref, rows_ref, weights_ref, channels_ref, attended_ref, matrix_ref, upstream_ref,
        grad_scores_ref,
    ) = refs
    rows_ref[...] = sent_ref[...].reshape(ROWS, COLS)
    channels_ref[...] = ordered_channels(rows_ref)

    def put_attended(tile, value):
        attended_ref[:, lanes(tile)] = value

    attend(rows_ref, weights_ref, put_attended)
    for here in range(4):

        @pl.when(x_ref[0] == here)
        def _():
            for core in range(2):
                for piece, place, pair, tile in half_tiles():
                    start = core * HALF + pair * ROWS
                    matrix_ref[start : start + ROWS, lanes(tile)] = pieces_refs[
                        (here - piece) & 3
                    ][:, lanes(place, core * PIECE)]

    upstream_ref[...] = dot(channels_ref[...], matrix_ref[...], 1, 0).astype(BF16)
    products = [
        head_products(upstream_ref, 0, rows_ref, 2 * WIDTH, index) for index in range(HEADS)
    ]
    for index in range(HEADS):
        weights, grad_weights = weights_ref[index], products[index]
        centred = grad_weights - jnp.sum(weights * grad_weights, axis=1, keepdims=True)
        grad_scores_ref[index] = (weights * centred * INV_ROOT).astype(BF16)

    def put(start, value):
        out_ref[:, :, start : start + value.shape[1]] = value.astype(BF16).reshape(64, 2, -1)

    projected = dot(attended_ref[...], matrix_ref[...], 1, 1).astype(BF16)
    put(3 * WIDTH, dot(projected, channel_order(), 1, 1))
    for tile in range(TILES):
        heads = tile_heads(tile)
        grad_scores = [grad_scores_ref[index] for index in heads]
        rounded = [weights_ref[index].astype(BF16) for index in heads]
        across, down = jnp.concatenate(grad_scores, axis=1), jnp.concatenate(grad_scores, axis=0)
        put(tile * LANES, dot(across, stacked_heads(rows_ref, WIDTH, tile), 1, 0))
        put(WIDTH + tile * LANES, dot(down, stacked_heads(rows_ref, 0, tile), 0, 0))
        put(
            2 * WIDTH + tile * LANES,
            dot(jnp.concatenate(rounded, axis=0), stacked_heads(upstream_ref, 0, tile), 0, 0),
        )


def owned_kernel(terms_ref, out_ref):
    rows = terms_ref[...].reshape(ROWS, HALF_WIDTH)
    target = lax.broadcasted_iota(jnp.int32, (8, ROWS), 0)
    source = lax.broadcasted_iota(jnp.int32, (8, ROWS), 1)
    chosen = jnp.where(target == (source & 1), 1.0, 0.0).astype(BF16)
    out_ref[...] = dot(chosen, rows, 1, 0)[:2]


def unpack_kernel(back_ref, projected_hbm, grads_hbm, rows_ref, sems):
    rows_ref[...] = back_ref[...].reshape(ROWS, BASE)
    parts = [(rows_ref.at[:, 3 * WIDTH :], projected_hbm)]
    for part in range(3):
        parts.append((rows_ref.at[:, part * WIDTH : (part + 1) * WIDTH], grads_hbm.at[part]))
    copies = [
        pltpu.make_async_copy(source, target, sems.at[place])
        for place, (source, target) in enumerate(parts)
    ]
    for copy in copies:
        copy.start()
    for copy in copies:
        copy.wait()


def group_kernel(*refs):
    *terms, out_ref = refs
    total = terms[0][...]
    for term in terms[1:]:
        total += term[...]
    out_ref[...] = total * GRAD_SCALE


def total_kernel(core_ref, mine_ref, theirs_ref, out_ref):
    for core in range(2):
        total = jnp.where(core_ref[0] == core, mine_ref[...], theirs_ref[...])
        for pair in range(3):
            start = 6 * core + 2 * pair
            out_ref[start : start + 2, :] = total[:, pair * WIDTH : (pair + 1) * WIDTH]


IN_VMEM = pl.BlockSpec(memory_space=pltpu.VMEM)
IN_SMEM = pl.BlockSpec(memory_space=pltpu.SMEM)
IN_HBM = pl.BlockSpec(memory_space=pltpu.HBM)


def call(kernel, name, operands, specs, outs, scratch=(), grant=12, micros=1, out_spec=IN_VMEM):
    return pl.pallas_call(
        kernel,
        out_shape=[jax.ShapeDtypeStruct(shape, dtype) for shape, dtype in outs],
        in_specs=specs,
        out_specs=[out_spec] * len(outs),
        scratch_shapes=list(scratch),
        compiler_params=pltpu.CompilerParams(vmem_limit_bytes=grant << 20),
        cost_estimate=pl.CostEstimate(
            flops=micros * 10**9, bytes_accessed=micros * 3 * 10**6, transcendentals=0
        ),
        name=name,
    )(*operands)


def exchange(value, axes):
    return lax.all_to_all(value, axes, 0, 0, tiled=True)


def swap(value):
    return lax.ppermute(value, "c", [(0, 1), (1, 0)])


def turn(value, axis, step):
    return lax.ppermute(value, axis, [(place, (place + step) % 4) for place in range(4)])


def on_device(query_key_value, out_weight, cotangent):
    core = lax.axis_index("c").astype(jnp.int32).reshape(1)
    x_place = lax.axis_index("x").astype(jnp.int32).reshape(1)
    (packed,) = call(
        pack_kernel,
        "pack",
        (core, query_key_value.reshape(3, ROWS, WIDTH), cotangent.reshape(ROWS, OUT), out_weight),
        [IN_SMEM] + [IN_HBM] * 3,
        [((64, 2, COLS), BF16)],
        [
            pltpu.VMEM((3, ROWS, WIDTH), BF16),
            pltpu.VMEM((ROWS, OUT), BF16),
            pltpu.VMEM((12, WIDTH), BF16),
            pltpu.SemaphoreType.DMA((5,)),
        ],
        grant=56,
    )
    sent = exchange(packed, SEQ)
    share, columns = call(
        forward_kernel,
        "forward",
        (core, sent),
        [IN_SMEM, IN_VMEM],
        [((ROWS, SHARE), BF16), ((ROWS, HALF), BF16)],
        [
            pltpu.VMEM((ROWS, COLS), BF16),
            pltpu.VMEM((HEADS, ROWS, ROWS), F32),
            pltpu.VMEM((ROWS, OUT), BF16),
        ],
        micros=3,
    )
    partial, pieces = call(
        weight_grad_kernel,
        "weight_grad",
        (core, share, swap(share), columns),
        [IN_SMEM] + [IN_VMEM] * 3,
        [((64, 2, HALF_WIDTH), BF16), ((ROWS, 2 * PIECE), BF16)],
    )
    collected = exchange(partial, SEQ)
    turned = [turn(pieces, "x", step) for step in range(1, 4)]
    (results,) = call(
        backward_kernel,
        "backward",
        (x_place, sent, pieces, *turned),
        [IN_SMEM] + [IN_VMEM] * 5,
        [((64, 2, BASE), BF16)],
        [
            pltpu.VMEM((ROWS, COLS), BF16),
            pltpu.VMEM((HEADS, ROWS, ROWS), F32),
            pltpu.VMEM((ROWS, OUT), BF16),
            pltpu.VMEM((ROWS, WIDTH), BF16),
            pltpu.VMEM((OUT, WIDTH), BF16),
            pltpu.VMEM((ROWS, WIDTH), BF16),
            pltpu.VMEM((HEADS, ROWS, ROWS), BF16),
        ],
        micros=4,
    )
    results, collected = lax.optimization_barrier((results, collected))
    back = exchange(results, SEQ)
    (owned,) = call(owned_kernel, "owned", (collected,), [IN_VMEM], [((2, HALF_WIDTH), F32)])
    turned = [turn(owned, "yl", step) for step in range(1, 4)]
    (group,) = call(
        group_kernel, "group", (owned, *turned), [IN_VMEM] * 4, [((2, HALF_WIDTH), F32)]
    )
    (total,) = call(
        total_kernel,
        "total",
        (core, group, swap(group)),
        [IN_SMEM] + [IN_VMEM] * 2,
        [((12, WIDTH), F32)],
    )
    projected, grads = call(
        unpack_kernel,
        "unpack",
        (back,),
        [IN_VMEM],
        [((ROWS, OUT), BF16), ((3, ROWS, WIDTH), BF16)],
        [pltpu.VMEM((ROWS, BASE), BF16), pltpu.SemaphoreType.DMA((4,))],
        out_spec=IN_HBM,
    )
    return (
        projected.reshape(1, 1, ROWS, OUT),
        grads.reshape(3, 1, 1, ROWS, WIDTH),
        total,
    )


def solution(mesh):
    split = Mesh(mesh.devices.reshape(4, 2, 2, 4, 8), ("yl", "c", "yh", "x", "z"))
    in_specs = (P(None, GROUPS, SEQ, None, None), P(SEQ, None), P(GROUPS, SEQ, None, None))
    out_specs = (P(GROUPS, SEQ, None, None), P(None, GROUPS, SEQ, None, None), P(SEQ, None))
    return jax.shard_map(
        on_device, mesh=split, in_specs=in_specs, out_specs=out_specs, check_vma=False
    )
```

```python
import math

import jax
import jax.numpy as jnp
from jax import lax
from jax.experimental import pallas as pl
from jax.experimental.pallas import tpu as pltpu
from jax.sharding import Mesh
from jax.sharding import PartitionSpec as P

HEADS = 16
HEAD_DIM = 72
ROWS = 128
LANES = 128
WIDTH = 1152
TILES = WIDTH // LANES
OUT = 768
HALF = OUT // 2
BASE = 3 * WIDTH + OUT
PIECE = 896
PIECE_TILES = PIECE // LANES
COLS = BASE + PIECE
HALF_WIDTH = 3 * WIDTH
INV_ROOT = 1.0 / math.sqrt(HEAD_DIM)
GRAD_SCALE = 1.0 / math.sqrt(512 * ROWS)
BF16 = jnp.bfloat16
F32 = jnp.float32

SEQ = ("yh", "x", "z")
GROUPS = ("yl", "c")


def dot(lhs, rhs, lhs_dim, rhs_dim):
    return lax.dot_general(
        lhs, rhs, (((lhs_dim,), (rhs_dim,)), ((), ())), preferred_element_type=F32
    )


def lanes(tile, base=0):
    return slice(base + tile * LANES, base + (tile + 1) * LANES)


def only_head(index, start, value):
    feature = lax.broadcasted_iota(jnp.int32, value.shape, 1) + start
    inside = (feature >= index * HEAD_DIM) & (feature < (index + 1) * HEAD_DIM)
    return jnp.where(inside, value, jnp.zeros_like(value))


def head_lanes(index):
    first = index * HEAD_DIM // LANES
    last = ((index + 1) * HEAD_DIM - 1) // LANES + 1
    return first * LANES, last * LANES


def head_products(lhs_ref, lhs_base, rhs_ref, rhs_base, index):
    start, stop = head_lanes(index)
    rhs = only_head(index, start, rhs_ref[:, rhs_base + start : rhs_base + stop])
    return dot(lhs_ref[:, lhs_base + start : lhs_base + stop], rhs, 1, 1)


def tile_heads(tile):
    return [
        index
        for index in range(HEADS)
        if index * HEAD_DIM < (tile + 1) * LANES and (index + 1) * HEAD_DIM > tile * LANES
    ]


def stacked_heads(ref, base, tile):
    value = ref[:, lanes(tile, base)]
    return jnp.concatenate(
        [only_head(index, tile * LANES, value) for index in tile_heads(tile)], axis=0
    )


def channel_order():
    natural = lax.broadcasted_iota(jnp.int32, (OUT, OUT), 0)
    place = lax.broadcasted_iota(jnp.int32, (OUT, OUT), 1)
    source = 12 * ((place & 127) >> 1) + 2 * (place >> 7) + (place & 1)
    return jnp.where(natural == source, 1.0, 0.0).astype(BF16)


def half_tiles():
    return [
        (tile // PIECE_TILES, tile % PIECE_TILES, tile // TILES, tile % TILES)
        for tile in range(3 * TILES)
    ]


def pack_kernel(
    core_ref, parts_hbm, cotangent_hbm, weight_hbm, out_ref, parts, cotangent, weight, sems
):
    pairs = [(parts_hbm.at[part], parts.at[part]) for part in range(3)]
    pairs += [(cotangent_hbm, cotangent), (weight_hbm, weight)]
    copies = [
        pltpu.make_async_copy(source, target, sems.at[place])
        for place, (source, target) in enumerate(pairs)
    ]
    for copy in copies:
        copy.start()
    row = lax.broadcasted_iota(jnp.int32, (ROWS, 12), 0)
    col = lax.broadcasted_iota(jnp.int32, (ROWS, 12), 1)
    copies[4].wait()
    repeated = []
    for pair in range(3):
        chosen = col == 6 * core_ref[0] + 2 * pair + (row & 1)
        repeated.append(
            dot(jnp.where(chosen, 1.0, 0.0).astype(BF16), weight[...], 1, 0).astype(BF16)
        )
    column = (lax.broadcasted_iota(jnp.int32, (ROWS, LANES), 0) >> 4) & 3
    for place in range(PIECE_TILES):
        value = jnp.zeros((ROWS, LANES), BF16)
        for piece, at, pair, tile in half_tiles():
            if at == place:
                value = jnp.where(column == piece, repeated[pair][:, lanes(tile)], value)
        out_ref[:, :, lanes(place, BASE)] = value.reshape(64, 2, LANES)
    for part in range(3):
        copies[part].wait()
        out_ref[:, :, part * WIDTH : (part + 1) * WIDTH] = parts[part].reshape(64, 2, WIDTH)
    copies[3].wait()
    out_ref[:, :, 3 * WIDTH : BASE] = cotangent[...].reshape(64, 2, OUT)


def attend(rows_ref, weights_ref, put):
    row = lax.broadcasted_iota(jnp.int32, (ROWS, ROWS), 0)
    col = lax.broadcasted_iota(jnp.int32, (ROWS, ROWS), 1)
    bias = jnp.where(((row ^ col) & 1) == 0, 0.0, -1e30)
    for index in range(HEADS):
        weights_ref[index] = head_products(rows_ref, 0, rows_ref, WIDTH, index)
    for index in range(HEADS):
        scores = weights_ref[index] * INV_ROOT + bias
        powers = jnp.exp(scores - jnp.max(scores, axis=1, keepdims=True))
        weights_ref[index] = powers * (1.0 / jnp.sum(powers, axis=1, keepdims=True))
    for tile in range(TILES):
        rounded = [weights_ref[index].astype(BF16) for index in tile_heads(tile)]
        values = stacked_heads(rows_ref, 2 * WIDTH, tile)
        put(tile, dot(jnp.concatenate(rounded, axis=1), values, 1, 0).astype(BF16))


def ordered_channels(rows_ref):
    return dot(rows_ref[:, 3 * WIDTH : BASE], channel_order(), 1, 0).astype(BF16)


def forward_kernel(core_ref, sent_ref, share_ref, columns_ref, rows_ref, weights_ref, channels_ref):
    rows_ref[...] = sent_ref[...].reshape(ROWS, COLS)
    channels_ref[...] = ordered_channels(rows_ref)

    def put(tile, value):
        share_ref[:, lanes(tile)] = value

    attend(rows_ref, weights_ref, put)
    own = pl.multiple_of(core_ref[0] * HALF, HALF)
    other = pl.multiple_of((1 - core_ref[0]) * HALF, HALF)
    columns_ref[...] = channels_ref[:, pl.ds(own, HALF)]
    share_ref[:, WIDTH:] = channels_ref[:, pl.ds(other, HALF)]


def weight_grad_kernel(share_ref, received_ref, columns_ref, out_ref):
    columns = jnp.concatenate([columns_ref[...], received_ref[:, WIDTH:]], axis=0)
    features = jnp.concatenate([share_ref[:, :WIDTH], received_ref[:, :WIDTH]], axis=0)
    partial = dot(columns, features, 0, 0).astype(BF16)
    for pair in range(3):
        out_ref[:, :, pair * WIDTH : (pair + 1) * WIDTH] = partial[
            pair * ROWS : (pair + 1) * ROWS
        ].reshape(64, 2, WIDTH)


def backward_kernel(
    core_ref, x_ref, sent_ref, mine_ref, theirs_ref,
    out_ref, rows_ref, weights_ref, channels_ref, attended_ref, matrix_ref, upstream_ref,
    grad_scores_ref,
):
    rows_ref[...] = sent_ref[...].reshape(ROWS, COLS)
    channels_ref[...] = ordered_channels(rows_ref)

    def put_attended(tile, value):
        attended_ref[:, lanes(tile)] = value

    attend(rows_ref, weights_ref, put_attended)
    own = pl.multiple_of(core_ref[0] * HALF, HALF)
    other = pl.multiple_of((1 - core_ref[0]) * HALF, HALF)
    for here in range(4):

        @pl.when(x_ref[0] == here)
        def _():
            for piece, place, pair, tile in half_tiles():
                for start, half_ref in ((own, mine_ref), (other, theirs_ref)):
                    matrix_ref[pl.ds(start + pair * ROWS, ROWS), lanes(tile)] = half_ref[
                        (here - piece) & 3, :, lanes(place)
                    ]

    upstream_ref[...] = dot(channels_ref[...], matrix_ref[...], 1, 0).astype(BF16)
    products = [
        head_products(upstream_ref, 0, rows_ref, 2 * WIDTH, index) for index in range(HEADS)
    ]
    for index in range(HEADS):
        weights, grad_weights = weights_ref[index], products[index]
        centred = grad_weights - jnp.sum(weights * grad_weights, axis=1, keepdims=True)
        grad_scores_ref[index] = (weights * centred * INV_ROOT).astype(BF16)

    def put(start, value):
        out_ref[:, :, start : start + value.shape[1]] = value.astype(BF16).reshape(64, 2, -1)

    projected = dot(attended_ref[...], matrix_ref[...], 1, 1).astype(BF16)
    put(3 * WIDTH, dot(projected, channel_order(), 1, 1))
    for tile in range(TILES):
        heads = tile_heads(tile)
        grad_scores = [grad_scores_ref[index] for index in heads]
        rounded = [weights_ref[index].astype(BF16) for index in heads]
        across, down = jnp.concatenate(grad_scores, axis=1), jnp.concatenate(grad_scores, axis=0)
        put(tile * LANES, dot(across, stacked_heads(rows_ref, WIDTH, tile), 1, 0))
        put(WIDTH + tile * LANES, dot(down, stacked_heads(rows_ref, 0, tile), 0, 0))
        put(
            2 * WIDTH + tile * LANES,
            dot(jnp.concatenate(rounded, axis=0), stacked_heads(upstream_ref, 0, tile), 0, 0),
        )


def owned_kernel(terms_ref, out_ref):
    rows = terms_ref[...].reshape(ROWS, HALF_WIDTH)
    target = lax.broadcasted_iota(jnp.int32, (8, ROWS), 0)
    source = lax.broadcasted_iota(jnp.int32, (8, ROWS), 1)
    chosen = jnp.where(target == (source & 1), 1.0, 0.0).astype(BF16)
    out_ref[...] = dot(chosen, rows, 1, 0)[:2]


def unpack_kernel(back_ref, projected_hbm, grads_hbm, rows_ref, sems):
    rows_ref[...] = back_ref[...].reshape(ROWS, BASE)
    parts = [(rows_ref.at[:, 3 * WIDTH :], projected_hbm)]
    for part in range(3):
        parts.append((rows_ref.at[:, part * WIDTH : (part + 1) * WIDTH], grads_hbm.at[part]))
    copies = [
        pltpu.make_async_copy(source, target, sems.at[place])
        for place, (source, target) in enumerate(parts)
    ]
    for copy in copies:
        copy.start()
    for copy in copies:
        copy.wait()


def group_kernel(*refs):
    *terms, out_ref = refs
    total = terms[0][...]
    for term in terms[1:]:
        total += term[...]
    out_ref[...] = total * GRAD_SCALE


def total_kernel(core_ref, mine_ref, theirs_ref, out_ref):
    for core in range(2):
        total = jnp.where(core_ref[0] == core, mine_ref[...], theirs_ref[...])
        for pair in range(3):
            start = 6 * core + 2 * pair
            out_ref[start : start + 2, :] = total[:, pair * WIDTH : (pair + 1) * WIDTH]


IN_VMEM = pl.BlockSpec(memory_space=pltpu.VMEM)
IN_SMEM = pl.BlockSpec(memory_space=pltpu.SMEM)
IN_HBM = pl.BlockSpec(memory_space=pltpu.HBM)


def call(kernel, name, operands, specs, outs, scratch=(), grant=12, micros=1, out_spec=IN_VMEM):
    return pl.pallas_call(
        kernel,
        out_shape=[jax.ShapeDtypeStruct(shape, dtype) for shape, dtype in outs],
        in_specs=specs,
        out_specs=[out_spec] * len(outs),
        scratch_shapes=list(scratch),
        compiler_params=pltpu.CompilerParams(vmem_limit_bytes=grant << 20),
        cost_estimate=pl.CostEstimate(
            flops=micros * 10**9, bytes_accessed=micros * 3 * 10**6, transcendentals=0
        ),
        name=name,
    )(*operands)


def exchange(value, axes):
    return lax.all_to_all(value, axes, 0, 0, tiled=True)


def swap(value):
    return lax.ppermute(value, "c", [(0, 1), (1, 0)])


def turn(value, axis, step):
    return lax.ppermute(value, axis, [(place, (place + step) % 4) for place in range(4)])


def on_device(query_key_value, out_weight, cotangent):
    core = lax.axis_index("c").astype(jnp.int32).reshape(1)
    x_place = lax.axis_index("x").astype(jnp.int32).reshape(1)
    (packed,) = call(
        pack_kernel,
        "pack",
        (core, query_key_value.reshape(3, ROWS, WIDTH), cotangent.reshape(ROWS, OUT), out_weight),
        [IN_SMEM] + [IN_HBM] * 3,
        [((64, 2, COLS), BF16)],
        [
            pltpu.VMEM((3, ROWS, WIDTH), BF16),
            pltpu.VMEM((ROWS, OUT), BF16),
            pltpu.VMEM((12, WIDTH), BF16),
            pltpu.SemaphoreType.DMA((5,)),
        ],
        grant=56,
    )
    sent = exchange(packed, SEQ)
    share, columns = call(
        forward_kernel,
        "forward",
        (core, sent),
        [IN_SMEM, IN_VMEM],
        [((ROWS, WIDTH + HALF), BF16), ((ROWS, HALF), BF16)],
        [
            pltpu.VMEM((ROWS, COLS), BF16),
            pltpu.VMEM((HEADS, ROWS, ROWS), F32),
            pltpu.VMEM((ROWS, OUT), BF16),
        ],
        micros=3,
    )
    piece = sent[:, :, BASE:].reshape(ROWS, PIECE)
    turned = [turn(piece, "x", step) for step in range(1, 4)]
    (partial,) = call(
        weight_grad_kernel,
        "weight_grad",
        (share, swap(share), columns),
        [IN_VMEM] * 3,
        [((64, 2, HALF_WIDTH), BF16)],
    )
    collected = exchange(partial, SEQ)
    piece, *turned = lax.optimization_barrier((piece, *turned, partial))[:4]
    mine = jnp.stack([piece, *turned])
    (results,) = call(
        backward_kernel,
        "backward",
        (core, x_place, sent, mine, swap(mine)),
        [IN_SMEM] * 2 + [IN_VMEM] * 3,
        [((64, 2, BASE), BF16)],
        [
            pltpu.VMEM((ROWS, COLS), BF16),
            pltpu.VMEM((HEADS, ROWS, ROWS), F32),
            pltpu.VMEM((ROWS, OUT), BF16),
            pltpu.VMEM((ROWS, WIDTH), BF16),
            pltpu.VMEM((OUT, WIDTH), BF16),
            pltpu.VMEM((ROWS, WIDTH), BF16),
            pltpu.VMEM((HEADS, ROWS, ROWS), BF16),
        ],
        micros=7,
    )
    results, collected = lax.optimization_barrier((results, collected))
    (owned,) = call(owned_kernel, "owned", (collected,), [IN_VMEM], [((2, HALF_WIDTH), F32)])
    turned = [turn(owned, "yl", step) for step in range(1, 4)]
    back = exchange(results, SEQ)
    (group,) = call(
        group_kernel, "group", (owned, *turned), [IN_VMEM] * 4, [((2, HALF_WIDTH), F32)]
    )
    (total,) = call(
        total_kernel,
        "total",
        (core, group, swap(group)),
        [IN_SMEM] + [IN_VMEM] * 2,
        [((12, WIDTH), F32)],
    )
    projected, grads = call(
        unpack_kernel,
        "unpack",
        (back,),
        [IN_VMEM],
        [((ROWS, OUT), BF16), ((3, ROWS, WIDTH), BF16)],
        [pltpu.VMEM((ROWS, BASE), BF16), pltpu.SemaphoreType.DMA((4,))],
        out_spec=IN_HBM,
    )
    return (
        projected.reshape(1, 1, ROWS, OUT),
        grads.reshape(3, 1, 1, ROWS, WIDTH),
        total,
    )


def solution(mesh):
    split = Mesh(mesh.devices.reshape(4, 2, 2, 4, 8), ("yl", "c", "yh", "x", "z"))
    in_specs = (P(None, GROUPS, SEQ, None, None), P(SEQ, None), P(GROUPS, SEQ, None, None))
    out_specs = (P(GROUPS, SEQ, None, None), P(None, GROUPS, SEQ, None, None), P(SEQ, None))
    return jax.shard_map(
        on_device, mesh=split, in_specs=in_specs, out_specs=out_specs, check_vma=False
    )
```

```python
import math

import jax
import jax.numpy as jnp
from jax import lax
from jax.experimental import pallas as pl
from jax.experimental.pallas import tpu as pltpu
from jax.sharding import Mesh
from jax.sharding import PartitionSpec as P

HEADS = 16
HEAD_DIM = 72
ROWS = 128
LANES = 128
WIDTH = 1152
TILES = WIDTH // LANES
OUT = 768
HALF = OUT // 2
BASE = 3 * WIDTH + OUT
PIECE = 896
PIECE_TILES = PIECE // LANES
COLS = BASE + PIECE
HALF_WIDTH = 3 * WIDTH
INV_ROOT = 1.0 / math.sqrt(HEAD_DIM)
GRAD_SCALE = 1.0 / math.sqrt(512 * ROWS)
BF16 = jnp.bfloat16
F32 = jnp.float32

SEQ = ("yh", "x", "z")
GROUPS = ("yl", "c")


def dot(lhs, rhs, lhs_dim, rhs_dim):
    return lax.dot_general(
        lhs, rhs, (((lhs_dim,), (rhs_dim,)), ((), ())), preferred_element_type=F32
    )


def lanes(tile, base=0):
    return slice(base + tile * LANES, base + (tile + 1) * LANES)


def only_head(index, start, value):
    feature = lax.broadcasted_iota(jnp.int32, value.shape, 1) + start
    inside = (feature >= index * HEAD_DIM) & (feature < (index + 1) * HEAD_DIM)
    return jnp.where(inside, value, jnp.zeros_like(value))


def head_lanes(index):
    first = index * HEAD_DIM // LANES
    last = ((index + 1) * HEAD_DIM - 1) // LANES + 1
    return first * LANES, last * LANES


def head_products(lhs_ref, lhs_base, rhs_ref, rhs_base, index):
    start, stop = head_lanes(index)
    rhs = only_head(index, start, rhs_ref[:, rhs_base + start : rhs_base + stop])
    return dot(lhs_ref[:, lhs_base + start : lhs_base + stop], rhs, 1, 1)


def tile_heads(tile):
    return [
        index
        for index in range(HEADS)
        if index * HEAD_DIM < (tile + 1) * LANES and (index + 1) * HEAD_DIM > tile * LANES
    ]


def stacked_heads(ref, base, tile):
    value = ref[:, lanes(tile, base)]
    return jnp.concatenate(
        [only_head(index, tile * LANES, value) for index in tile_heads(tile)], axis=0
    )


def channel_order():
    natural = lax.broadcasted_iota(jnp.int32, (OUT, OUT), 0)
    place = lax.broadcasted_iota(jnp.int32, (OUT, OUT), 1)
    source = 12 * ((place & 127) >> 1) + 2 * (place >> 7) + (place & 1)
    return jnp.where(natural == source, 1.0, 0.0).astype(BF16)


def half_tiles():
    return [
        (tile // PIECE_TILES, tile % PIECE_TILES, tile // TILES, tile % TILES)
        for tile in range(3 * TILES)
    ]


def pack_kernel(
    core_ref, parts_hbm, cotangent_hbm, weight_hbm, out_ref, parts, cotangent, weight, sems
):
    pairs = [(parts_hbm.at[part], parts.at[part]) for part in range(3)]
    pairs += [(cotangent_hbm, cotangent), (weight_hbm, weight)]
    copies = [
        pltpu.make_async_copy(source, target, sems.at[place])
        for place, (source, target) in enumerate(pairs)
    ]
    for copy in copies:
        copy.start()
    row = lax.broadcasted_iota(jnp.int32, (ROWS, 12), 0)
    col = lax.broadcasted_iota(jnp.int32, (ROWS, 12), 1)
    copies[4].wait()
    repeated = []
    for pair in range(3):
        chosen = col == 6 * core_ref[0] + 2 * pair + (row & 1)
        repeated.append(
            dot(jnp.where(chosen, 1.0, 0.0).astype(BF16), weight[...], 1, 0).astype(BF16)
        )
    column = (lax.broadcasted_iota(jnp.int32, (ROWS, LANES), 0) >> 4) & 3
    for place in range(PIECE_TILES):
        value = jnp.zeros((ROWS, LANES), BF16)
        for piece, at, pair, tile in half_tiles():
            if at == place:
                value = jnp.where(column == piece, repeated[pair][:, lanes(tile)], value)
        out_ref[:, :, lanes(place, BASE)] = value.reshape(64, 2, LANES)
    for part in range(3):
        copies[part].wait()
        out_ref[:, :, part * WIDTH : (part + 1) * WIDTH] = parts[part].reshape(64, 2, WIDTH)
    copies[3].wait()
    out_ref[:, :, 3 * WIDTH : BASE] = cotangent[...].reshape(64, 2, OUT)


def attend(rows_ref, weights_ref, put):
    row = lax.broadcasted_iota(jnp.int32, (ROWS, ROWS), 0)
    col = lax.broadcasted_iota(jnp.int32, (ROWS, ROWS), 1)
    bias = jnp.where(((row ^ col) & 1) == 0, 0.0, -1e30)
    for index in range(HEADS):
        weights_ref[index] = head_products(rows_ref, 0, rows_ref, WIDTH, index)
    for index in range(HEADS):
        scores = weights_ref[index] * INV_ROOT + bias
        powers = jnp.exp(scores - jnp.max(scores, axis=1, keepdims=True))
        weights_ref[index] = powers * (1.0 / jnp.sum(powers, axis=1, keepdims=True))
    for tile in range(TILES):
        rounded = [weights_ref[index].astype(BF16) for index in tile_heads(tile)]
        values = stacked_heads(rows_ref, 2 * WIDTH, tile)
        put(tile, dot(jnp.concatenate(rounded, axis=1), values, 1, 0).astype(BF16))


def ordered_channels(rows_ref):
    return dot(rows_ref[:, 3 * WIDTH : BASE], channel_order(), 1, 0).astype(BF16)


def forward_kernel(core_ref, sent_ref, share_ref, columns_ref, rows_ref, weights_ref, channels_ref):
    rows_ref[...] = sent_ref[...].reshape(ROWS, COLS)
    channels_ref[...] = ordered_channels(rows_ref)

    def put(tile, value):
        share_ref[:, lanes(tile)] = value

    attend(rows_ref, weights_ref, put)
    own = pl.multiple_of(core_ref[0] * HALF, HALF)
    other = pl.multiple_of((1 - core_ref[0]) * HALF, HALF)
    columns_ref[...] = channels_ref[:, pl.ds(own, HALF)]
    share_ref[:, WIDTH:] = channels_ref[:, pl.ds(other, HALF)]


def weight_grad_kernel(
    share_ref, received_ref, columns_ref, piece_ref, near_ref, out_ref, pieces_ref
):
    pieces_ref[0] = piece_ref[...]
    pieces_ref[1] = near_ref[...]
    columns = jnp.concatenate([columns_ref[...], received_ref[:, WIDTH:]], axis=0)
    features = jnp.concatenate([share_ref[:, :WIDTH], received_ref[:, :WIDTH]], axis=0)
    partial = dot(columns, features, 0, 0).astype(BF16)
    for pair in range(3):
        out_ref[:, :, pair * WIDTH : (pair + 1) * WIDTH] = partial[
            pair * ROWS : (pair + 1) * ROWS
        ].reshape(64, 2, WIDTH)


def backward_kernel(
    core_ref, x_ref, sent_ref, near_ref, far_ref, their_near_ref, their_far_ref,
    out_ref, rows_ref, weights_ref, channels_ref, attended_ref, matrix_ref, upstream_ref,
    grad_scores_ref,
):
    rows_ref[...] = sent_ref[...].reshape(ROWS, COLS)
    channels_ref[...] = ordered_channels(rows_ref)

    def put_attended(tile, value):
        attended_ref[:, lanes(tile)] = value

    attend(rows_ref, weights_ref, put_attended)
    own = pl.multiple_of(core_ref[0] * HALF, HALF)
    other = pl.multiple_of((1 - core_ref[0]) * HALF, HALF)
    for here in range(4):

        @pl.when(x_ref[0] == here)
        def _():
            for piece, place, pair, tile in half_tiles():
                slot = here ^ piece
                mine = (near_ref, far_ref)[slot >> 1]
                theirs = (their_near_ref, their_far_ref)[slot >> 1]
                for start, half_ref in ((own, mine), (other, theirs)):
                    matrix_ref[pl.ds(start + pair * ROWS, ROWS), lanes(tile)] = half_ref[
                        slot & 1, :, lanes(place)
                    ]

    upstream_ref[...] = dot(channels_ref[...], matrix_ref[...], 1, 0).astype(BF16)
    products = [
        head_products(upstream_ref, 0, rows_ref, 2 * WIDTH, index) for index in range(HEADS)
    ]
    for index in range(HEADS):
        weights, grad_weights = weights_ref[index], products[index]
        centred = grad_weights - jnp.sum(weights * grad_weights, axis=1, keepdims=True)
        grad_scores_ref[index] = (weights * centred * INV_ROOT).astype(BF16)

    def put(start, value):
        out_ref[:, :, start : start + value.shape[1]] = value.astype(BF16).reshape(64, 2, -1)

    projected = dot(attended_ref[...], matrix_ref[...], 1, 1).astype(BF16)
    put(3 * WIDTH, dot(projected, channel_order(), 1, 1))
    for tile in range(TILES):
        heads = tile_heads(tile)
        grad_scores = [grad_scores_ref[index] for index in heads]
        rounded = [weights_ref[index].astype(BF16) for index in heads]
        across, down = jnp.concatenate(grad_scores, axis=1), jnp.concatenate(grad_scores, axis=0)
        put(tile * LANES, dot(across, stacked_heads(rows_ref, WIDTH, tile), 1, 0))
        put(WIDTH + tile * LANES, dot(down, stacked_heads(rows_ref, 0, tile), 0, 0))
        put(
            2 * WIDTH + tile * LANES,
            dot(jnp.concatenate(rounded, axis=0), stacked_heads(upstream_ref, 0, tile), 0, 0),
        )


def owned_kernel(terms_ref, out_ref):
    rows = terms_ref[...].reshape(ROWS, HALF_WIDTH)
    target = lax.broadcasted_iota(jnp.int32, (8, ROWS), 0)
    source = lax.broadcasted_iota(jnp.int32, (8, ROWS), 1)
    chosen = jnp.where(target == (source & 1), 1.0, 0.0).astype(BF16)
    out_ref[...] = dot(chosen, rows, 1, 0)[:2]


def unpack_kernel(back_ref, projected_hbm, grads_hbm, rows_ref, sems):
    rows_ref[...] = back_ref[...].reshape(ROWS, BASE)
    parts = [(rows_ref.at[:, 3 * WIDTH :], projected_hbm)]
    for part in range(3):
        parts.append((rows_ref.at[:, part * WIDTH : (part + 1) * WIDTH], grads_hbm.at[part]))
    copies = [
        pltpu.make_async_copy(source, target, sems.at[place])
        for place, (source, target) in enumerate(parts)
    ]
    for copy in copies:
        copy.start()
    for copy in copies:
        copy.wait()


def group_kernel(*refs):
    *terms, out_ref = refs
    total = terms[0][...]
    for term in terms[1:]:
        total += term[...]
    out_ref[...] = total * GRAD_SCALE


def total_kernel(core_ref, mine_ref, theirs_ref, out_ref):
    for core in range(2):
        total = jnp.where(core_ref[0] == core, mine_ref[...], theirs_ref[...])
        for pair in range(3):
            start = 6 * core + 2 * pair
            out_ref[start : start + 2, :] = total[:, pair * WIDTH : (pair + 1) * WIDTH]


IN_VMEM = pl.BlockSpec(memory_space=pltpu.VMEM)
IN_SMEM = pl.BlockSpec(memory_space=pltpu.SMEM)
IN_HBM = pl.BlockSpec(memory_space=pltpu.HBM)


def call(kernel, name, operands, specs, outs, scratch=(), grant=12, micros=1, out_spec=IN_VMEM):
    return pl.pallas_call(
        kernel,
        out_shape=[jax.ShapeDtypeStruct(shape, dtype) for shape, dtype in outs],
        in_specs=specs,
        out_specs=[out_spec] * len(outs),
        scratch_shapes=list(scratch),
        compiler_params=pltpu.CompilerParams(vmem_limit_bytes=grant << 20),
        cost_estimate=pl.CostEstimate(
            flops=micros * 10**9, bytes_accessed=micros * 3 * 10**6, transcendentals=0
        ),
        name=name,
    )(*operands)


def exchange(value, axes):
    return lax.all_to_all(value, axes, 0, 0, tiled=True)


def swap(value):
    return lax.ppermute(value, "c", [(0, 1), (1, 0)])


def turn(value, axis, step):
    return lax.ppermute(value, axis, [(place, (place + step) % 4) for place in range(4)])


def across(value, bit):
    return lax.ppermute(value, "x", [(place, place ^ bit) for place in range(4)])


def on_device(query_key_value, out_weight, cotangent):
    core = lax.axis_index("c").astype(jnp.int32).reshape(1)
    x_place = lax.axis_index("x").astype(jnp.int32).reshape(1)
    (packed,) = call(
        pack_kernel,
        "pack",
        (core, query_key_value.reshape(3, ROWS, WIDTH), cotangent.reshape(ROWS, OUT), out_weight),
        [IN_SMEM] + [IN_HBM] * 3,
        [((64, 2, COLS), BF16)],
        [
            pltpu.VMEM((3, ROWS, WIDTH), BF16),
            pltpu.VMEM((ROWS, OUT), BF16),
            pltpu.VMEM((12, WIDTH), BF16),
            pltpu.SemaphoreType.DMA((5,)),
        ],
        grant=56,
    )
    sent = exchange(packed, SEQ)
    share, columns = call(
        forward_kernel,
        "forward",
        (core, sent),
        [IN_SMEM, IN_VMEM],
        [((ROWS, WIDTH + HALF), BF16), ((ROWS, HALF), BF16)],
        [
            pltpu.VMEM((ROWS, COLS), BF16),
            pltpu.VMEM((HEADS, ROWS, ROWS), F32),
            pltpu.VMEM((ROWS, OUT), BF16),
        ],
        micros=3,
    )
    piece = sent[:, :, BASE:].reshape(ROWS, PIECE)
    partial, pieces = call(
        weight_grad_kernel,
        "weight_grad",
        (share, swap(share), columns, piece, across(piece, 1)),
        [IN_VMEM] * 5,
        [((64, 2, HALF_WIDTH), BF16), ((2, ROWS, PIECE), BF16)],
    )
    far_pieces = across(pieces, 2)
    collected = exchange(partial, SEQ)
    (results,) = call(
        backward_kernel,
        "backward",
        (core, x_place, sent, pieces, far_pieces, swap(pieces), swap(far_pieces)),
        [IN_SMEM] * 2 + [IN_VMEM] * 5,
        [((64, 2, BASE), BF16)],
        [
            pltpu.VMEM((ROWS, COLS), BF16),
            pltpu.VMEM((HEADS, ROWS, ROWS), F32),
            pltpu.VMEM((ROWS, OUT), BF16),
            pltpu.VMEM((ROWS, WIDTH), BF16),
            pltpu.VMEM((OUT, WIDTH), BF16),
            pltpu.VMEM((ROWS, WIDTH), BF16),
            pltpu.VMEM((HEADS, ROWS, ROWS), BF16),
        ],
        micros=10,
    )
    results, collected = lax.optimization_barrier((results, collected))
    (owned,) = call(owned_kernel, "owned", (collected,), [IN_VMEM], [((2, HALF_WIDTH), F32)])
    turned = [turn(owned, "yl", step) for step in range(1, 4)]
    back = exchange(results, SEQ)
    (group,) = call(
        group_kernel, "group", (owned, *turned), [IN_VMEM] * 4, [((2, HALF_WIDTH), F32)]
    )
    (total,) = call(
        total_kernel,
        "total",
        (core, group, swap(group)),
        [IN_SMEM] + [IN_VMEM] * 2,
        [((12, WIDTH), F32)],
    )
    projected, grads = call(
        unpack_kernel,
        "unpack",
        (back,),
        [IN_VMEM],
        [((ROWS, OUT), BF16), ((3, ROWS, WIDTH), BF16)],
        [pltpu.VMEM((ROWS, BASE), BF16), pltpu.SemaphoreType.DMA((4,))],
        out_spec=IN_HBM,
    )
    return (
        projected.reshape(1, 1, ROWS, OUT),
        grads.reshape(3, 1, 1, ROWS, WIDTH),
        total,
    )


def solution(mesh):
    split = Mesh(mesh.devices.reshape(4, 2, 2, 4, 8), ("yl", "c", "yh", "x", "z"))
    in_specs = (P(None, GROUPS, SEQ, None, None), P(SEQ, None), P(GROUPS, SEQ, None, None))
    out_specs = (P(GROUPS, SEQ, None, None), P(None, GROUPS, SEQ, None, None), P(SEQ, None))
    return jax.shard_map(
        on_device, mesh=split, in_specs=in_specs, out_specs=out_specs, check_vma=False
    )
```

```python
import math

import jax
import jax.numpy as jnp
from jax import lax
from jax.experimental import pallas as pl
from jax.experimental.pallas import tpu as pltpu
from jax.sharding import Mesh
from jax.sharding import PartitionSpec as P

HEADS = 16
HEAD_DIM = 72
ROWS = 128
LANES = 128
WIDTH = 1152
TILES = WIDTH // LANES
OUT = 768
HALF = OUT // 2
BASE = 3 * WIDTH + OUT
PIECE = 896
PIECE_TILES = PIECE // LANES
COLS = BASE + PIECE
HALF_WIDTH = 3 * WIDTH
INV_ROOT = 1.0 / math.sqrt(HEAD_DIM)
GRAD_SCALE = 1.0 / math.sqrt(512 * ROWS)
BF16 = jnp.bfloat16
F32 = jnp.float32

SEQ = ("yh", "x", "z")
GROUPS = ("yl", "c")


def dot(lhs, rhs, lhs_dim, rhs_dim):
    return lax.dot_general(
        lhs, rhs, (((lhs_dim,), (rhs_dim,)), ((), ())), preferred_element_type=F32
    )


def lanes(tile, base=0):
    return slice(base + tile * LANES, base + (tile + 1) * LANES)


def only_head(index, start, value):
    feature = lax.broadcasted_iota(jnp.int32, value.shape, 1) + start
    inside = (feature >= index * HEAD_DIM) & (feature < (index + 1) * HEAD_DIM)
    return jnp.where(inside, value, jnp.zeros_like(value))


def head_lanes(index):
    first = index * HEAD_DIM // LANES
    last = ((index + 1) * HEAD_DIM - 1) // LANES + 1
    return first * LANES, last * LANES


def head_products(lhs_ref, lhs_base, rhs_ref, rhs_base, index):
    start, stop = head_lanes(index)
    rhs = only_head(index, start, rhs_ref[:, rhs_base + start : rhs_base + stop])
    return dot(lhs_ref[:, lhs_base + start : lhs_base + stop], rhs, 1, 1)


def tile_heads(tile):
    return [
        index
        for index in range(HEADS)
        if index * HEAD_DIM < (tile + 1) * LANES and (index + 1) * HEAD_DIM > tile * LANES
    ]


def stacked_heads(ref, base, tile):
    value = ref[:, lanes(tile, base)]
    return jnp.concatenate(
        [only_head(index, tile * LANES, value) for index in tile_heads(tile)], axis=0
    )


def channel_order():
    natural = lax.broadcasted_iota(jnp.int32, (OUT, OUT), 0)
    place = lax.broadcasted_iota(jnp.int32, (OUT, OUT), 1)
    source = 12 * ((place & 127) >> 1) + 2 * (place >> 7) + (place & 1)
    return jnp.where(natural == source, 1.0, 0.0).astype(BF16)


def half_tiles():
    return [
        (tile // PIECE_TILES, tile % PIECE_TILES, tile // TILES, tile % TILES)
        for tile in range(3 * TILES)
    ]


def pack_kernel(
    core_ref, parts_hbm, cotangent_hbm, weight_hbm, out_ref, parts, cotangent, weight, sems
):
    pairs = [(parts_hbm.at[part], parts.at[part]) for part in range(3)]
    pairs += [(cotangent_hbm, cotangent), (weight_hbm, weight)]
    copies = [
        pltpu.make_async_copy(source, target, sems.at[place])
        for place, (source, target) in enumerate(pairs)
    ]
    for copy in copies:
        copy.start()
    row = lax.broadcasted_iota(jnp.int32, (ROWS, 12), 0)
    col = lax.broadcasted_iota(jnp.int32, (ROWS, 12), 1)
    copies[4].wait()
    repeated = []
    for pair in range(3):
        chosen = col == 6 * core_ref[0] + 2 * pair + (row & 1)
        repeated.append(
            dot(jnp.where(chosen, 1.0, 0.0).astype(BF16), weight[...], 1, 0).astype(BF16)
        )
    column = (lax.broadcasted_iota(jnp.int32, (ROWS, LANES), 0) >> 4) & 3
    for place in range(PIECE_TILES):
        value = jnp.zeros((ROWS, LANES), BF16)
        for piece, at, pair, tile in half_tiles():
            if at == place:
                value = jnp.where(column == piece, repeated[pair][:, lanes(tile)], value)
        out_ref[:, :, lanes(place, BASE)] = value.reshape(64, 2, LANES)
    for part in range(3):
        copies[part].wait()
        out_ref[:, :, part * WIDTH : (part + 1) * WIDTH] = parts[part].reshape(64, 2, WIDTH)
    copies[3].wait()
    out_ref[:, :, 3 * WIDTH : BASE] = cotangent[...].reshape(64, 2, OUT)


def attend(rows_ref, weights_ref, put):
    row = lax.broadcasted_iota(jnp.int32, (ROWS, ROWS), 0)
    col = lax.broadcasted_iota(jnp.int32, (ROWS, ROWS), 1)
    bias = jnp.where(((row ^ col) & 1) == 0, 0.0, -1e30)
    for index in range(HEADS):
        weights_ref[index] = head_products(rows_ref, 0, rows_ref, WIDTH, index)
    for index in range(HEADS):
        scores = weights_ref[index] * INV_ROOT + bias
        powers = jnp.exp(scores - jnp.max(scores, axis=1, keepdims=True))
        weights_ref[index] = powers * (1.0 / jnp.sum(powers, axis=1, keepdims=True))
    for tile in range(TILES):
        rounded = [weights_ref[index].astype(BF16) for index in tile_heads(tile)]
        values = stacked_heads(rows_ref, 2 * WIDTH, tile)
        put(tile, dot(jnp.concatenate(rounded, axis=1), values, 1, 0).astype(BF16))


def ordered_channels(rows_ref):
    return dot(rows_ref[:, 3 * WIDTH : BASE], channel_order(), 1, 0).astype(BF16)


def forward_kernel(core_ref, sent_ref, share_ref, columns_ref, rows_ref, weights_ref, channels_ref):
    rows_ref[...] = sent_ref[...].reshape(ROWS, COLS)
    channels_ref[...] = ordered_channels(rows_ref)

    def put(tile, value):
        share_ref[:, lanes(tile)] = value

    attend(rows_ref, weights_ref, put)
    own = pl.multiple_of(core_ref[0] * HALF, HALF)
    other = pl.multiple_of((1 - core_ref[0]) * HALF, HALF)
    columns_ref[...] = channels_ref[:, pl.ds(own, HALF)]
    share_ref[:, WIDTH:] = channels_ref[:, pl.ds(other, HALF)]


def weight_grad_kernel(share_ref, received_ref, columns_ref, out_ref):
    columns = jnp.concatenate([columns_ref[...], received_ref[:, WIDTH:]], axis=0)
    features = jnp.concatenate([share_ref[:, :WIDTH], received_ref[:, :WIDTH]], axis=0)
    partial = dot(columns, features, 0, 0).astype(BF16)
    for target in range(4):
        for high in range(2):
            for pair in range(3):
                start = pair * ROWS + high * 64 + target * 16
                out_ref[
                    target, high * 16 : high * 16 + 16, pair * WIDTH : (pair + 1) * WIDTH
                ] = partial[start : start + 16]


def backward_kernel(core_ref, x_ref, sent_ref, *refs):
    mine_refs, their_refs, refs = refs[:4], refs[4:8], refs[8:]
    (
        out_ref, rows_ref, weights_ref, channels_ref, attended_ref, matrix_ref, upstream_ref,
        grad_scores_ref,
    ) = refs
    rows_ref[...] = sent_ref[...].reshape(ROWS, COLS)
    channels_ref[...] = ordered_channels(rows_ref)

    def put_attended(tile, value):
        attended_ref[:, lanes(tile)] = value

    attend(rows_ref, weights_ref, put_attended)
    own = pl.multiple_of(core_ref[0] * HALF, HALF)
    other = pl.multiple_of((1 - core_ref[0]) * HALF, HALF)
    for here in range(4):

        @pl.when(x_ref[0] == here)
        def _():
            for piece, place, pair, tile in half_tiles():
                for start, half_refs in ((own, mine_refs), (other, their_refs)):
                    matrix_ref[pl.ds(start + pair * ROWS, ROWS), lanes(tile)] = half_refs[
                        (here - piece) & 3
                    ][:, lanes(place)]

    upstream_ref[...] = dot(channels_ref[...], matrix_ref[...], 1, 0).astype(BF16)
    products = [
        head_products(upstream_ref, 0, rows_ref, 2 * WIDTH, index) for index in range(HEADS)
    ]
    for index in range(HEADS):
        weights, grad_weights = weights_ref[index], products[index]
        centred = grad_weights - jnp.sum(weights * grad_weights, axis=1, keepdims=True)
        grad_scores_ref[index] = (weights * centred * INV_ROOT).astype(BF16)

    def put(start, value):
        out_ref[:, :, start : start + value.shape[1]] = value.astype(BF16).reshape(64, 2, -1)

    projected = dot(attended_ref[...], matrix_ref[...], 1, 1).astype(BF16)
    put(3 * WIDTH, dot(projected, channel_order(), 1, 1))
    for tile in range(TILES):
        heads = tile_heads(tile)
        grad_scores = [grad_scores_ref[index] for index in heads]
        rounded = [weights_ref[index].astype(BF16) for index in heads]
        across, down = jnp.concatenate(grad_scores, axis=1), jnp.concatenate(grad_scores, axis=0)
        put(tile * LANES, dot(across, stacked_heads(rows_ref, WIDTH, tile), 1, 0))
        put(WIDTH + tile * LANES, dot(down, stacked_heads(rows_ref, 0, tile), 0, 0))
        put(
            2 * WIDTH + tile * LANES,
            dot(jnp.concatenate(rounded, axis=0), stacked_heads(upstream_ref, 0, tile), 0, 0),
        )


def merge_kernel(terms_ref, out_ref):
    total = terms_ref[0].astype(F32)
    for place in range(1, 4):
        total += terms_ref[place].astype(F32)
    out_ref[...] = total.astype(BF16).reshape(16, 2, HALF_WIDTH)


def owned_kernel(terms_ref, out_ref):
    rows = terms_ref[...].reshape(32, HALF_WIDTH)
    target = lax.broadcasted_iota(jnp.int32, (8, 32), 0)
    source = lax.broadcasted_iota(jnp.int32, (8, 32), 1)
    chosen = jnp.where(target == (source & 1), 1.0, 0.0).astype(BF16)
    out_ref[...] = dot(chosen, rows, 1, 0)[:2]


def unpack_kernel(back_ref, projected_hbm, grads_hbm, rows_ref, sems):
    rows_ref[...] = back_ref[...].reshape(ROWS, BASE)
    parts = [(rows_ref.at[:, 3 * WIDTH :], projected_hbm)]
    for part in range(3):
        parts.append((rows_ref.at[:, part * WIDTH : (part + 1) * WIDTH], grads_hbm.at[part]))
    copies = [
        pltpu.make_async_copy(source, target, sems.at[place])
        for place, (source, target) in enumerate(parts)
    ]
    for copy in copies:
        copy.start()
    for copy in copies:
        copy.wait()


def group_kernel(*refs):
    *terms, out_ref = refs
    total = terms[0][...]
    for term in terms[1:]:
        total += term[...]
    out_ref[...] = total * GRAD_SCALE


def total_kernel(core_ref, mine_ref, theirs_ref, out_ref):
    for core in range(2):
        total = jnp.where(core_ref[0] == core, mine_ref[...], theirs_ref[...])
        for pair in range(3):
            start = 6 * core + 2 * pair
            out_ref[start : start + 2, :] = total[:, pair * WIDTH : (pair + 1) * WIDTH]


IN_VMEM = pl.BlockSpec(memory_space=pltpu.VMEM)
IN_SMEM = pl.BlockSpec(memory_space=pltpu.SMEM)
IN_HBM = pl.BlockSpec(memory_space=pltpu.HBM)


def call(kernel, name, operands, specs, outs, scratch=(), grant=12, micros=1, out_spec=IN_VMEM):
    return pl.pallas_call(
        kernel,
        out_shape=[jax.ShapeDtypeStruct(shape, dtype) for shape, dtype in outs],
        in_specs=specs,
        out_specs=[out_spec] * len(outs),
        scratch_shapes=list(scratch),
        compiler_params=pltpu.CompilerParams(vmem_limit_bytes=grant << 20),
        cost_estimate=pl.CostEstimate(
            flops=micros * 10**9, bytes_accessed=micros * 3 * 10**6, transcendentals=0
        ),
        name=name,
    )(*operands)


def exchange(value, axes):
    return lax.all_to_all(value, axes, 0, 0, tiled=True)


def swap(value):
    return lax.ppermute(value, "c", [(0, 1), (1, 0)])


def turn(value, axis, step):
    return lax.ppermute(value, axis, [(place, (place + step) % 4) for place in range(4)])


def on_device(query_key_value, out_weight, cotangent):
    core = lax.axis_index("c").astype(jnp.int32).reshape(1)
    x_place = lax.axis_index("x").astype(jnp.int32).reshape(1)
    (packed,) = call(
        pack_kernel,
        "pack",
        (core, query_key_value.reshape(3, ROWS, WIDTH), cotangent.reshape(ROWS, OUT), out_weight),
        [IN_SMEM] + [IN_HBM] * 3,
        [((64, 2, COLS), BF16)],
        [
            pltpu.VMEM((3, ROWS, WIDTH), BF16),
            pltpu.VMEM((ROWS, OUT), BF16),
            pltpu.VMEM((12, WIDTH), BF16),
            pltpu.SemaphoreType.DMA((5,)),
        ],
        grant=56,
    )
    sent = exchange(packed, SEQ)
    share, columns = call(
        forward_kernel,
        "forward",
        (core, sent),
        [IN_SMEM, IN_VMEM],
        [((ROWS, WIDTH + HALF), BF16), ((ROWS, HALF), BF16)],
        [
            pltpu.VMEM((ROWS, COLS), BF16),
            pltpu.VMEM((HEADS, ROWS, ROWS), F32),
            pltpu.VMEM((ROWS, OUT), BF16),
        ],
        micros=3,
    )
    (partial,) = call(
        weight_grad_kernel,
        "weight_grad",
        (share, swap(share), columns),
        [IN_VMEM] * 3,
        [((4, 32, HALF_WIDTH), BF16)],
    )
    piece, partial = lax.optimization_barrier((sent[:, :, BASE:].reshape(ROWS, PIECE), partial))
    terms = exchange(partial, "x")
    turned = [turn(piece, "x", step) for step in range(1, 4)]
    (summed,) = call(
        merge_kernel, "merge", (terms,), [IN_VMEM], [((16, 2, HALF_WIDTH), BF16)]
    )
    collected = exchange(summed, ("yh", "z"))
    mine = [piece, *lax.optimization_barrier((*turned, summed))[:3]]
    (results,) = call(
        backward_kernel,
        "backward",
        (core, x_place, sent, *mine, *(swap(part) for part in mine)),
        [IN_SMEM] * 2 + [IN_VMEM] * 9,
        [((64, 2, BASE), BF16)],
        [
            pltpu.VMEM((ROWS, COLS), BF16),
            pltpu.VMEM((HEADS, ROWS, ROWS), F32),
            pltpu.VMEM((ROWS, OUT), BF16),
            pltpu.VMEM((ROWS, WIDTH), BF16),
            pltpu.VMEM((OUT, WIDTH), BF16),
            pltpu.VMEM((ROWS, WIDTH), BF16),
            pltpu.VMEM((HEADS, ROWS, ROWS), BF16),
        ],
        micros=0,
    )
    results, collected = lax.optimization_barrier((results, collected))
    (owned,) = call(owned_kernel, "owned", (collected,), [IN_VMEM], [((2, HALF_WIDTH), F32)])
    turned = [turn(owned, "yl", step) for step in range(1, 4)]
    back = exchange(results, SEQ)
    (group,) = call(
        group_kernel, "group", (owned, *turned), [IN_VMEM] * 4, [((2, HALF_WIDTH), F32)]
    )
    (total,) = call(
        total_kernel,
        "total",
        (core, group, swap(group)),
        [IN_SMEM] + [IN_VMEM] * 2,
        [((12, WIDTH), F32)],
    )
    projected, grads = call(
        unpack_kernel,
        "unpack",
        (back,),
        [IN_VMEM],
        [((ROWS, OUT), BF16), ((3, ROWS, WIDTH), BF16)],
        [pltpu.VMEM((ROWS, BASE), BF16), pltpu.SemaphoreType.DMA((4,))],
        out_spec=IN_HBM,
    )
    return (
        projected.reshape(1, 1, ROWS, OUT),
        grads.reshape(3, 1, 1, ROWS, WIDTH),
        total,
    )


def solution(mesh):
    split = Mesh(mesh.devices.reshape(4, 2, 2, 4, 8), ("yl", "c", "yh", "x", "z"))
    in_specs = (P(None, GROUPS, SEQ, None, None), P(SEQ, None), P(GROUPS, SEQ, None, None))
    out_specs = (P(GROUPS, SEQ, None, None), P(None, GROUPS, SEQ, None, None), P(SEQ, None))
    return jax.shard_map(
        on_device, mesh=split, in_specs=in_specs, out_specs=out_specs, check_vma=False
    )
```

```python
import math

import jax
import jax.numpy as jnp
from jax import lax
from jax.experimental import pallas as pl
from jax.experimental.pallas import tpu as pltpu
from jax.sharding import Mesh
from jax.sharding import PartitionSpec as P

HEADS = 16
HEAD_DIM = 72
ROWS = 128
LANES = 128
WIDTH = 1152
TILES = WIDTH // LANES
OUT = 768
HALF = OUT // 2
BASE = 3 * WIDTH + OUT
PIECE = 896
PIECE_TILES = PIECE // LANES
COLS = BASE + PIECE
HALF_WIDTH = 3 * WIDTH
INV_ROOT = 1.0 / math.sqrt(HEAD_DIM)
GRAD_SCALE = 1.0 / math.sqrt(512 * ROWS)
BF16 = jnp.bfloat16
F32 = jnp.float32

SEQ = ("yh", "x", "z")
GROUPS = ("yl", "c")


def dot(lhs, rhs, lhs_dim, rhs_dim):
    return lax.dot_general(
        lhs, rhs, (((lhs_dim,), (rhs_dim,)), ((), ())), preferred_element_type=F32
    )


def lanes(tile, base=0):
    return slice(base + tile * LANES, base + (tile + 1) * LANES)


def only_head(index, start, value):
    feature = lax.broadcasted_iota(jnp.int32, value.shape, 1) + start
    inside = (feature >= index * HEAD_DIM) & (feature < (index + 1) * HEAD_DIM)
    return jnp.where(inside, value, jnp.zeros_like(value))


def head_lanes(index):
    first = index * HEAD_DIM // LANES
    last = ((index + 1) * HEAD_DIM - 1) // LANES + 1
    return first * LANES, last * LANES


def head_products(lhs_ref, lhs_base, rhs_ref, rhs_base, index):
    start, stop = head_lanes(index)
    rhs = only_head(index, start, rhs_ref[:, rhs_base + start : rhs_base + stop])
    return dot(lhs_ref[:, lhs_base + start : lhs_base + stop], rhs, 1, 1)


def tile_heads(tile):
    return [
        index
        for index in range(HEADS)
        if index * HEAD_DIM < (tile + 1) * LANES and (index + 1) * HEAD_DIM > tile * LANES
    ]


def stacked_heads(ref, base, tile):
    value = ref[:, lanes(tile, base)]
    return jnp.concatenate(
        [only_head(index, tile * LANES, value) for index in tile_heads(tile)], axis=0
    )


def channel_order():
    natural = lax.broadcasted_iota(jnp.int32, (OUT, OUT), 0)
    place = lax.broadcasted_iota(jnp.int32, (OUT, OUT), 1)
    source = 12 * ((place & 127) >> 1) + 2 * (place >> 7) + (place & 1)
    return jnp.where(natural == source, 1.0, 0.0).astype(BF16)


def half_tiles():
    return [
        (tile // PIECE_TILES, tile % PIECE_TILES, tile // TILES, tile % TILES)
        for tile in range(3 * TILES)
    ]


def pack_kernel(
    core_ref, parts_hbm, cotangent_hbm, weight_hbm, out_ref, parts, cotangent, weight, sems
):
    pairs = [(parts_hbm.at[part], parts.at[part]) for part in range(3)]
    pairs += [(cotangent_hbm, cotangent), (weight_hbm, weight)]
    copies = [
        pltpu.make_async_copy(source, target, sems.at[place])
        for place, (source, target) in enumerate(pairs)
    ]
    for copy in copies:
        copy.start()
    row = lax.broadcasted_iota(jnp.int32, (ROWS, 12), 0)
    col = lax.broadcasted_iota(jnp.int32, (ROWS, 12), 1)
    copies[4].wait()
    repeated = []
    for pair in range(3):
        chosen = col == 6 * core_ref[0] + 2 * pair + (row & 1)
        repeated.append(
            dot(jnp.where(chosen, 1.0, 0.0).astype(BF16), weight[...], 1, 0).astype(BF16)
        )
    column = (lax.broadcasted_iota(jnp.int32, (ROWS, LANES), 0) >> 4) & 3
    for place in range(PIECE_TILES):
        value = jnp.zeros((ROWS, LANES), BF16)
        for piece, at, pair, tile in half_tiles():
            if at == place:
                value = jnp.where(column == piece, repeated[pair][:, lanes(tile)], value)
        out_ref[:, :, lanes(place, BASE)] = value.reshape(64, 2, LANES)
    for part in range(3):
        copies[part].wait()
        out_ref[:, :, part * WIDTH : (part + 1) * WIDTH] = parts[part].reshape(64, 2, WIDTH)
    copies[3].wait()
    out_ref[:, :, 3 * WIDTH : BASE] = cotangent[...].reshape(64, 2, OUT)


def attend(rows_ref, weights_ref, put):
    row = lax.broadcasted_iota(jnp.int32, (ROWS, ROWS), 0)
    col = lax.broadcasted_iota(jnp.int32, (ROWS, ROWS), 1)
    bias = jnp.where(((row ^ col) & 1) == 0, 0.0, -1e30)
    for index in range(HEADS):
        weights_ref[index] = head_products(rows_ref, 0, rows_ref, WIDTH, index)
    for index in range(HEADS):
        scores = weights_ref[index] * INV_ROOT + bias
        powers = jnp.exp(scores - jnp.max(scores, axis=1, keepdims=True))
        weights_ref[index] = powers * (1.0 / jnp.sum(powers, axis=1, keepdims=True))
    for tile in range(TILES):
        rounded = [weights_ref[index].astype(BF16) for index in tile_heads(tile)]
        values = stacked_heads(rows_ref, 2 * WIDTH, tile)
        put(tile, dot(jnp.concatenate(rounded, axis=1), values, 1, 0).astype(BF16))


def ordered_channels(rows_ref):
    return dot(rows_ref[:, 3 * WIDTH : BASE], channel_order(), 1, 0).astype(BF16)


def forward_kernel(core_ref, sent_ref, share_ref, columns_ref, rows_ref, weights_ref, channels_ref):
    rows_ref[...] = sent_ref[...].reshape(ROWS, COLS)
    channels_ref[...] = ordered_channels(rows_ref)

    def put(tile, value):
        share_ref[:, lanes(tile)] = value

    attend(rows_ref, weights_ref, put)
    own = pl.multiple_of(core_ref[0] * HALF, HALF)
    other = pl.multiple_of((1 - core_ref[0]) * HALF, HALF)
    columns_ref[...] = channels_ref[:, pl.ds(own, HALF)]
    share_ref[:, WIDTH:] = channels_ref[:, pl.ds(other, HALF)]


def weight_grad_kernel(share_ref, received_ref, columns_ref, out_ref):
    columns = jnp.concatenate([columns_ref[...], received_ref[:, WIDTH:]], axis=0)
    features = jnp.concatenate([share_ref[:, :WIDTH], received_ref[:, :WIDTH]], axis=0)
    partial = dot(columns, features, 0, 0).astype(BF16)
    for high in range(2):
        for pair in range(3):
            start, column = pair * ROWS + high * 64, high * HALF_WIDTH + pair * WIDTH
            out_ref[:, :, column : column + WIDTH] = partial[start : start + 64].reshape(
                32, 2, WIDTH
            )


def backward_kernel(
    core_ref, x_ref, sent_ref, mine_ref, theirs_ref,
    out_ref, rows_ref, weights_ref, channels_ref, attended_ref, matrix_ref, upstream_ref,
    grad_scores_ref,
):
    rows_ref[...] = sent_ref[...].reshape(ROWS, COLS)
    channels_ref[...] = ordered_channels(rows_ref)

    def put_attended(tile, value):
        attended_ref[:, lanes(tile)] = value

    attend(rows_ref, weights_ref, put_attended)
    own = pl.multiple_of(core_ref[0] * HALF, HALF)
    other = pl.multiple_of((1 - core_ref[0]) * HALF, HALF)
    for here in range(4):

        @pl.when(x_ref[0] == here)
        def _():
            for piece, place, pair, tile in half_tiles():
                for start, half_ref in ((own, mine_ref), (other, theirs_ref)):
                    matrix_ref[pl.ds(start + pair * ROWS, ROWS), lanes(tile)] = half_ref[
                        (here - piece) & 3, :, lanes(place)
                    ]

    upstream_ref[...] = dot(channels_ref[...], matrix_ref[...], 1, 0).astype(BF16)
    products = [
        head_products(upstream_ref, 0, rows_ref, 2 * WIDTH, index) for index in range(HEADS)
    ]
    for index in range(HEADS):
        weights, grad_weights = weights_ref[index], products[index]
        centred = grad_weights - jnp.sum(weights * grad_weights, axis=1, keepdims=True)
        grad_scores_ref[index] = (weights * centred * INV_ROOT).astype(BF16)

    def put(start, value):
        out_ref[:, :, start : start + value.shape[1]] = value.astype(BF16).reshape(64, 2, -1)

    projected = dot(attended_ref[...], matrix_ref[...], 1, 1).astype(BF16)
    put(3 * WIDTH, dot(projected, channel_order(), 1, 1))
    for tile in range(TILES):
        heads = tile_heads(tile)
        grad_scores = [grad_scores_ref[index] for index in heads]
        rounded = [weights_ref[index].astype(BF16) for index in heads]
        across, down = jnp.concatenate(grad_scores, axis=1), jnp.concatenate(grad_scores, axis=0)
        put(tile * LANES, dot(across, stacked_heads(rows_ref, WIDTH, tile), 1, 0))
        put(WIDTH + tile * LANES, dot(down, stacked_heads(rows_ref, 0, tile), 0, 0))
        put(
            2 * WIDTH + tile * LANES,
            dot(jnp.concatenate(rounded, axis=0), stacked_heads(upstream_ref, 0, tile), 0, 0),
        )


def owned_kernel(terms_ref, out_ref):
    rows = terms_ref[...].reshape(64, 2 * HALF_WIDTH)
    target = lax.broadcasted_iota(jnp.int32, (8, 64), 0)
    source = lax.broadcasted_iota(jnp.int32, (8, 64), 1)
    chosen = jnp.where(target == (source & 1), 1.0, 0.0).astype(BF16)
    out_ref[...] = dot(chosen, rows, 1, 0)[:2]


def unpack_kernel(back_ref, projected_hbm, grads_hbm, rows_ref, sems):
    rows_ref[...] = back_ref[...].reshape(ROWS, BASE)
    parts = [(rows_ref.at[:, 3 * WIDTH :], projected_hbm)]
    for part in range(3):
        parts.append((rows_ref.at[:, part * WIDTH : (part + 1) * WIDTH], grads_hbm.at[part]))
    copies = [
        pltpu.make_async_copy(source, target, sems.at[place])
        for place, (source, target) in enumerate(parts)
    ]
    for copy in copies:
        copy.start()
    for copy in copies:
        copy.wait()


def group_kernel(high_ref, *refs):
    *terms, keep_ref, send_ref = refs
    own = pl.multiple_of(high_ref[0] * HALF_WIDTH, LANES)
    other = pl.multiple_of((1 - high_ref[0]) * HALF_WIDTH, LANES)
    for start, out_ref in ((own, keep_ref), (other, send_ref)):
        total = terms[0][:, pl.ds(start, HALF_WIDTH)]
        for term in terms[1:]:
            total += term[:, pl.ds(start, HALF_WIDTH)]
        out_ref[...] = total * GRAD_SCALE


def total_kernel(core_ref, keep_ref, crossed_ref, their_keep_ref, their_crossed_ref, out_ref):
    mine = keep_ref[...] + crossed_ref[...]
    theirs = their_keep_ref[...] + their_crossed_ref[...]
    for core in range(2):
        total = jnp.where(core_ref[0] == core, mine, theirs)
        for pair in range(3):
            start = 6 * core + 2 * pair
            out_ref[start : start + 2, :] = total[:, pair * WIDTH : (pair + 1) * WIDTH]


IN_VMEM = pl.BlockSpec(memory_space=pltpu.VMEM)
IN_SMEM = pl.BlockSpec(memory_space=pltpu.SMEM)
IN_HBM = pl.BlockSpec(memory_space=pltpu.HBM)


def call(kernel, name, operands, specs, outs, scratch=(), grant=12, micros=1, out_spec=IN_VMEM):
    return pl.pallas_call(
        kernel,
        out_shape=[jax.ShapeDtypeStruct(shape, dtype) for shape, dtype in outs],
        in_specs=specs,
        out_specs=[out_spec] * len(outs),
        scratch_shapes=list(scratch),
        compiler_params=pltpu.CompilerParams(vmem_limit_bytes=grant << 20),
        cost_estimate=pl.CostEstimate(
            flops=micros * 10**9, bytes_accessed=micros * 3 * 10**6, transcendentals=0
        ),
        name=name,
    )(*operands)


def exchange(value, axes):
    return lax.all_to_all(value, axes, 0, 0, tiled=True)


def swap(value):
    return lax.ppermute(value, "c", [(0, 1), (1, 0)])


def turn(value, axis, step):
    return lax.ppermute(value, axis, [(place, (place + step) % 4) for place in range(4)])


def on_device(query_key_value, out_weight, cotangent):
    core = lax.axis_index("c").astype(jnp.int32).reshape(1)
    x_place = lax.axis_index("x").astype(jnp.int32).reshape(1)
    y_high = lax.axis_index("yh").astype(jnp.int32).reshape(1)
    (packed,) = call(
        pack_kernel,
        "pack",
        (core, query_key_value.reshape(3, ROWS, WIDTH), cotangent.reshape(ROWS, OUT), out_weight),
        [IN_SMEM] + [IN_HBM] * 3,
        [((64, 2, COLS), BF16)],
        [
            pltpu.VMEM((3, ROWS, WIDTH), BF16),
            pltpu.VMEM((ROWS, OUT), BF16),
            pltpu.VMEM((12, WIDTH), BF16),
            pltpu.SemaphoreType.DMA((5,)),
        ],
        grant=56,
    )
    sent = exchange(packed, SEQ)
    share, columns = call(
        forward_kernel,
        "forward",
        (core, sent),
        [IN_SMEM, IN_VMEM],
        [((ROWS, WIDTH + HALF), BF16), ((ROWS, HALF), BF16)],
        [
            pltpu.VMEM((ROWS, COLS), BF16),
            pltpu.VMEM((HEADS, ROWS, ROWS), F32),
            pltpu.VMEM((ROWS, OUT), BF16),
        ],
        micros=3,
    )
    piece = sent[:, :, BASE:].reshape(ROWS, PIECE)
    turned = [turn(piece, "x", step) for step in range(1, 4)]
    (partial,) = call(
        weight_grad_kernel,
        "weight_grad",
        (share, swap(share), columns),
        [IN_VMEM] * 3,
        [((32, 2, 2 * HALF_WIDTH), BF16)],
    )
    collected = exchange(partial, ("x", "z"))
    piece, *turned = lax.optimization_barrier((piece, *turned, partial))[:4]
    mine = jnp.stack([piece, *turned])
    (results,) = call(
        backward_kernel,
        "backward",
        (core, x_place, sent, mine, swap(mine)),
        [IN_SMEM] * 2 + [IN_VMEM] * 3,
        [((64, 2, BASE), BF16)],
        [
            pltpu.VMEM((ROWS, COLS), BF16),
            pltpu.VMEM((HEADS, ROWS, ROWS), F32),
            pltpu.VMEM((ROWS, OUT), BF16),
            pltpu.VMEM((ROWS, WIDTH), BF16),
            pltpu.VMEM((OUT, WIDTH), BF16),
            pltpu.VMEM((ROWS, WIDTH), BF16),
            pltpu.VMEM((HEADS, ROWS, ROWS), BF16),
        ],
        micros=7,
    )
    results, collected = lax.optimization_barrier((results, collected))
    back = exchange(results, SEQ)
    (owned,) = call(
        owned_kernel, "owned", (collected,), [IN_VMEM], [((2, 2 * HALF_WIDTH), F32)]
    )
    turned = [turn(owned, "yl", step) for step in range(1, 4)]
    keep, send = call(
        group_kernel,
        "group",
        (y_high, owned, *turned),
        [IN_SMEM] + [IN_VMEM] * 4,
        [((2, HALF_WIDTH), F32)] * 2,
    )
    crossed = lax.ppermute(send, "yh", [(0, 1), (1, 0)])
    both = lax.ppermute(send, ("c", "yh"), [(place, 3 - place) for place in range(4)])
    (total,) = call(
        total_kernel,
        "total",
        (core, keep, crossed, swap(keep), both),
        [IN_SMEM] + [IN_VMEM] * 4,
        [((12, WIDTH), F32)],
    )
    projected, grads = call(
        unpack_kernel,
        "unpack",
        (back,),
        [IN_VMEM],
        [((ROWS, OUT), BF16), ((3, ROWS, WIDTH), BF16)],
        [pltpu.VMEM((ROWS, BASE), BF16), pltpu.SemaphoreType.DMA((4,))],
        out_spec=IN_HBM,
    )
    return (
        projected.reshape(1, 1, ROWS, OUT),
        grads.reshape(3, 1, 1, ROWS, WIDTH),
        total,
    )


def solution(mesh):
    split = Mesh(mesh.devices.reshape(4, 2, 2, 4, 8), ("yl", "c", "yh", "x", "z"))
    in_specs = (P(None, GROUPS, SEQ, None, None), P(SEQ, None), P(GROUPS, SEQ, None, None))
    out_specs = (P(GROUPS, SEQ, None, None), P(None, GROUPS, SEQ, None, None), P(SEQ, None))
    return jax.shard_map(
        on_device, mesh=split, in_specs=in_specs, out_specs=out_specs, check_vma=False
    )
```

```python
import math

import jax
import jax.numpy as jnp
from jax import lax
from jax.experimental import pallas as pl
from jax.experimental.pallas import tpu as pltpu
from jax.sharding import Mesh
from jax.sharding import PartitionSpec as P

HEADS = 16
HEAD_DIM = 72
ROWS = 128
LANES = 128
WIDTH = 1152
TILES = WIDTH // LANES
OUT = 768
HALF = OUT // 2
BASE = 3 * WIDTH + OUT
PIECE = 896
PIECE_TILES = PIECE // LANES
COLS = BASE + PIECE
HALF_WIDTH = 3 * WIDTH
INV_ROOT = 1.0 / math.sqrt(HEAD_DIM)
GRAD_SCALE = 1.0 / math.sqrt(512 * ROWS)
BF16 = jnp.bfloat16
F32 = jnp.float32

SEQ = ("yh", "x", "z")
GROUPS = ("yl", "c")


def dot(lhs, rhs, lhs_dim, rhs_dim):
    return lax.dot_general(
        lhs, rhs, (((lhs_dim,), (rhs_dim,)), ((), ())), preferred_element_type=F32
    )


def lanes(tile, base=0):
    return slice(base + tile * LANES, base + (tile + 1) * LANES)


def only_head(index, start, value):
    feature = lax.broadcasted_iota(jnp.int32, value.shape, 1) + start
    inside = (feature >= index * HEAD_DIM) & (feature < (index + 1) * HEAD_DIM)
    return jnp.where(inside, value, jnp.zeros_like(value))


def head_lanes(index):
    first = index * HEAD_DIM // LANES
    last = ((index + 1) * HEAD_DIM - 1) // LANES + 1
    return first * LANES, last * LANES


def head_products(lhs_ref, lhs_base, rhs_ref, rhs_base, index):
    start, stop = head_lanes(index)
    rhs = only_head(index, start, rhs_ref[:, rhs_base + start : rhs_base + stop])
    return dot(lhs_ref[:, lhs_base + start : lhs_base + stop], rhs, 1, 1)


def tile_heads(tile):
    return [
        index
        for index in range(HEADS)
        if index * HEAD_DIM < (tile + 1) * LANES and (index + 1) * HEAD_DIM > tile * LANES
    ]


def stacked_heads(ref, base, tile):
    value = ref[:, lanes(tile, base)]
    return jnp.concatenate(
        [only_head(index, tile * LANES, value) for index in tile_heads(tile)], axis=0
    )


def channel_order():
    natural = lax.broadcasted_iota(jnp.int32, (OUT, OUT), 0)
    place = lax.broadcasted_iota(jnp.int32, (OUT, OUT), 1)
    source = 12 * ((place & 127) >> 1) + 2 * (place >> 7) + (place & 1)
    return jnp.where(natural == source, 1.0, 0.0).astype(BF16)


def half_tiles():
    return [
        (tile // PIECE_TILES, tile % PIECE_TILES, tile // TILES, tile % TILES)
        for tile in range(3 * TILES)
    ]


def pack_kernel(
    core_ref, parts_hbm, cotangent_hbm, weight_hbm, out_ref, parts, cotangent, weight, sems
):
    pairs = [(weight_hbm, weight)]
    pairs += [(parts_hbm.at[part], parts.at[part]) for part in range(3)]
    pairs += [(cotangent_hbm, cotangent)]
    copies = [
        pltpu.make_async_copy(source, target, sems.at[place])
        for place, (source, target) in enumerate(pairs)
    ]
    for copy in copies:
        copy.start()
    row = lax.broadcasted_iota(jnp.int32, (ROWS, 12), 0)
    col = lax.broadcasted_iota(jnp.int32, (ROWS, 12), 1)
    copies[0].wait()
    repeated = []
    for pair in range(3):
        chosen = col == 6 * core_ref[0] + 2 * pair + (row & 1)
        repeated.append(
            dot(jnp.where(chosen, 1.0, 0.0).astype(BF16), weight[...], 1, 0).astype(BF16)
        )
    column = (lax.broadcasted_iota(jnp.int32, (ROWS, LANES), 0) >> 4) & 3
    for place in range(PIECE_TILES):
        value = jnp.zeros((ROWS, LANES), BF16)
        for piece, at, pair, tile in half_tiles():
            if at == place:
                value = jnp.where(column == piece, repeated[pair][:, lanes(tile)], value)
        out_ref[:, :, lanes(place, BASE)] = value.reshape(64, 2, LANES)
    for part in range(3):
        copies[1 + part].wait()
        out_ref[:, :, part * WIDTH : (part + 1) * WIDTH] = parts[part].reshape(64, 2, WIDTH)
    copies[4].wait()
    out_ref[:, :, 3 * WIDTH : BASE] = cotangent[...].reshape(64, 2, OUT)


def attend(rows_ref, weights_ref, put):
    row = lax.broadcasted_iota(jnp.int32, (ROWS, ROWS), 0)
    col = lax.broadcasted_iota(jnp.int32, (ROWS, ROWS), 1)
    bias = jnp.where(((row ^ col) & 1) == 0, 0.0, -1e30)
    for index in range(HEADS):
        weights_ref[index] = head_products(rows_ref, 0, rows_ref, WIDTH, index)
    for index in range(HEADS):
        scores = weights_ref[index] * INV_ROOT + bias
        powers = jnp.exp(scores - jnp.max(scores, axis=1, keepdims=True))
        weights_ref[index] = powers * (1.0 / jnp.sum(powers, axis=1, keepdims=True))
    for tile in range(TILES):
        rounded = [weights_ref[index].astype(BF16) for index in tile_heads(tile)]
        values = stacked_heads(rows_ref, 2 * WIDTH, tile)
        put(tile, dot(jnp.concatenate(rounded, axis=1), values, 1, 0).astype(BF16))


def ordered_channels(rows_ref):
    return dot(rows_ref[:, 3 * WIDTH : BASE], channel_order(), 1, 0).astype(BF16)


def forward_kernel(core_ref, sent_ref, share_ref, columns_ref, rows_ref, weights_ref, channels_ref):
    rows_ref[...] = sent_ref[...].reshape(ROWS, COLS)
    channels_ref[...] = ordered_channels(rows_ref)

    def put(tile, value):
        share_ref[:, lanes(tile)] = value

    attend(rows_ref, weights_ref, put)
    own = pl.multiple_of(core_ref[0] * HALF, HALF)
    other = pl.multiple_of((1 - core_ref[0]) * HALF, HALF)
    columns_ref[...] = channels_ref[:, pl.ds(own, HALF)]
    share_ref[:, WIDTH:] = channels_ref[:, pl.ds(other, HALF)]


def weight_grad_kernel(share_ref, received_ref, columns_ref, out_ref):
    columns = jnp.concatenate([columns_ref[...], received_ref[:, WIDTH:]], axis=0)
    features = jnp.concatenate([share_ref[:, :WIDTH], received_ref[:, :WIDTH]], axis=0)
    partial = dot(columns, features, 0, 0).astype(BF16)
    for pair in range(3):
        out_ref[:, :, pair * WIDTH : (pair + 1) * WIDTH] = partial[
            pair * ROWS : (pair + 1) * ROWS
        ].reshape(64, 2, WIDTH)


def backward_kernel(
    core_ref, x_ref, sent_ref, mine_ref, theirs_ref,
    out_ref, rows_ref, weights_ref, channels_ref, attended_ref, matrix_ref, upstream_ref,
    grad_scores_ref,
):
    rows_ref[...] = sent_ref[...].reshape(ROWS, COLS)
    channels_ref[...] = ordered_channels(rows_ref)

    def put_attended(tile, value):
        attended_ref[:, lanes(tile)] = value

    attend(rows_ref, weights_ref, put_attended)
    own = pl.multiple_of(core_ref[0] * HALF, HALF)
    other = pl.multiple_of((1 - core_ref[0]) * HALF, HALF)
    for here in range(4):

        @pl.when(x_ref[0] == here)
        def _():
            for piece, place, pair, tile in half_tiles():
                for start, half_ref in ((own, mine_ref), (other, theirs_ref)):
                    matrix_ref[pl.ds(start + pair * ROWS, ROWS), lanes(tile)] = half_ref[
                        (here - piece) & 3, :, lanes(place)
                    ]

    upstream_ref[...] = dot(channels_ref[...], matrix_ref[...], 1, 0).astype(BF16)
    products = [
        head_products(upstream_ref, 0, rows_ref, 2 * WIDTH, index) for index in range(HEADS)
    ]
    for index in range(HEADS):
        weights, grad_weights = weights_ref[index], products[index]
        centred = grad_weights - jnp.sum(weights * grad_weights, axis=1, keepdims=True)
        grad_scores_ref[index] = (weights * centred * INV_ROOT).astype(BF16)

    def put(start, value):
        out_ref[:, :, start : start + value.shape[1]] = value.astype(BF16).reshape(64, 2, -1)

    projected = dot(attended_ref[...], matrix_ref[...], 1, 1).astype(BF16)
    put(3 * WIDTH, dot(projected, channel_order(), 1, 1))
    for tile in range(TILES):
        heads = tile_heads(tile)
        grad_scores = [grad_scores_ref[index] for index in heads]
        rounded = [weights_ref[index].astype(BF16) for index in heads]
        across, down = jnp.concatenate(grad_scores, axis=1), jnp.concatenate(grad_scores, axis=0)
        put(tile * LANES, dot(across, stacked_heads(rows_ref, WIDTH, tile), 1, 0))
        put(WIDTH + tile * LANES, dot(down, stacked_heads(rows_ref, 0, tile), 0, 0))
        put(
            2 * WIDTH + tile * LANES,
            dot(jnp.concatenate(rounded, axis=0), stacked_heads(upstream_ref, 0, tile), 0, 0),
        )


def owned_kernel(terms_ref, out_ref):
    rows = terms_ref[...].reshape(ROWS, HALF_WIDTH)
    target = lax.broadcasted_iota(jnp.int32, (8, ROWS), 0)
    source = lax.broadcasted_iota(jnp.int32, (8, ROWS), 1)
    chosen = jnp.where(target == (source & 1), 1.0, 0.0).astype(BF16)
    out_ref[...] = dot(chosen, rows, 1, 0)[:2]


def unpack_kernel(back_ref, projected_hbm, grads_hbm, rows_ref, sems):
    rows_ref[...] = back_ref[...].reshape(ROWS, BASE)
    parts = [(rows_ref.at[:, 3 * WIDTH :], projected_hbm)]
    for part in range(3):
        parts.append((rows_ref.at[:, part * WIDTH : (part + 1) * WIDTH], grads_hbm.at[part]))
    copies = [
        pltpu.make_async_copy(source, target, sems.at[place])
        for place, (source, target) in enumerate(parts)
    ]
    for copy in copies:
        copy.start()
    for copy in copies:
        copy.wait()


def group_kernel(*refs):
    *terms, out_ref = refs
    total = terms[0][...]
    for term in terms[1:]:
        total += term[...]
    out_ref[...] = total * GRAD_SCALE


def total_kernel(core_ref, mine_ref, theirs_ref, out_ref):
    for core in range(2):
        total = jnp.where(core_ref[0] == core, mine_ref[...], theirs_ref[...])
        for pair in range(3):
            start = 6 * core + 2 * pair
            out_ref[start : start + 2, :] = total[:, pair * WIDTH : (pair + 1) * WIDTH]


IN_VMEM = pl.BlockSpec(memory_space=pltpu.VMEM)
IN_SMEM = pl.BlockSpec(memory_space=pltpu.SMEM)
IN_HBM = pl.BlockSpec(memory_space=pltpu.HBM)


def call(kernel, name, operands, specs, outs, scratch=(), grant=12, micros=1, out_spec=IN_VMEM):
    return pl.pallas_call(
        kernel,
        out_shape=[jax.ShapeDtypeStruct(shape, dtype) for shape, dtype in outs],
        in_specs=specs,
        out_specs=[out_spec] * len(outs),
        scratch_shapes=list(scratch),
        compiler_params=pltpu.CompilerParams(vmem_limit_bytes=grant << 20),
        cost_estimate=pl.CostEstimate(
            flops=micros * 10**9, bytes_accessed=micros * 3 * 10**6, transcendentals=0
        ),
        name=name,
    )(*operands)


def exchange(value, axes):
    return lax.all_to_all(value, axes, 0, 0, tiled=True)


def swap(value):
    return lax.ppermute(value, "c", [(0, 1), (1, 0)])


def turn(value, axis, step):
    return lax.ppermute(value, axis, [(place, (place + step) % 4) for place in range(4)])


def on_device(query_key_value, out_weight, cotangent):
    core = lax.axis_index("c").astype(jnp.int32).reshape(1)
    x_place = lax.axis_index("x").astype(jnp.int32).reshape(1)
    (packed,) = call(
        pack_kernel,
        "pack",
        (core, query_key_value.reshape(3, ROWS, WIDTH), cotangent.reshape(ROWS, OUT), out_weight),
        [IN_SMEM] + [IN_HBM] * 3,
        [((64, 2, COLS), BF16)],
        [
            pltpu.VMEM((3, ROWS, WIDTH), BF16),
            pltpu.VMEM((ROWS, OUT), BF16),
            pltpu.VMEM((12, WIDTH), BF16),
            pltpu.SemaphoreType.DMA((5,)),
        ],
        grant=56,
    )
    sent = exchange(packed, SEQ)
    share, columns = call(
        forward_kernel,
        "forward",
        (core, sent),
        [IN_SMEM, IN_VMEM],
        [((ROWS, WIDTH + HALF), BF16), ((ROWS, HALF), BF16)],
        [
            pltpu.VMEM((ROWS, COLS), BF16),
            pltpu.VMEM((HEADS, ROWS, ROWS), F32),
            pltpu.VMEM((ROWS, OUT), BF16),
        ],
        micros=3,
    )
    piece = sent[:, :, BASE:].reshape(ROWS, PIECE)
    turned = [turn(piece, "x", step) for step in range(1, 4)]
    (partial,) = call(
        weight_grad_kernel,
        "weight_grad",
        (share, swap(share), columns),
        [IN_VMEM] * 3,
        [((64, 2, HALF_WIDTH), BF16)],
    )
    collected = exchange(partial, SEQ)
    piece, *turned = lax.optimization_barrier((piece, *turned, partial))[:4]
    mine = jnp.stack([piece, *turned])
    (results,) = call(
        backward_kernel,
        "backward",
        (core, x_place, sent, mine, swap(mine)),
        [IN_SMEM] * 2 + [IN_VMEM] * 3,
        [((64, 2, BASE), BF16)],
        [
            pltpu.VMEM((ROWS, COLS), BF16),
            pltpu.VMEM((HEADS, ROWS, ROWS), F32),
            pltpu.VMEM((ROWS, OUT), BF16),
            pltpu.VMEM((ROWS, WIDTH), BF16),
            pltpu.VMEM((OUT, WIDTH), BF16),
            pltpu.VMEM((ROWS, WIDTH), BF16),
            pltpu.VMEM((HEADS, ROWS, ROWS), BF16),
        ],
        micros=7,
    )
    results, collected = lax.optimization_barrier((results, collected))
    (owned,) = call(owned_kernel, "owned", (collected,), [IN_VMEM], [((2, HALF_WIDTH), F32)])
    turned = [turn(owned, "yl", step) for step in range(1, 4)]
    back = exchange(results, SEQ)
    (group,) = call(
        group_kernel, "group", (owned, *turned), [IN_VMEM] * 4, [((2, HALF_WIDTH), F32)]
    )
    (total,) = call(
        total_kernel,
        "total",
        (core, group, swap(group)),
        [IN_SMEM] + [IN_VMEM] * 2,
        [((12, WIDTH), F32)],
    )
    projected, grads = call(
        unpack_kernel,
        "unpack",
        (back,),
        [IN_VMEM],
        [((ROWS, OUT), BF16), ((3, ROWS, WIDTH), BF16)],
        [pltpu.VMEM((ROWS, BASE), BF16), pltpu.SemaphoreType.DMA((4,))],
        out_spec=IN_HBM,
    )
    return (
        projected.reshape(1, 1, ROWS, OUT),
        grads.reshape(3, 1, 1, ROWS, WIDTH),
        total,
    )


def solution(mesh):
    split = Mesh(mesh.devices.reshape(4, 2, 2, 4, 8), ("yl", "c", "yh", "x", "z"))
    in_specs = (P(None, GROUPS, SEQ, None, None), P(SEQ, None), P(GROUPS, SEQ, None, None))
    out_specs = (P(GROUPS, SEQ, None, None), P(None, GROUPS, SEQ, None, None), P(SEQ, None))
    return jax.shard_map(
        on_device, mesh=split, in_specs=in_specs, out_specs=out_specs, check_vma=False
    )
```

```python
import math

import jax
import jax.numpy as jnp
from jax import lax
from jax.experimental import pallas as pl
from jax.experimental.pallas import tpu as pltpu
from jax.sharding import Mesh
from jax.sharding import PartitionSpec as P

HEADS = 16
HEAD_DIM = 72
ROWS = 128
LANES = 128
WIDTH = 1152
TILES = WIDTH // LANES
OUT = 768
HALF = OUT // 2
BASE = 3 * WIDTH + OUT
PIECE = 896
PIECE_TILES = PIECE // LANES
COLS = BASE + PIECE
HALF_WIDTH = 3 * WIDTH
INV_ROOT = 1.0 / math.sqrt(HEAD_DIM)
GRAD_SCALE = 1.0 / math.sqrt(512 * ROWS)
BF16 = jnp.bfloat16
F32 = jnp.float32

SEQ = ("yh", "x", "z")
GROUPS = ("yl", "c")


def dot(lhs, rhs, lhs_dim, rhs_dim):
    return lax.dot_general(
        lhs, rhs, (((lhs_dim,), (rhs_dim,)), ((), ())), preferred_element_type=F32
    )


def lanes(tile, base=0):
    return slice(base + tile * LANES, base + (tile + 1) * LANES)


def only_head(index, start, value):
    feature = lax.broadcasted_iota(jnp.int32, value.shape, 1) + start
    inside = (feature >= index * HEAD_DIM) & (feature < (index + 1) * HEAD_DIM)
    return jnp.where(inside, value, jnp.zeros_like(value))


def head_lanes(index):
    first = index * HEAD_DIM // LANES
    last = ((index + 1) * HEAD_DIM - 1) // LANES + 1
    return first * LANES, last * LANES


def head_products(lhs_ref, lhs_base, rhs_ref, rhs_base, index):
    start, stop = head_lanes(index)
    rhs = only_head(index, start, rhs_ref[:, rhs_base + start : rhs_base + stop])
    return dot(lhs_ref[:, lhs_base + start : lhs_base + stop], rhs, 1, 1)


def tile_heads(tile):
    return [
        index
        for index in range(HEADS)
        if index * HEAD_DIM < (tile + 1) * LANES and (index + 1) * HEAD_DIM > tile * LANES
    ]


def stacked_heads(ref, base, tile):
    value = ref[:, lanes(tile, base)]
    return jnp.concatenate(
        [only_head(index, tile * LANES, value) for index in tile_heads(tile)], axis=0
    )


def channel_order():
    natural = lax.broadcasted_iota(jnp.int32, (OUT, OUT), 0)
    place = lax.broadcasted_iota(jnp.int32, (OUT, OUT), 1)
    source = 12 * ((place & 127) >> 1) + 2 * (place >> 7) + (place & 1)
    return jnp.where(natural == source, 1.0, 0.0).astype(BF16)


def half_tiles():
    return [
        (tile // PIECE_TILES, tile % PIECE_TILES, tile // TILES, tile % TILES)
        for tile in range(3 * TILES)
    ]


def pack_kernel(
    core_ref, parts_hbm, cotangent_hbm, weight_ref, out_ref, parts, cotangent, sems
):
    pairs = [(parts_hbm.at[part], parts.at[part]) for part in range(3)]
    pairs += [(cotangent_hbm, cotangent)]
    copies = [
        pltpu.make_async_copy(source, target, sems.at[place])
        for place, (source, target) in enumerate(pairs)
    ]
    for copy in copies:
        copy.start()
    row = lax.broadcasted_iota(jnp.int32, (ROWS, 12), 0)
    col = lax.broadcasted_iota(jnp.int32, (ROWS, 12), 1)
    repeated = []
    for pair in range(3):
        chosen = col == 6 * core_ref[0] + 2 * pair + (row & 1)
        repeated.append(
            dot(jnp.where(chosen, 1.0, 0.0).astype(BF16), weight_ref[...], 1, 0).astype(BF16)
        )
    column = (lax.broadcasted_iota(jnp.int32, (ROWS, LANES), 0) >> 4) & 3
    for place in range(PIECE_TILES):
        value = jnp.zeros((ROWS, LANES), BF16)
        for piece, at, pair, tile in half_tiles():
            if at == place:
                value = jnp.where(column == piece, repeated[pair][:, lanes(tile)], value)
        out_ref[:, :, lanes(place, BASE)] = value.reshape(64, 2, LANES)
    for part in range(3):
        copies[part].wait()
        out_ref[:, :, part * WIDTH : (part + 1) * WIDTH] = parts[part].reshape(64, 2, WIDTH)
    copies[3].wait()
    out_ref[:, :, 3 * WIDTH : BASE] = cotangent[...].reshape(64, 2, OUT)


def attend(rows_ref, weights_ref, put):
    row = lax.broadcasted_iota(jnp.int32, (ROWS, ROWS), 0)
    col = lax.broadcasted_iota(jnp.int32, (ROWS, ROWS), 1)
    bias = jnp.where(((row ^ col) & 1) == 0, 0.0, -1e30)
    for index in range(HEADS):
        weights_ref[index] = head_products(rows_ref, 0, rows_ref, WIDTH, index)
    for index in range(HEADS):
        scores = weights_ref[index] * INV_ROOT + bias
        powers = jnp.exp(scores - jnp.max(scores, axis=1, keepdims=True))
        weights_ref[index] = powers * (1.0 / jnp.sum(powers, axis=1, keepdims=True))
    for tile in range(TILES):
        rounded = [weights_ref[index].astype(BF16) for index in tile_heads(tile)]
        values = stacked_heads(rows_ref, 2 * WIDTH, tile)
        put(tile, dot(jnp.concatenate(rounded, axis=1), values, 1, 0).astype(BF16))


def ordered_channels(rows_ref):
    return dot(rows_ref[:, 3 * WIDTH : BASE], channel_order(), 1, 0).astype(BF16)


def forward_kernel(core_ref, sent_ref, share_ref, columns_ref, rows_ref, weights_ref, channels_ref):
    rows_ref[...] = sent_ref[...].reshape(ROWS, COLS)
    channels_ref[...] = ordered_channels(rows_ref)

    def put(tile, value):
        share_ref[:, lanes(tile)] = value

    attend(rows_ref, weights_ref, put)
    own = pl.multiple_of(core_ref[0] * HALF, HALF)
    other = pl.multiple_of((1 - core_ref[0]) * HALF, HALF)
    columns_ref[...] = channels_ref[:, pl.ds(own, HALF)]
    share_ref[:, WIDTH:] = channels_ref[:, pl.ds(other, HALF)]


def weight_grad_kernel(share_ref, received_ref, columns_ref, out_ref):
    columns = jnp.concatenate([columns_ref[...], received_ref[:, WIDTH:]], axis=0)
    features = jnp.concatenate([share_ref[:, :WIDTH], received_ref[:, :WIDTH]], axis=0)
    partial = dot(columns, features, 0, 0).astype(BF16)
    for pair in range(3):
        out_ref[:, :, pair * WIDTH : (pair + 1) * WIDTH] = partial[
            pair * ROWS : (pair + 1) * ROWS
        ].reshape(64, 2, WIDTH)


def backward_kernel(
    core_ref, x_ref, sent_ref, mine_ref, theirs_ref,
    out_ref, rows_ref, weights_ref, channels_ref, attended_ref, matrix_ref, upstream_ref,
    grad_scores_ref,
):
    rows_ref[...] = sent_ref[...].reshape(ROWS, COLS)
    channels_ref[...] = ordered_channels(rows_ref)

    def put_attended(tile, value):
        attended_ref[:, lanes(tile)] = value

    attend(rows_ref, weights_ref, put_attended)
    own = pl.multiple_of(core_ref[0] * HALF, HALF)
    other = pl.multiple_of((1 - core_ref[0]) * HALF, HALF)
    for here in range(4):

        @pl.when(x_ref[0] == here)
        def _():
            for piece, place, pair, tile in half_tiles():
                for start, half_ref in ((own, mine_ref), (other, theirs_ref)):
                    matrix_ref[pl.ds(start + pair * ROWS, ROWS), lanes(tile)] = half_ref[
                        (here - piece) & 3, :, lanes(place)
                    ]

    upstream_ref[...] = dot(channels_ref[...], matrix_ref[...], 1, 0).astype(BF16)
    products = [
        head_products(upstream_ref, 0, rows_ref, 2 * WIDTH, index) for index in range(HEADS)
    ]
    for index in range(HEADS):
        weights, grad_weights = weights_ref[index], products[index]
        centred = grad_weights - jnp.sum(weights * grad_weights, axis=1, keepdims=True)
        grad_scores_ref[index] = (weights * centred * INV_ROOT).astype(BF16)

    def put(start, value):
        out_ref[:, :, start : start + value.shape[1]] = value.astype(BF16).reshape(64, 2, -1)

    projected = dot(attended_ref[...], matrix_ref[...], 1, 1).astype(BF16)
    put(3 * WIDTH, dot(projected, channel_order(), 1, 1))
    for tile in range(TILES):
        heads = tile_heads(tile)
        grad_scores = [grad_scores_ref[index] for index in heads]
        rounded = [weights_ref[index].astype(BF16) for index in heads]
        across, down = jnp.concatenate(grad_scores, axis=1), jnp.concatenate(grad_scores, axis=0)
        put(tile * LANES, dot(across, stacked_heads(rows_ref, WIDTH, tile), 1, 0))
        put(WIDTH + tile * LANES, dot(down, stacked_heads(rows_ref, 0, tile), 0, 0))
        put(
            2 * WIDTH + tile * LANES,
            dot(jnp.concatenate(rounded, axis=0), stacked_heads(upstream_ref, 0, tile), 0, 0),
        )


def owned_kernel(terms_ref, out_ref):
    rows = terms_ref[...].reshape(ROWS, HALF_WIDTH)
    target = lax.broadcasted_iota(jnp.int32, (8, ROWS), 0)
    source = lax.broadcasted_iota(jnp.int32, (8, ROWS), 1)
    chosen = jnp.where(target == (source & 1), 1.0, 0.0).astype(BF16)
    out_ref[...] = dot(chosen, rows, 1, 0)[:2]


def unpack_kernel(back_ref, projected_hbm, grads_hbm, rows_ref, sems):
    rows_ref[...] = back_ref[...].reshape(ROWS, BASE)
    parts = [(rows_ref.at[:, 3 * WIDTH :], projected_hbm)]
    for part in range(3):
        parts.append((rows_ref.at[:, part * WIDTH : (part + 1) * WIDTH], grads_hbm.at[part]))
    copies = [
        pltpu.make_async_copy(source, target, sems.at[place])
        for place, (source, target) in enumerate(parts)
    ]
    for copy in copies:
        copy.start()
    for copy in copies:
        copy.wait()


def group_kernel(*refs):
    *terms, out_ref = refs
    total = terms[0][...]
    for term in terms[1:]:
        total += term[...]
    out_ref[...] = total * GRAD_SCALE


def total_kernel(core_ref, mine_ref, theirs_ref, out_ref):
    for core in range(2):
        total = jnp.where(core_ref[0] == core, mine_ref[...], theirs_ref[...])
        for pair in range(3):
            start = 6 * core + 2 * pair
            out_ref[start : start + 2, :] = total[:, pair * WIDTH : (pair + 1) * WIDTH]


IN_VMEM = pl.BlockSpec(memory_space=pltpu.VMEM)
IN_SMEM = pl.BlockSpec(memory_space=pltpu.SMEM)
IN_HBM = pl.BlockSpec(memory_space=pltpu.HBM)


def call(kernel, name, operands, specs, outs, scratch=(), grant=12, micros=1, out_spec=IN_VMEM):
    return pl.pallas_call(
        kernel,
        out_shape=[jax.ShapeDtypeStruct(shape, dtype) for shape, dtype in outs],
        in_specs=specs,
        out_specs=[out_spec] * len(outs),
        scratch_shapes=list(scratch),
        compiler_params=pltpu.CompilerParams(vmem_limit_bytes=grant << 20),
        cost_estimate=pl.CostEstimate(
            flops=micros * 10**9, bytes_accessed=micros * 3 * 10**6, transcendentals=0
        ),
        name=name,
    )(*operands)


def exchange(value, axes):
    return lax.all_to_all(value, axes, 0, 0, tiled=True)


def swap(value):
    return lax.ppermute(value, "c", [(0, 1), (1, 0)])


def turn(value, axis, step):
    return lax.ppermute(value, axis, [(place, (place + step) % 4) for place in range(4)])


def on_device(query_key_value, out_weight, cotangent):
    core = lax.axis_index("c").astype(jnp.int32).reshape(1)
    x_place = lax.axis_index("x").astype(jnp.int32).reshape(1)
    (packed,) = call(
        pack_kernel,
        "pack",
        (core, query_key_value.reshape(3, ROWS, WIDTH), cotangent.reshape(ROWS, OUT), out_weight),
        [IN_SMEM] + [IN_HBM] * 2 + [IN_VMEM],
        [((64, 2, COLS), BF16)],
        [
            pltpu.VMEM((3, ROWS, WIDTH), BF16),
            pltpu.VMEM((ROWS, OUT), BF16),
            pltpu.SemaphoreType.DMA((4,)),
        ],
        grant=56,
    )
    sent = exchange(packed, SEQ)
    share, columns = call(
        forward_kernel,
        "forward",
        (core, sent),
        [IN_SMEM, IN_VMEM],
        [((ROWS, WIDTH + HALF), BF16), ((ROWS, HALF), BF16)],
        [
            pltpu.VMEM((ROWS, COLS), BF16),
            pltpu.VMEM((HEADS, ROWS, ROWS), F32),
            pltpu.VMEM((ROWS, OUT), BF16),
        ],
        micros=3,
    )
    piece = sent[:, :, BASE:].reshape(ROWS, PIECE)
    turned = [turn(piece, "x", step) for step in range(1, 4)]
    (partial,) = call(
        weight_grad_kernel,
        "weight_grad",
        (share, swap(share), columns),
        [IN_VMEM] * 3,
        [((64, 2, HALF_WIDTH), BF16)],
    )
    collected = exchange(partial, SEQ)
    piece, *turned = lax.optimization_barrier((piece, *turned, partial))[:4]
    mine = jnp.stack([piece, *turned])
    (results,) = call(
        backward_kernel,
        "backward",
        (core, x_place, sent, mine, swap(mine)),
        [IN_SMEM] * 2 + [IN_VMEM] * 3,
        [((64, 2, BASE), BF16)],
        [
            pltpu.VMEM((ROWS, COLS), BF16),
            pltpu.VMEM((HEADS, ROWS, ROWS), F32),
            pltpu.VMEM((ROWS, OUT), BF16),
            pltpu.VMEM((ROWS, WIDTH), BF16),
            pltpu.VMEM((OUT, WIDTH), BF16),
            pltpu.VMEM((ROWS, WIDTH), BF16),
            pltpu.VMEM((HEADS, ROWS, ROWS), BF16),
        ],
        micros=7,
    )
    results, collected = lax.optimization_barrier((results, collected))
    (owned,) = call(owned_kernel, "owned", (collected,), [IN_VMEM], [((2, HALF_WIDTH), F32)])
    turned = [turn(owned, "yl", step) for step in range(1, 4)]
    back = exchange(results, SEQ)
    (group,) = call(
        group_kernel, "group", (owned, *turned), [IN_VMEM] * 4, [((2, HALF_WIDTH), F32)]
    )
    (total,) = call(
        total_kernel,
        "total",
        (core, group, swap(group)),
        [IN_SMEM] + [IN_VMEM] * 2,
        [((12, WIDTH), F32)],
    )
    projected, grads = call(
        unpack_kernel,
        "unpack",
        (back,),
        [IN_VMEM],
        [((ROWS, OUT), BF16), ((3, ROWS, WIDTH), BF16)],
        [pltpu.VMEM((ROWS, BASE), BF16), pltpu.SemaphoreType.DMA((4,))],
        out_spec=IN_HBM,
    )
    return (
        projected.reshape(1, 1, ROWS, OUT),
        grads.reshape(3, 1, 1, ROWS, WIDTH),
        total,
    )


def solution(mesh):
    split = Mesh(mesh.devices.reshape(4, 2, 2, 4, 8), ("yl", "c", "yh", "x", "z"))
    in_specs = (P(None, GROUPS, SEQ, None, None), P(SEQ, None), P(GROUPS, SEQ, None, None))
    out_specs = (P(GROUPS, SEQ, None, None), P(None, GROUPS, SEQ, None, None), P(SEQ, None))
    return jax.shard_map(
        on_device, mesh=split, in_specs=in_specs, out_specs=out_specs, check_vma=False
    )
```
